32 devices in a mesh: wide: 8 (over z, y), grp: 4 (over x, core).
Axes of the slice: x: 2, y: 2, z: 4, core: 2. Of those that a mesh axis runs over, the one named last changes fastest.
Arguments:
- slab: float32 [64, 4, 16, 128], P(None, 'grp', 'wide'), may hold values from -400 to 400
- hblocks: float32 [4, 16, 5, 128, 128], P('grp', 'wide'), may hold values from -0.25 to 0.25
- blist: int32 [4, 16, 5], P('grp', 'wide'), may hold values from 0 to 8, as said below
- rotation: float32 [8, 8, 8], replicated, may hold values from -2 to 2
Outputs:
- rotated: float32 [64, 4, 16, 128], P('wide', 'grp')
The draws below stay inside these ranges and needn't reach their ends.
Inputs may be any that keep to these rules, and one draw needn't show every extreme that they name: `blist`: entry 0 of every row block's list is 4 (the block itself); the other entries are distinct codes other than 4.
All inputs are finite; a program needn't handle non-finite values.
Results may differ from the reference program's by a relative error of at most 0.00012.
Values sent between devices are 32-bit elements; how exact they have to be, the bound alone decides.
No kernel may reach another device: no remote copies, remote signals or barrier semaphores. Data moves between devices by JAX's collectives and lax.ppermute only.
A program may use at most 64 MiB of HBM per device.

```python
import jax
import jax.numpy as jnp
from jax import lax

VEC = 8
BS = 128
K = 5
DEG = 4
S = 64
SBLK = 8
GRPS = 4
QBLK = 16
NODES = 8192


def draw_blist(key, part):
    key = jax.random.fold_in(key, 7)
    scores = jax.random.randint(key, (GRPS, QBLK, 8), 0, 1 << 20, dtype=jnp.int32)
    scores = scores * 8 + jnp.arange(8, dtype=jnp.int32)
    ordering = jnp.argsort(scores, axis=-1).astype(jnp.int32)
    neighbours = ordering + (ordering >= 4).astype(jnp.int32)
    self_code = jnp.full((GRPS, QBLK, 1), 4, jnp.int32)
    return jnp.concatenate([self_code, neighbours[:, :, :K - 1]], axis=-1)


def draw_slab(key, part):
    key = jax.random.fold_in(key, 11)
    key_list = jax.random.split(key, 3)
    rising = 3.0 ** (jnp.arange(QBLK, dtype=jnp.float32) / max(QBLK - 1, 1))
    block_scale = 10.0 ** jax.random.uniform(key_list[1], (1, GRPS, QBLK, 1), jnp.float32)
    state_scale = 10.0 ** jax.random.uniform(key_list[2], (S, 1, 1, 1), jnp.float32)
    basic_values = jnp.clip(jax.random.normal(key_list[0], (S, GRPS, QBLK, BS), jnp.float32), -6.0, 6.0)
    return basic_values * rising[None, None, :, None] * block_scale * state_scale / 10.0


def shard_levels(stream_key, dims, shards, least, high):
    def one(position, parts):
        heights = jax.random.uniform(jax.random.fold_in(jax.random.fold_in(stream_key, 6), position), (parts,), jnp.float32, least / len(shards), high / len(shards))
        return jnp.repeat(jnp.exp(heights), dims[position] // parts).reshape((-1,) + (1,) * (len(dims) - position - 1))

    gain = one(*shards[0])
    for cut in shards[1:]:
        gain = gain * one(*cut)
    return gain


def gaussian(rng, dims, deviation, reach, pieces=(), kind=jnp.bfloat16):
    factor_of = shard_levels(rng, dims, pieces, -0.22, 0.18) if pieces else 1.0
    entries = jax.random.normal(rng, dims, jnp.float32) * deviation * factor_of
    return jnp.minimum(jnp.maximum(entries, -reach), reach).astype(kind)


def setup_inputs(seed: int = 0) -> dict:
    key_of = jax.random.split(jax.random.key(seed), 5)
    return {
        "slab": draw_slab(jax.random.fold_in(key_of[4], 71), 0),
        "hblocks": gaussian(key_of[1], (GRPS, QBLK, K, BS, BS), (K * BS) ** -0.5, 0.25, ((0, 4), (1, 8)), jnp.float32),
        "blist": draw_blist(jax.random.fold_in(key_of[4], 71), 0),
        "rotation": gaussian(key_of[3], (SBLK, VEC, VEC), VEC ** -0.5, 2.0, (), jnp.float32),
    }


def apply_operator(field_in, hblocks, blist):
    padded = jnp.pad(field_in, ((0, 0), (1, 1), (1, 1), (0, 0)))
    grp_rows = jnp.arange(field_in.shape[1], dtype=jnp.int32)[:, None]
    blk_cols = jnp.arange(field_in.shape[2], dtype=jnp.int32)[None, :]
    summed = jnp.zeros(field_in.shape, jnp.float32)
    for slot_index in range(blist.shape[2]):
        block_code = blist[:, :, slot_index]
        picked = padded[:, grp_rows + block_code // 3, blk_cols + block_code % 3]
        summed = summed + jnp.einsum('gqij,sgqj->sgqi', hblocks[:, :, slot_index], picked, precision=lax.Precision.HIGHEST)
    return summed

def mixing(gram_mat, rotation):
    lower = jnp.linalg.cholesky(gram_mat)
    return lax.linalg.triangular_solve(lower, jnp.swapaxes(rotation, -1, -2), left_side=False, lower=True)

def reference(slab, hblocks, blist, rotation):
    previous = slab
    current = apply_operator(slab, hblocks, blist)
    for degree_step in range(DEG - 1):
        following = 2.0 * apply_operator(current, hblocks, blist) - previous
        previous, current = (current, following)
    state_blocks = current.reshape(SBLK, VEC, -1)
    gram_mat = jnp.einsum('bam,bcm->bac', state_blocks, state_blocks, precision=lax.Precision.HIGHEST) / NODES
    mixer = mixing(gram_mat, rotation)
    rotated = jnp.einsum('bad,bdm->bam', mixer, state_blocks, precision=lax.Precision.HIGHEST)
    return rotated.reshape(current.shape)
```

```python
import functools

import jax
import jax.numpy as jnp
from jax import lax
from jax.experimental import pallas as pl
from jax.experimental.pallas import tpu as pltpu
from jax.sharding import PartitionSpec as P

VEC = 8
DEG = 4
LIMIT = 16 * 2**20
BLOCKS = 9
VMEM = pl.BlockSpec(memory_space=pltpu.VMEM)
SMEM = pl.BlockSpec(memory_space=pltpu.SMEM)
NT = (((1,), (1,)), ((), ()))


def split(x):
    high = x.astype(jnp.bfloat16)
    low = (x - high.astype(jnp.float32)).astype(jnp.bfloat16)
    return high, low


def flag(flags_ref, n, shape):
    return jnp.broadcast_to(flags_ref[n * VEC : n * VEC + 1, :], shape) == 1


def arrange_kernel(flags_ref, codes_ref, slab_ref, out_ref):
    all_states, _, cols, size = slab_ref.shape
    slots, states = codes_ref.shape[2], all_states // 2
    odd = flag(flags_ref, 0, (all_states, size))
    second = flag(flags_ref, 2, (states, size))
    both = [slab_ref[:, 0, c, :] for c in range(cols)]
    for u in range(cols):
        value = jnp.where(odd, both[cols - 1 - u], both[u])
        low, high = value[:states], value[states:]
        rows = slice(u * states, (u + 1) * states)
        out_ref[0, rows, :] = jnp.where(second, high, low)
        out_ref[1, rows, :] = jnp.where(second, low, high)
    codes = codes_ref[0].astype(jnp.float32)
    for h in range(2):
        out_ref[h, cols * states :, :] = jnp.zeros((VEC, size), jnp.float32)
        out_ref[h, cols * states : cols * states + cols, 0:slots] = codes


def arrange(flags, blist, slab):
    all_states, _, cols, size = slab.shape
    return pl.pallas_call(
        arrange_kernel,
        in_specs=[VMEM] * 3,
        out_specs=VMEM,
        out_shape=jax.ShapeDtypeStruct((2, cols * all_states // 2 + VEC, size), jnp.float32),
        compiler_params=pltpu.CompilerParams(vmem_limit_bytes=LIMIT),
        name="arrange",
    )(flags, blist, slab)


def pick_kernel(flags_ref, own_ref, core_ref, border_ref, inner_ref):
    shape = own_ref.shape[3:]
    edge, half = flag(flags_ref, 1, shape), flag(flags_ref, 2, shape)
    for k in range(own_ref.shape[2]):
        own = jnp.where(half, own_ref[0, 1, k], own_ref[0, 0, k])
        core = jnp.where(half, core_ref[0, 1, k], core_ref[0, 0, k])
        border_ref[0, 0, k] = jnp.where(edge, own, core)
        inner_ref[0, 0, k] = jnp.where(edge, core, own)


def pick(flags, own, core):
    rows, cols, *block = own.shape
    return pl.pallas_call(
        pick_kernel,
        in_specs=[VMEM] * 3,
        out_specs=[VMEM] * 2,
        out_shape=[jax.ShapeDtypeStruct((rows, 1, *block), own.dtype)] * 2,
        compiler_params=pltpu.CompilerParams(vmem_limit_bytes=LIMIT),
        name="pick",
    )(flags, own, core)


def prepare_kernel(mode, codes_ref, *refs):
    *h_refs, out_ref = refs
    _, cols, slots, size, _ = h_refs[0].shape
    odd, edge, half, x = (codes_ref[n] for n in range(4))
    out_ref[...] = jnp.zeros_like(out_ref)

    def convert(h_ref, h_col, c, q, row):
        u = jnp.bitwise_xor(c, odd)
        for k in range(slots):
            code = codes_ref[4 + (row * 2 + c) * slots + k]
            down = (code >= 3).astype(jnp.int32) + (code >= 6).astype(jnp.int32)
            along = code - 3 * down
            down = jnp.where(x == 1, 2 - down, down)
            along = u + jnp.where(odd == 1, 2 - along, along)
            rim = (along == 0) | (along == 3)
            block = jnp.where(rim, 6 + down, 2 * down + along - 1)
            lanes = pl.ds(pl.multiple_of(block * size, size), size)
            high, low = split(h_ref[0, h_col, k])
            out_ref[q, u, 0:size, lanes] = high
            out_ref[q, u, size : 2 * size, lanes] = low

    for h, h_ref in enumerate(h_refs):
        if mode == "chip":
            for c in range(cols):
                convert(h_ref, c, c, jnp.bitwise_xor(edge, h), h)
        else:
            row = 3 - edge if mode == "border" else 2 + edge
            convert(h_ref, 0, jnp.bitwise_xor(half, h), 0, row)


def prepare(mode, codes, *h_rows):
    _, _, slots, size, _ = h_rows[0].shape
    rows = 2 if mode == "chip" else 1
    return pl.pallas_call(
        functools.partial(prepare_kernel, mode),
        in_specs=[SMEM] + [VMEM] * len(h_rows),
        out_specs=VMEM,
        out_shape=jax.ShapeDtypeStruct((rows, 2, 2 * size, BLOCKS * size), jnp.bfloat16),
        compiler_params=pltpu.CompilerParams(vmem_limit_bytes=LIMIT),
        name="prepare_" + mode,
    )(codes, *h_rows)


def fill(x_ref, fields):
    rows, states, size = fields[0].shape
    for q in range(rows):
        for n, field in enumerate(fields):
            at = (q * len(fields) + n) * size
            high, low = split(field[q])
            x_ref[0:states, at : at + size] = high
            x_ref[states : 2 * states, at : at + size] = low


def step_kernel(kind, u, count, *refs):
    h_refs, (own_0, own_1, rim_ref, *refs) = refs[:count], refs[count:]
    *refs, own_x, rim_x = refs
    before, refs = (None, refs) if kind == "first" else (refs[0], refs[1:])
    rows_in, states, size = rim_ref.shape
    h_rows = [h_ref.at[q] for h_ref in h_refs for q in range(h_ref.shape[0])]
    fill(own_x, [own_0, own_1])
    fill(rim_x, [rim_ref])
    values = []
    for q, h_row in enumerate(h_rows):
        low, high = max(q - 1, 0), min(q + 2, rows_in)
        acc = 0.0
        for x_ref, width, first in ((own_x, 2 * size, 0), (rim_x, size, 6 * size)):
            at = first + (low - q + 1) * width
            acc = acc + lax.dot_general(
                x_ref[:, low * width : high * width],
                h_row[u, :, at : at + (high - low) * width],
                NT,
                preferred_element_type=jnp.float32,
            )
        small = acc[states:, size:] + (acc[states:, :size] + acc[:states, size:])
        value = acc[:states, :size] + small
        values.append(value if kind == "first" else 2.0 * value - before[q])
    if kind in ("other", "last"):
        flat = [jnp.concatenate(part, axis=1) for part in zip(*map(split, values))]
        flat = jnp.concatenate(flat)
        gram = lax.dot_general(flat, flat, NT, preferred_element_type=jnp.float32)
        gram = gram[:states] + gram[states:]
        gram = gram[:, :states] + gram[:, states:]
    if kind != "last":
        for q, value in enumerate(values):
            refs[0][q] = value
        if kind == "other":
            refs[1][:, 0:states] = gram
        return
    other_ref, other_gram_ref, flags_ref, packed_ref, sent_ref = refs
    odd, edge = flag(flags_ref, 0, (states, size)), flag(flags_ref, 1, (states, size))
    nodes = [[other_ref[q] for q in range(len(values))], values]
    gram = gram + other_gram_ref[:, 0:states]
    for c in range(2):
        inner = jnp.where(odd, nodes[1 - c][0], nodes[c][0])
        border = jnp.where(odd, nodes[1 - c][1], nodes[c][1])
        kept, sent = jnp.where(edge, border, inner), jnp.where(edge, inner, border)
        for b in range(states // VEC):
            packed_ref[b, c * VEC : (c + 1) * VEC, :] = kept[b * VEC : (b + 1) * VEC]
            sent_ref[b, c * VEC : (c + 1) * VEC, :] = sent[b * VEC : (b + 1) * VEC]
    for b in range(states // VEC):
        rows = slice(b * VEC, (b + 1) * VEC)
        for ref in (packed_ref, sent_ref):
            ref[b, 2 * VEC :, :] = jnp.zeros((VEC, size), jnp.float32)
            ref[b, 2 * VEC :, 0:VEC] = gram[rows, rows]


def step(kind, u, name, h_ready, own, rim, *others):
    rows_in, states, size = rim.shape
    rows_out = sum(h.shape[0] for h in h_ready)
    shapes = [(rows_out, states, size)]
    if kind == "other":
        shapes.append((states, pl.cdiv(states, size) * size))
    elif kind == "last":
        blocks = states // VEC
        shapes = [(2 * blocks, 3 * VEC, size), (blocks, 3 * VEC, size)]
    operands = [*h_ready, *own, rim, *others]
    cost = pl.CostEstimate(
        flops=8 * BLOCKS * rows_out * states * size * size,
        bytes_accessed=4 * BLOCKS * rows_out * size * size,
        transcendentals=0,
    )
    outs = pl.pallas_call(
        functools.partial(step_kernel, kind, u, len(h_ready)),
        in_specs=[VMEM] * len(operands),
        out_specs=[VMEM] * len(shapes),
        out_shape=[jax.ShapeDtypeStruct(shape, jnp.float32) for shape in shapes],
        scratch_shapes=[
            pltpu.VMEM((2 * states, rows_in * width * size), jnp.bfloat16) for width in (2, 1)
        ],
        compiler_params=pltpu.CompilerParams(vmem_limit_bytes=LIMIT),
        cost_estimate=cost,
        name=name,
    )(*operands)
    return outs[0] if len(outs) == 1 else outs


def finish_kernel(cols, node_count, flags_ref, parts_ref, rot_ref, out_ref):
    wide = parts_ref.shape[0]
    gram = parts_ref[0, cols * VEC : (cols + 1) * VEC, 0:VEC]
    for w in range(1, wide):
        gram = gram + parts_ref[w, cols * VEC : (cols + 1) * VEC, 0:VEC]
    gram = gram / node_count
    row = lax.broadcasted_iota(jnp.int32, (VEC, VEC), 0)
    col = lax.broadcasted_iota(jnp.int32, (VEC, VEC), 1)
    inverse = jnp.where(row == col, 1.0, 0.0).astype(jnp.float32)
    for k in range(VEC):
        scale = 1.0 / jnp.sqrt(gram[k : k + 1, k : k + 1])
        top = gram[k : k + 1, :] * scale
        top_inverse = inverse[k : k + 1, :] * scale
        factor = gram[:, k : k + 1] * scale
        gram = gram - factor * top
        inverse = jnp.where(row == k, top_inverse, jnp.where(row > k, inverse - factor * top_inverse, inverse))
    turn = rot_ref[...]
    mixer = turn[:, 0:1] * inverse[0:1, :]
    for k in range(1, VEC):
        mixer = mixer + turn[:, k : k + 1] * inverse[k : k + 1, :]
    columns = [mixer[:, d : d + 1] for d in range(VEC)]
    mixed = []
    for w in range(wide):
        for c in range(cols):
            block = parts_ref[w, c * VEC : (c + 1) * VEC, :]
            total = columns[0] * block[0:1, :]
            for d in range(1, VEC):
                total = total + columns[d] * block[d : d + 1, :]
            mixed.append(total)
    half = flag(flags_ref, 2, mixed[0].shape)
    for at, total in enumerate(mixed):
        turned = mixed[(at + len(mixed) // 2) % len(mixed)]
        out_ref[:, 0, at, :] = jnp.where(half, turned, total)


def finish(flags, cols, node_count, parts, turn):
    wide, _, size = parts.shape
    return pl.pallas_call(
        functools.partial(finish_kernel, cols, node_count),
        in_specs=[VMEM] * 3,
        out_specs=VMEM,
        out_shape=jax.ShapeDtypeStruct((VEC, 1, wide * cols, size), jnp.float32),
        compiler_params=pltpu.CompilerParams(vmem_limit_bytes=LIMIT),
        name="finish",
    )(flags, parts, turn)


def after(x, token):
    return lax.optimization_barrier((x, token))[0]


def body(slab, hblocks, blist, rotation):
    wide, grp = lax.axis_size("wide"), lax.axis_size("grp")
    _, _, cols, size = slab.shape
    slots = hblocks.shape[2]
    near = [(i, i ^ 1) for i in range(wide)]
    far = [(i, ((i + 1) ^ 1) - 1) for i in range(1, wide - 1)]
    mine, odd = lax.axis_index("grp"), lax.axis_index("wide") % 2
    x = mine // 2
    edge = half = x ^ (mine % 2)
    place = jnp.stack([odd, edge, half, x]).astype(jnp.int32)
    flags = jnp.broadcast_to(jnp.repeat(place, VEC)[:, None], (4 * VEC, size))

    def across(value):
        return lax.ppermute(value, "grp", [(i, i ^ 3) for i in range(grp)])

    def core(value):
        return lax.ppermute(value, "grp", [(i, i ^ 1) for i in range(grp)])

    def over_far(value):
        return lax.ppermute(value, "wide", far)

    def over_near(value):
        return lax.ppermute(value, "wide", near)

    own = arrange(flags, blist, slab)
    own_core = core(own[1])
    h_core = core(hblocks)
    border, inside = pick(flags, hblocks, h_core)
    own_across = across(after(jnp.stack([own[0], own_core]), border))
    rows = [own[0], own_core, own_across[0], own_across[1]]
    codes = jnp.stack([row[-VEC : cols - VEC, :slots] for row in rows]).astype(jnp.int32).reshape(-1)
    codes = jnp.concatenate([place, codes])
    states = (own.shape[1] - VEC) // cols
    zero = []
    for u in range(cols):
        parts = [row[u * states : (u + 1) * states] for row in rows]
        border_mine = jnp.stack([parts[m] for m in (1, 0, 2, 3)])
        border_core = jnp.stack([parts[m] for m in (0, 1, 3, 2)])
        zero.append(jnp.where(edge == 1, border_mine, border_core))

    zero[1] = after(zero[1], zero[0])
    far_rim, near_rim = over_far(zero[0]), over_near(zero[1])
    border = across(after(border, own_core))
    inside = across(after(inside, zero[1]))
    h_two = [prepare("chip", codes, hblocks, h_core)]
    border_core = core(after(border, (far_rim, near_rim, h_two)))
    h_three = h_two + [prepare("border", codes, border, border_core)]

    one = [step("first", 0, "one_0", h_three, zero, far_rim)]
    rim = after(near_rim, one[0])
    one.append(step("first", 1, "one_1", h_three, zero, rim))
    rims = over_far(one[0]), over_near(one[1])
    two, sent, before = [], (), []
    for u in range(cols):
        rim = after(rims[u], (sent, inside))
        two.append(step("next", u, f"two_{u}", h_two, one, rim, zero[u]))
        sent = jnp.concatenate([two[u], one[u][:1]])
        other = across(sent)
        two[u] = jnp.concatenate([two[u], other[1:2], other[0:1]])
        before.append(jnp.concatenate([one[u], other[2:]]))
    inside_core = core(after(inside, two[0]))
    h_four = h_three + [prepare("inner", codes, inside, inside_core)]
    rims = over_far(two[0]), over_near(two[1])
    three = [step("next", 0, "three_0", h_four, two, rims[0], before[0])]
    rim = after(rims[1], three[0])
    three.append(step("next", 1, "three_1", h_four, two, rim, before[1]))
    rims = over_far(three[0]), over_near(three[1])
    four = step("other", 0, "four_0", h_four, three, rims[0], two[0])
    packed, sent = step("last", 1, "four_1", h_four, three, rims[1], two[1], *four, flags)

    packed = lax.dynamic_update_slice(packed, core(sent), (sent.shape[0], 0, 0))
    owners = wide // 2
    groups = [
        [((i + owners * (g // 2 ^ g % 2)) % wide) * grp + g for i in range(wide)] for g in range(grp)
    ]
    packed = lax.all_to_all(
        packed,
        ("wide", "grp"),
        split_axis=0,
        concat_axis=0,
        tiled=True,
        axis_index_groups=groups,
    )
    turn = lax.dynamic_index_in_dim(rotation, lax.axis_index("wide"), 0, keepdims=False)
    node_count = grp * wide * cols * size
    return finish(flags, cols, node_count, packed, turn.T)


def solution(mesh):
    in_specs = (
        P(None, "grp", "wide", None),
        P("grp", "wide", None, None, None),
        P("grp", "wide", None),
        P(),
    )
    out_specs = P("wide", "grp", None, None)
    return jax.shard_map(body, mesh=mesh, in_specs=in_specs, out_specs=out_specs, check_vma=False)
```

```python
import functools

import jax
import jax.numpy as jnp
from jax import lax
from jax.experimental import pallas as pl
from jax.experimental.pallas import tpu as pltpu
from jax.sharding import PartitionSpec as P

VEC = 8
DEG = 4
LIMIT = 16 * 2**20
BLOCKS = 9
VMEM = pl.BlockSpec(memory_space=pltpu.VMEM)
SMEM = pl.BlockSpec(memory_space=pltpu.SMEM)
NT = (((1,), (1,)), ((), ()))


def split(x):
    high = x.astype(jnp.bfloat16)
    low = (x - high.astype(jnp.float32)).astype(jnp.bfloat16)
    return high, low


def flag(flags_ref, n, shape):
    return jnp.broadcast_to(flags_ref[n * VEC : n * VEC + 1, :], shape) == 1


def arrange_kernel(flags_ref, codes_ref, slab_ref, out_ref):
    all_states, _, cols, size = slab_ref.shape
    slots, states = codes_ref.shape[2], all_states // 2
    odd = flag(flags_ref, 0, (all_states, size))
    second = flag(flags_ref, 2, (states, size))
    both = [slab_ref[:, 0, c, :] for c in range(cols)]
    for u in range(cols):
        value = jnp.where(odd, both[cols - 1 - u], both[u])
        low, high = value[:states], value[states:]
        rows = slice(u * states, (u + 1) * states)
        out_ref[0, rows, :] = jnp.where(second, high, low)
        out_ref[1, rows, :] = jnp.where(second, low, high)
    codes = codes_ref[0].astype(jnp.float32)
    for h in range(2):
        out_ref[h, cols * states :, :] = jnp.zeros((VEC, size), jnp.float32)
        out_ref[h, cols * states : cols * states + cols, 0:slots] = codes


def arrange(flags, blist, slab):
    all_states, _, cols, size = slab.shape
    return pl.pallas_call(
        arrange_kernel,
        in_specs=[VMEM] * 3,
        out_specs=VMEM,
        out_shape=jax.ShapeDtypeStruct((2, cols * all_states // 2 + VEC, size), jnp.float32),
        compiler_params=pltpu.CompilerParams(vmem_limit_bytes=LIMIT),
        name="arrange",
    )(flags, blist, slab)


def pick_kernel(flags_ref, own_ref, core_ref, border_ref, inner_ref):
    shape = own_ref.shape[3:]
    edge, half = flag(flags_ref, 1, shape), flag(flags_ref, 2, shape)
    for k in range(own_ref.shape[2]):
        own = jnp.where(half, own_ref[0, 1, k], own_ref[0, 0, k])
        core = jnp.where(half, core_ref[0, 1, k], core_ref[0, 0, k])
        border_ref[0, 0, k] = jnp.where(edge, own, core)
        inner_ref[0, 0, k] = jnp.where(edge, core, own)


def pick(flags, own, core):
    rows, cols, *block = own.shape
    return pl.pallas_call(
        pick_kernel,
        in_specs=[VMEM] * 3,
        out_specs=[VMEM] * 2,
        out_shape=[jax.ShapeDtypeStruct((rows, 1, *block), own.dtype)] * 2,
        compiler_params=pltpu.CompilerParams(vmem_limit_bytes=LIMIT),
        name="pick",
    )(flags, own, core)


def prepare_kernel(mode, codes_ref, *refs):
    *h_refs, out_ref = refs
    _, cols, slots, size, _ = h_refs[0].shape
    odd, edge, half, x = (codes_ref[n] for n in range(4))
    out_ref[...] = jnp.zeros_like(out_ref)

    def convert(h_ref, h_col, c, q, row):
        u = jnp.bitwise_xor(c, odd)
        for k in range(slots):
            code = codes_ref[4 + (row * 2 + c) * slots + k]
            down = (code >= 3).astype(jnp.int32) + (code >= 6).astype(jnp.int32)
            along = code - 3 * down
            down = jnp.where(x == 1, 2 - down, down)
            along = u + jnp.where(odd == 1, 2 - along, along)
            rim = (along == 0) | (along == 3)
            block = jnp.where(rim, 6 + down, 2 * down + along - 1)
            lanes = pl.ds(pl.multiple_of(block * size, size), size)
            high, low = split(h_ref[0, h_col, k])
            out_ref[q, u, 0:size, lanes] = high
            out_ref[q, u, size : 2 * size, lanes] = low

    for h, h_ref in enumerate(h_refs):
        if mode == "chip":
            for c in range(cols):
                convert(h_ref, c, c, jnp.bitwise_xor(edge, h), h)
        else:
            row = 3 - edge if mode == "border" else 2 + edge
            convert(h_ref, 0, jnp.bitwise_xor(half, h), 0, row)


def prepare(mode, codes, *h_rows):
    _, _, slots, size, _ = h_rows[0].shape
    rows = 2 if mode == "chip" else 1
    return pl.pallas_call(
        functools.partial(prepare_kernel, mode),
        in_specs=[SMEM] + [VMEM] * len(h_rows),
        out_specs=VMEM,
        out_shape=jax.ShapeDtypeStruct((rows, 2, 2 * size, BLOCKS * size), jnp.bfloat16),
        compiler_params=pltpu.CompilerParams(vmem_limit_bytes=LIMIT),
        name="prepare_" + mode,
    )(codes, *h_rows)


def fill(x_ref, fields):
    rows, states, size = fields[0].shape
    for q in range(rows):
        for n, field in enumerate(fields):
            at = (q * len(fields) + n) * size
            high, low = split(field[q])
            x_ref[0:states, at : at + size] = high
            x_ref[states : 2 * states, at : at + size] = low


def step_kernel(kind, u, count, *refs):
    h_refs, (own_0, own_1, rim_ref, *refs) = refs[:count], refs[count:]
    *refs, own_x, rim_x = refs
    before, refs = (None, refs) if kind == "first" else (refs[0], refs[1:])
    rows_in, states, size = rim_ref.shape
    h_rows = [h_ref.at[q] for h_ref in h_refs for q in range(h_ref.shape[0])]
    fill(own_x, [own_0, own_1])
    fill(rim_x, [rim_ref])
    values = []
    for q, h_row in enumerate(h_rows):
        low, high = max(q - 1, 0), min(q + 2, rows_in)
        acc = 0.0
        for x_ref, width, first in ((own_x, 2 * size, 0), (rim_x, size, 6 * size)):
            at = first + (low - q + 1) * width
            acc = acc + lax.dot_general(
                x_ref[:, low * width : high * width],
                h_row[u, :, at : at + (high - low) * width],
                NT,
                preferred_element_type=jnp.float32,
            )
        small = acc[states:, size:] + (acc[states:, :size] + acc[:states, size:])
        value = acc[:states, :size] + small
        values.append(value if kind == "first" else 2.0 * value - before[q])
    if kind in ("other", "last"):
        flat = [jnp.concatenate(part, axis=1) for part in zip(*map(split, values))]
        flat = jnp.concatenate(flat)
        gram = lax.dot_general(flat, flat, NT, preferred_element_type=jnp.float32)
        gram = gram[:states] + gram[states:]
        gram = gram[:, :states] + gram[:, states:]
    if kind != "last":
        for q, value in enumerate(values):
            refs[0][q] = value
        if kind == "other":
            refs[1][:, 0:states] = gram
        return
    other_ref, other_gram_ref, flags_ref, kept_ref, sent_ref = refs
    odd, edge = flag(flags_ref, 0, (states, size)), flag(flags_ref, 1, (states, size))
    nodes = [[other_ref[q] for q in range(len(values))], values]
    gram = gram + other_gram_ref[:, 0:states]
    blocks = states // VEC
    for c in range(2):
        inner = jnp.where(odd, nodes[1 - c][0], nodes[c][0])
        border = jnp.where(odd, nodes[1 - c][1], nodes[c][1])
        kept, sent = jnp.where(edge, border, inner), jnp.where(edge, inner, border)
        for b in range(blocks):
            rows = slice(b * VEC, (b + 1) * VEC)
            kept_ref[blocks - 1 - b, c * VEC : (c + 1) * VEC, :] = kept[rows]
            sent_ref[blocks - 1 - b, c * VEC : (c + 1) * VEC, :] = sent[rows]
    for b in range(blocks):
        rows = slice(b * VEC, (b + 1) * VEC)
        for ref in (kept_ref, sent_ref):
            ref[blocks - 1 - b, 2 * VEC :, :] = jnp.zeros((VEC, size), jnp.float32)
            ref[blocks - 1 - b, 2 * VEC :, 0:VEC] = gram[rows, rows]


def step(kind, u, name, h_ready, own, rim, *others):
    rows_in, states, size = rim.shape
    rows_out = sum(h.shape[0] for h in h_ready)
    shapes = [(rows_out, states, size)]
    if kind == "other":
        shapes.append((states, pl.cdiv(states, size) * size))
    elif kind == "last":
        blocks = states // VEC
        shapes = [(blocks, 3 * VEC, size)] * 2
    operands = [*h_ready, *own, rim, *others]
    cost = pl.CostEstimate(
        flops=8 * BLOCKS * rows_out * states * size * size,
        bytes_accessed=4 * BLOCKS * rows_out * size * size,
        transcendentals=0,
    )
    outs = pl.pallas_call(
        functools.partial(step_kernel, kind, u, len(h_ready)),
        in_specs=[VMEM] * len(operands),
        out_specs=[VMEM] * len(shapes),
        out_shape=[jax.ShapeDtypeStruct(shape, jnp.float32) for shape in shapes],
        scratch_shapes=[
            pltpu.VMEM((2 * states, rows_in * width * size), jnp.bfloat16) for width in (2, 1)
        ],
        compiler_params=pltpu.CompilerParams(vmem_limit_bytes=LIMIT),
        cost_estimate=cost,
        name=name,
    )(*operands)
    return outs[0] if len(outs) == 1 else outs


def finish_kernel(cols, node_count, flags_ref, parts_ref, rot_ref, out_ref):
    wide = parts_ref.shape[0]
    gram = parts_ref[0, cols * VEC : (cols + 1) * VEC, 0:VEC]
    for w in range(1, wide):
        gram = gram + parts_ref[w, cols * VEC : (cols + 1) * VEC, 0:VEC]
    gram = gram / node_count
    row = lax.broadcasted_iota(jnp.int32, (VEC, VEC), 0)
    col = lax.broadcasted_iota(jnp.int32, (VEC, VEC), 1)
    inverse = jnp.where(row == col, 1.0, 0.0).astype(jnp.float32)
    for k in range(VEC):
        scale = 1.0 / jnp.sqrt(gram[k : k + 1, k : k + 1])
        top = gram[k : k + 1, :] * scale
        top_inverse = inverse[k : k + 1, :] * scale
        factor = gram[:, k : k + 1] * scale
        gram = gram - factor * top
        inverse = jnp.where(row == k, top_inverse, jnp.where(row > k, inverse - factor * top_inverse, inverse))
    turn = rot_ref[...]
    mixer = turn[:, 0:1] * inverse[0:1, :]
    for k in range(1, VEC):
        mixer = mixer + turn[:, k : k + 1] * inverse[k : k + 1, :]
    columns = [mixer[:, d : d + 1] for d in range(VEC)]
    mixed = []
    for w in range(wide):
        for c in range(cols):
            block = parts_ref[w, c * VEC : (c + 1) * VEC, :]
            total = columns[0] * block[0:1, :]
            for d in range(1, VEC):
                total = total + columns[d] * block[d : d + 1, :]
            mixed.append(total)
    half = flag(flags_ref, 2, mixed[0].shape)
    for w in range(wide):
        for c in range(cols):
            first = mixed[(wide - 1 - w) * cols + c]
            second = mixed[(wide - 1 - w + wide // 2) % wide * cols + c]
            out_ref[:, 0, w * cols + c, :] = jnp.where(half, second, first)


def finish(flags, cols, node_count, parts, turn):
    wide, _, size = parts.shape
    return pl.pallas_call(
        functools.partial(finish_kernel, cols, node_count),
        in_specs=[VMEM] * 3,
        out_specs=VMEM,
        out_shape=jax.ShapeDtypeStruct((VEC, 1, wide * cols, size), jnp.float32),
        compiler_params=pltpu.CompilerParams(vmem_limit_bytes=LIMIT),
        name="finish",
    )(flags, parts, turn)


def after(x, token):
    return lax.optimization_barrier((x, token))[0]


def body(slab, hblocks, blist, rotation):
    wide, grp = lax.axis_size("wide"), lax.axis_size("grp")
    _, _, cols, size = slab.shape
    slots = hblocks.shape[2]
    near = [(i, i ^ 1) for i in range(wide)]
    far = [(i, ((i + 1) ^ 1) - 1) for i in range(1, wide - 1)]
    mine, odd = lax.axis_index("grp"), lax.axis_index("wide") % 2
    x = mine // 2
    edge = half = x ^ (mine % 2)
    place = jnp.stack([odd, edge, half, x]).astype(jnp.int32)
    flags = jnp.broadcast_to(jnp.repeat(place, VEC)[:, None], (4 * VEC, size))

    def across(value):
        return lax.ppermute(value, "grp", [(i, i ^ 3) for i in range(grp)])

    def core(value):
        return lax.ppermute(value, "grp", [(i, i ^ 1) for i in range(grp)])

    def over_far(value):
        return lax.ppermute(value, "wide", far)

    def over_near(value):
        return lax.ppermute(value, "wide", near)

    own = arrange(flags, blist, slab)
    own_core = core(own[1])
    h_core = core(hblocks)
    border, inside = pick(flags, hblocks, h_core)
    own_across = across(after(jnp.stack([own[0], own_core]), border))
    rows = [own[0], own_core, own_across[0], own_across[1]]
    codes = jnp.stack([row[-VEC : cols - VEC, :slots] for row in rows]).astype(jnp.int32).reshape(-1)
    codes = jnp.concatenate([place, codes])
    states = (own.shape[1] - VEC) // cols
    zero = []
    for u in range(cols):
        parts = [row[u * states : (u + 1) * states] for row in rows]
        border_mine = jnp.stack([parts[m] for m in (1, 0, 2, 3)])
        border_core = jnp.stack([parts[m] for m in (0, 1, 3, 2)])
        zero.append(jnp.where(edge == 1, border_mine, border_core))

    zero[1] = after(zero[1], zero[0])
    far_rim, near_rim = over_far(zero[0]), over_near(zero[1])
    border = across(after(border, own_core))
    inside = across(after(inside, near_rim))
    h_two = [prepare("chip", codes, hblocks, h_core)]
    border_core = core(after(border, (far_rim, h_two)))
    h_three = h_two + [prepare("border", codes, border, border_core)]

    one = [step("first", 0, "one_0", h_three, zero, far_rim)]
    rim = after(near_rim, one[0])
    one.append(step("first", 1, "one_1", h_three, zero, rim))
    rims = over_far(one[0]), over_near(one[1])
    two, sent, before = [], (), []
    for u in range(cols):
        rim = after(rims[u], (sent, inside))
        two.append(step("next", u, f"two_{u}", h_two, one, rim, zero[u]))
        sent = jnp.concatenate([two[u], one[u][:1]])
        other = across(sent)
        two[u] = jnp.concatenate([two[u], other[1:2], other[0:1]])
        before.append(jnp.concatenate([one[u], other[2:]]))
    inside_core = core(after(inside, two[0]))
    h_four = h_three + [prepare("inner", codes, inside, inside_core)]
    rims = over_far(two[0]), over_near(two[1])
    three = [step("next", 0, "three_0", h_four, two, rims[0], before[0])]
    rim = after(rims[1], three[0])
    three.append(step("next", 1, "three_1", h_four, two, rim, before[1]))
    rims = over_far(three[0]), over_near(three[1])
    four = step("other", 0, "four_0", h_four, three, rims[0], two[0])
    kept, sent = step("last", 1, "four_1", h_four, three, rims[1], two[1], *four, flags)

    packed = jnp.concatenate([core(sent), kept])
    owners = wide // 2
    groups = [
        [((wide - 1 - i + owners * (g // 2 ^ g % 2)) % wide) * grp + g for i in range(wide)]
        for g in range(grp)
    ]
    packed = lax.all_to_all(
        packed,
        ("wide", "grp"),
        split_axis=0,
        concat_axis=0,
        tiled=True,
        axis_index_groups=groups,
    )
    turn = lax.dynamic_index_in_dim(rotation, lax.axis_index("wide"), 0, keepdims=False)
    node_count = grp * wide * cols * size
    return finish(flags, cols, node_count, packed, turn.T)


def solution(mesh):
    in_specs = (
        P(None, "grp", "wide", None),
        P("grp", "wide", None, None, None),
        P("grp", "wide", None),
        P(),
    )
    out_specs = P("wide", "grp", None, None)
    return jax.shard_map(body, mesh=mesh, in_specs=in_specs, out_specs=out_specs, check_vma=False)
```

```python
import functools

import jax
import jax.numpy as jnp
from jax import lax
from jax.experimental import pallas as pl
from jax.experimental.pallas import tpu as pltpu
from jax.sharding import PartitionSpec as P

VEC = 8
DEG = 4
LIMIT = 16 * 2**20
BLOCKS = 9
VMEM = pl.BlockSpec(memory_space=pltpu.VMEM)
SMEM = pl.BlockSpec(memory_space=pltpu.SMEM)
NT = (((1,), (1,)), ((), ()))


def split(x):
    high = x.astype(jnp.bfloat16)
    low = (x - high.astype(jnp.float32)).astype(jnp.bfloat16)
    return high, low


def flag(flags_ref, n, shape):
    return jnp.broadcast_to(flags_ref[n * VEC : n * VEC + 1, :], shape) == 1


def arrange_kernel(flags_ref, codes_ref, slab_ref, out_ref):
    all_states, _, cols, size = slab_ref.shape
    slots, states = codes_ref.shape[2], all_states // 2
    odd = flag(flags_ref, 0, (all_states, size))
    second = flag(flags_ref, 2, (states, size))
    both = [slab_ref[:, 0, c, :] for c in range(cols)]
    for u in range(cols):
        value = jnp.where(odd, both[cols - 1 - u], both[u])
        low, high = value[:states], value[states:]
        rows = slice(u * states, (u + 1) * states)
        out_ref[0, rows, :] = jnp.where(second, high, low)
        out_ref[1, rows, :] = jnp.where(second, low, high)
    codes = codes_ref[0].astype(jnp.float32)
    for h in range(2):
        out_ref[h, cols * states :, :] = jnp.zeros((VEC, size), jnp.float32)
        out_ref[h, cols * states : cols * states + cols, 0:slots] = codes


def arrange(flags, blist, slab):
    all_states, _, cols, size = slab.shape
    return pl.pallas_call(
        arrange_kernel,
        in_specs=[VMEM] * 3,
        out_specs=VMEM,
        out_shape=jax.ShapeDtypeStruct((2, cols * all_states // 2 + VEC, size), jnp.float32),
        compiler_params=pltpu.CompilerParams(vmem_limit_bytes=LIMIT),
        name="arrange",
    )(flags, blist, slab)


def pick_kernel(flags_ref, own_ref, core_ref, border_ref, inner_ref):
    shape = own_ref.shape[3:]
    edge, half = flag(flags_ref, 1, shape), flag(flags_ref, 2, shape)
    for k in range(own_ref.shape[2]):
        own = jnp.where(half, own_ref[0, 1, k], own_ref[0, 0, k])
        core = jnp.where(half, core_ref[0, 1, k], core_ref[0, 0, k])
        border_ref[0, 0, k] = jnp.where(edge, own, core)
        inner_ref[0, 0, k] = jnp.where(edge, core, own)


def pick(flags, own, core):
    rows, cols, *block = own.shape
    return pl.pallas_call(
        pick_kernel,
        in_specs=[VMEM] * 3,
        out_specs=[VMEM] * 2,
        out_shape=[jax.ShapeDtypeStruct((rows, 1, *block), own.dtype)] * 2,
        compiler_params=pltpu.CompilerParams(vmem_limit_bytes=LIMIT),
        name="pick",
    )(flags, own, core)


def prepare_kernel(mode, codes_ref, *refs):
    *h_refs, out_ref = refs
    _, cols, slots, size, _ = h_refs[0].shape
    odd, edge, half, x = (codes_ref[n] for n in range(4))
    out_ref[...] = jnp.zeros_like(out_ref)

    def convert(h_ref, h_col, c, q, row):
        u = jnp.bitwise_xor(c, odd)
        for k in range(slots):
            code = codes_ref[4 + (row * 2 + c) * slots + k]
            down = (code >= 3).astype(jnp.int32) + (code >= 6).astype(jnp.int32)
            along = code - 3 * down
            down = jnp.where(x == 1, 2 - down, down)
            along = u + jnp.where(odd == 1, 2 - along, along)
            rim = (along == 0) | (along == 3)
            block = jnp.where(rim, 6 + down, 2 * down + along - 1)
            lanes = pl.ds(pl.multiple_of(block * size, size), size)
            high, low = split(h_ref[0, h_col, k])
            out_ref[q, u, 0:size, lanes] = high
            out_ref[q, u, size : 2 * size, lanes] = low

    for h, h_ref in enumerate(h_refs):
        if mode == "chip":
            for c in range(cols):
                convert(h_ref, c, c, jnp.bitwise_xor(edge, h), h)
        else:
            row = 3 - edge if mode == "border" else 2 + edge
            convert(h_ref, 0, jnp.bitwise_xor(half, h), 0, row)


def prepare(mode, codes, *h_rows):
    _, _, slots, size, _ = h_rows[0].shape
    rows = 2 if mode == "chip" else 1
    return pl.pallas_call(
        functools.partial(prepare_kernel, mode),
        in_specs=[SMEM] + [VMEM] * len(h_rows),
        out_specs=VMEM,
        out_shape=jax.ShapeDtypeStruct((rows, 2, 2 * size, BLOCKS * size), jnp.bfloat16),
        compiler_params=pltpu.CompilerParams(vmem_limit_bytes=LIMIT),
        name="prepare_" + mode,
    )(codes, *h_rows)


def fill(x_ref, fields):
    rows, states, size = fields[0].shape
    for q in range(rows):
        for n, field in enumerate(fields):
            at = (q * len(fields) + n) * size
            high, low = split(field[q])
            x_ref[0:states, at : at + size] = high
            x_ref[states : 2 * states, at : at + size] = low


def step_kernel(kind, u, count, *refs):
    h_refs, (own_0, own_1, rim_ref, *refs) = refs[:count], refs[count:]
    *refs, own_x, rim_x = refs
    before, refs = (None, refs) if kind == "first" else (refs[0], refs[1:])
    rows_in, states, size = rim_ref.shape
    h_rows = [h_ref.at[q] for h_ref in h_refs for q in range(h_ref.shape[0])]
    fill(own_x, [own_0, own_1])
    fill(rim_x, [rim_ref])
    values = []
    for q, h_row in enumerate(h_rows):
        low, high = max(q - 1, 0), min(q + 2, rows_in)
        acc = 0.0
        for x_ref, width, first in ((own_x, 2 * size, 0), (rim_x, size, 6 * size)):
            at = first + (low - q + 1) * width
            acc = acc + lax.dot_general(
                x_ref[:, low * width : high * width],
                h_row[u, :, at : at + (high - low) * width],
                NT,
                preferred_element_type=jnp.float32,
            )
        small = acc[states:, size:] + (acc[states:, :size] + acc[:states, size:])
        value = acc[:states, :size] + small
        values.append(value if kind == "first" else 2.0 * value - before[q])
    if kind in ("other", "last"):
        flat = [jnp.concatenate(part, axis=1) for part in zip(*map(split, values))]
        flat = jnp.concatenate(flat)
        gram = lax.dot_general(flat, flat, NT, preferred_element_type=jnp.float32)
        gram = gram[:states] + gram[states:]
        gram = gram[:, :states] + gram[:, states:]
    if kind != "last":
        for q, value in enumerate(values):
            refs[0][q] = value
        if kind == "other":
            refs[1][:, 0:states] = gram
        return
    other_ref, other_gram_ref, flags_ref, kept_ref, sent_ref = refs
    odd, edge = flag(flags_ref, 0, (states, size)), flag(flags_ref, 1, (states, size))
    nodes = [[other_ref[q] for q in range(len(values))], values]
    gram = gram + other_gram_ref[:, 0:states]
    blocks = states // VEC
    for c in range(2):
        inner = jnp.where(odd, nodes[1 - c][0], nodes[c][0])
        border = jnp.where(odd, nodes[1 - c][1], nodes[c][1])
        kept, sent = jnp.where(edge, border, inner), jnp.where(edge, inner, border)
        for b in range(blocks):
            rows = slice(b * VEC, (b + 1) * VEC)
            kept_ref[blocks - 1 - b, c * VEC : (c + 1) * VEC, :] = kept[rows]
            sent_ref[blocks - 1 - b, c * VEC : (c + 1) * VEC, :] = sent[rows]
    for b in range(blocks):
        rows = slice(b * VEC, (b + 1) * VEC)
        for ref in (kept_ref, sent_ref):
            ref[blocks - 1 - b, 2 * VEC :, :] = jnp.zeros((VEC, size), jnp.float32)
            ref[blocks - 1 - b, 2 * VEC :, 0:VEC] = gram[rows, rows]


def step(kind, u, name, h_ready, own, rim, *others):
    rows_in, states, size = rim.shape
    rows_out = sum(h.shape[0] for h in h_ready)
    shapes = [(rows_out, states, size)]
    if kind == "other":
        shapes.append((states, pl.cdiv(states, size) * size))
    elif kind == "last":
        blocks = states // VEC
        shapes = [(blocks, 3 * VEC, size)] * 2
    operands = [*h_ready, *own, rim, *others]
    cost = pl.CostEstimate(
        flops=8 * BLOCKS * rows_out * states * size * size,
        bytes_accessed=4 * BLOCKS * rows_out * size * size,
        transcendentals=0,
    )
    outs = pl.pallas_call(
        functools.partial(step_kernel, kind, u, len(h_ready)),
        in_specs=[VMEM] * len(operands),
        out_specs=[VMEM] * len(shapes),
        out_shape=[jax.ShapeDtypeStruct(shape, jnp.float32) for shape in shapes],
        scratch_shapes=[
            pltpu.VMEM((2 * states, rows_in * width * size), jnp.bfloat16) for width in (2, 1)
        ],
        compiler_params=pltpu.CompilerParams(vmem_limit_bytes=LIMIT),
        cost_estimate=cost,
        name=name,
    )(*operands)
    return outs[0] if len(outs) == 1 else outs


def finish_kernel(cols, node_count, flags_ref, parts_ref, rot_ref, out_ref):
    wide = parts_ref.shape[0]
    gram = parts_ref[0, cols * VEC : (cols + 1) * VEC, 0:VEC]
    for w in range(1, wide):
        gram = gram + parts_ref[w, cols * VEC : (cols + 1) * VEC, 0:VEC]
    gram = gram / node_count
    row = lax.broadcasted_iota(jnp.int32, (VEC, VEC), 0)
    col = lax.broadcasted_iota(jnp.int32, (VEC, VEC), 1)
    both = jnp.concatenate([gram, jnp.where(row == col, 1.0, 0.0).astype(jnp.float32)], axis=1)
    below = lax.broadcasted_iota(jnp.int32, both.shape, 0)
    for k in range(VEC - 1):
        factor = both[:, k : k + 1] * (1.0 / both[k : k + 1, k : k + 1])
        both = jnp.where(below > k, both - factor * both[k : k + 1, :], both)
    pivots = jnp.sum(jnp.where(row == col, both[:, :VEC], 0.0), axis=1, keepdims=True)
    inverse = both[:, VEC:] * (1.0 / jnp.sqrt(pivots))
    turn = rot_ref[...]
    mixer = turn[:, 0:1] * inverse[0:1, :]
    for k in range(1, VEC):
        mixer = mixer + turn[:, k : k + 1] * inverse[k : k + 1, :]
    columns = [mixer[:, d : d + 1] for d in range(VEC)]
    mixed = []
    for w in range(wide):
        for c in range(cols):
            block = parts_ref[w, c * VEC : (c + 1) * VEC, :]
            total = columns[0] * block[0:1, :]
            for d in range(1, VEC):
                total = total + columns[d] * block[d : d + 1, :]
            mixed.append(total)
    half = flag(flags_ref, 2, mixed[0].shape)
    for w in range(wide):
        for c in range(cols):
            first = mixed[(wide - 1 - w) * cols + c]
            second = mixed[(wide - 1 - w + wide // 2) % wide * cols + c]
            out_ref[:, 0, w * cols + c, :] = jnp.where(half, second, first)


def finish(flags, cols, node_count, parts, turn):
    wide, _, size = parts.shape
    return pl.pallas_call(
        functools.partial(finish_kernel, cols, node_count),
        in_specs=[VMEM] * 3,
        out_specs=VMEM,
        out_shape=jax.ShapeDtypeStruct((VEC, 1, wide * cols, size), jnp.float32),
        compiler_params=pltpu.CompilerParams(vmem_limit_bytes=LIMIT),
        name="finish",
    )(flags, parts, turn)


def after(x, token):
    return lax.optimization_barrier((x, token))[0]


def body(slab, hblocks, blist, rotation):
    wide, grp = lax.axis_size("wide"), lax.axis_size("grp")
    _, _, cols, size = slab.shape
    slots = hblocks.shape[2]
    near = [(i, i ^ 1) for i in range(wide)]
    far = [(i, ((i + 1) ^ 1) - 1) for i in range(1, wide - 1)]
    mine, odd = lax.axis_index("grp"), lax.axis_index("wide") % 2
    x = mine // 2
    edge = half = x ^ (mine % 2)
    place = jnp.stack([odd, edge, half, x]).astype(jnp.int32)
    flags = jnp.broadcast_to(jnp.repeat(place, VEC)[:, None], (4 * VEC, size))

    def across(value):
        return lax.ppermute(value, "grp", [(i, i ^ 3) for i in range(grp)])

    def core(value):
        return lax.ppermute(value, "grp", [(i, i ^ 1) for i in range(grp)])

    def over_far(value):
        return lax.ppermute(value, "wide", far)

    def over_near(value):
        return lax.ppermute(value, "wide", near)

    own = arrange(flags, blist, slab)
    own_core = core(own[1])
    h_core = core(hblocks)
    border, inside = pick(flags, hblocks, h_core)
    own_across = across(after(jnp.stack([own[0], own_core]), border))
    rows = [own[0], own_core, own_across[0], own_across[1]]
    codes = jnp.stack([row[-VEC : cols - VEC, :slots] for row in rows]).astype(jnp.int32).reshape(-1)
    codes = jnp.concatenate([place, codes])
    states = (own.shape[1] - VEC) // cols
    zero = []
    for u in range(cols):
        parts = [row[u * states : (u + 1) * states] for row in rows]
        border_mine = jnp.stack([parts[m] for m in (1, 0, 2, 3)])
        border_core = jnp.stack([parts[m] for m in (0, 1, 3, 2)])
        zero.append(jnp.where(edge == 1, border_mine, border_core))

    zero[0] = after(zero[0], zero[1])
    far_rim, near_rim = over_far(zero[0]), over_near(zero[1])
    border = across(after(border, own_core))
    inside = across(after(inside, border))
    h_two = [prepare("chip", after(codes, near_rim), hblocks, h_core)]
    border_core = core(after(border, (far_rim, h_two)))
    h_three = h_two + [prepare("border", codes, border, border_core)]

    one = [step("first", 0, "one_0", h_three, zero, far_rim)]
    rim = after(near_rim, one[0])
    one.append(step("first", 1, "one_1", h_three, zero, rim))
    rims = over_far(one[0]), over_near(one[1])
    two, sent, before = [], (), []
    for u in range(cols):
        rim = after(rims[u], (sent, inside))
        two.append(step("next", u, f"two_{u}", h_two, one, rim, zero[u]))
        sent = jnp.concatenate([two[u], one[u][:1]])
        other = across(sent)
        two[u] = jnp.concatenate([two[u], other[1:2], other[0:1]])
        before.append(jnp.concatenate([one[u], other[2:]]))
    inside_core = core(after(inside, two[0]))
    h_four = h_three + [prepare("inner", codes, inside, inside_core)]
    rims = over_far(two[0]), over_near(two[1])
    three = [step("next", 0, "three_0", h_four, two, rims[0], before[0])]
    rim = after(rims[1], three[0])
    three.append(step("next", 1, "three_1", h_four, two, rim, before[1]))
    rims = over_far(three[0]), over_near(three[1])
    four = step("other", 0, "four_0", h_four, three, rims[0], two[0])
    kept, sent = step("last", 1, "four_1", h_four, three, rims[1], two[1], *four, flags)

    packed = jnp.concatenate([core(sent), kept])
    owners = wide // 2
    groups = [
        [((wide - 1 - i + owners * (g // 2 ^ g % 2)) % wide) * grp + g for i in range(wide)]
        for g in range(grp)
    ]
    packed = lax.all_to_all(
        packed,
        ("wide", "grp"),
        split_axis=0,
        concat_axis=0,
        tiled=True,
        axis_index_groups=groups,
    )
    turn = lax.dynamic_index_in_dim(rotation, lax.axis_index("wide"), 0, keepdims=False)
    node_count = grp * wide * cols * size
    return finish(flags, cols, node_count, packed, turn.T)


def solution(mesh):
    in_specs = (
        P(None, "grp", "wide", None),
        P("grp", "wide", None, None, None),
        P("grp", "wide", None),
        P(),
    )
    out_specs = P("wide", "grp", None, None)
    return jax.shard_map(body, mesh=mesh, in_specs=in_specs, out_specs=out_specs, check_vma=False)
```

```python
import functools

import jax
import jax.numpy as jnp
from jax import lax
from jax.experimental import pallas as pl
from jax.experimental.pallas import tpu as pltpu
from jax.sharding import PartitionSpec as P

VEC = 8
DEG = 4
LIMIT = 16 * 2**20
BLOCKS = 9
VMEM = pl.BlockSpec(memory_space=pltpu.VMEM)
SMEM = pl.BlockSpec(memory_space=pltpu.SMEM)
NT = (((1,), (1,)), ((), ()))


def split(x):
    high = x.astype(jnp.bfloat16)
    low = (x - high.astype(jnp.float32)).astype(jnp.bfloat16)
    return high, low


def flag(flags_ref, n, shape):
    return jnp.broadcast_to(flags_ref[n * VEC : n * VEC + 1, :], shape) == 1


def arrange_kernel(flags_ref, codes_ref, slab_ref, out_ref):
    all_states, _, cols, size = slab_ref.shape
    slots, states = codes_ref.shape[2], all_states // 2
    odd = flag(flags_ref, 0, (all_states, size))
    second = flag(flags_ref, 2, (states, size))
    both = [slab_ref[:, 0, c, :] for c in range(cols)]
    for u in range(cols):
        value = jnp.where(odd, both[cols - 1 - u], both[u])
        low, high = value[:states], value[states:]
        rows = slice(u * states, (u + 1) * states)
        out_ref[0, rows, :] = jnp.where(second, high, low)
        out_ref[1, rows, :] = jnp.where(second, low, high)
    codes = codes_ref[0].astype(jnp.float32)
    for h in range(2):
        out_ref[h, cols * states :, :] = jnp.zeros((VEC, size), jnp.float32)
        out_ref[h, cols * states : cols * states + cols, 0:slots] = codes


def arrange(flags, blist, slab):
    all_states, _, cols, size = slab.shape
    return pl.pallas_call(
        arrange_kernel,
        in_specs=[VMEM] * 3,
        out_specs=VMEM,
        out_shape=jax.ShapeDtypeStruct((2, cols * all_states // 2 + VEC, size), jnp.float32),
        compiler_params=pltpu.CompilerParams(vmem_limit_bytes=LIMIT),
        name="arrange",
    )(flags, blist, slab)


def pick_kernel(flags_ref, own_ref, core_ref, border_ref, inner_ref):
    shape = own_ref.shape[3:]
    edge, half = flag(flags_ref, 1, shape), flag(flags_ref, 2, shape)
    for k in range(own_ref.shape[2]):
        own = jnp.where(half, own_ref[0, 1, k], own_ref[0, 0, k])
        core = jnp.where(half, core_ref[0, 1, k], core_ref[0, 0, k])
        border_ref[0, 0, k] = jnp.where(edge, own, core)
        inner_ref[0, 0, k] = jnp.where(edge, core, own)


def pick(flags, own, core):
    rows, cols, *block = own.shape
    return pl.pallas_call(
        pick_kernel,
        in_specs=[VMEM] * 3,
        out_specs=[VMEM] * 2,
        out_shape=[jax.ShapeDtypeStruct((rows, 1, *block), own.dtype)] * 2,
        compiler_params=pltpu.CompilerParams(vmem_limit_bytes=LIMIT),
        name="pick",
    )(flags, own, core)


def prepare_kernel(mode, codes_ref, *refs):
    *h_refs, out_ref = refs
    _, cols, slots, size, _ = h_refs[0].shape
    odd, edge, half, x = (codes_ref[n] for n in range(4))
    out_ref[...] = jnp.zeros_like(out_ref)

    def convert(h_ref, h_col, c, q, row):
        u = jnp.bitwise_xor(c, odd)
        for k in range(slots):
            code = codes_ref[4 + (row * 2 + c) * slots + k]
            down = (code >= 3).astype(jnp.int32) + (code >= 6).astype(jnp.int32)
            along = code - 3 * down
            down = jnp.where(x == 1, 2 - down, down)
            along = u + jnp.where(odd == 1, 2 - along, along)
            rim = (along == 0) | (along == 3)
            block = jnp.where(rim, 6 + down, 2 * down + along - 1)
            lanes = pl.ds(pl.multiple_of(block * size, size), size)
            high, low = split(h_ref[0, h_col, k])
            out_ref[q, u, 0:size, lanes] = high
            out_ref[q, u, size : 2 * size, lanes] = low

    for h, h_ref in enumerate(h_refs):
        if mode == "chip":
            for c in range(cols):
                convert(h_ref, c, c, jnp.bitwise_xor(edge, h), h)
        else:
            row = 3 - edge if mode == "border" else 2 + edge
            convert(h_ref, 0, jnp.bitwise_xor(half, h), 0, row)


def prepare(mode, codes, *h_rows):
    _, _, slots, size, _ = h_rows[0].shape
    rows = 2 if mode == "chip" else 1
    return pl.pallas_call(
        functools.partial(prepare_kernel, mode),
        in_specs=[SMEM] + [VMEM] * len(h_rows),
        out_specs=VMEM,
        out_shape=jax.ShapeDtypeStruct((rows, 2, 2 * size, BLOCKS * size), jnp.bfloat16),
        compiler_params=pltpu.CompilerParams(vmem_limit_bytes=LIMIT),
        name="prepare_" + mode,
    )(codes, *h_rows)


def fill(x_ref, fields):
    rows, states, size = fields[0].shape
    for q in range(rows):
        for n, field in enumerate(fields):
            at = (q * len(fields) + n) * size
            high, low = split(field[q])
            x_ref[0:states, at : at + size] = high
            x_ref[states : 2 * states, at : at + size] = low


def step_kernel(kind, u, count, *refs):
    h_refs, (own_0, own_1, rim_ref, *refs) = refs[:count], refs[count:]
    *refs, own_x, rim_x = refs
    before, refs = (None, refs) if kind == "first" else (refs[0], refs[1:])
    rows_in, states, size = rim_ref.shape
    h_rows = [h_ref.at[q] for h_ref in h_refs for q in range(h_ref.shape[0])]
    fill(own_x, [own_0, own_1])
    fill(rim_x, [rim_ref])
    values = []
    for q, h_row in enumerate(h_rows):
        low, high = max(q - 1, 0), min(q + 2, rows_in)
        acc = 0.0
        for x_ref, width, first in ((own_x, 2 * size, 0), (rim_x, size, 6 * size)):
            at = first + (low - q + 1) * width
            acc = acc + lax.dot_general(
                x_ref[:, low * width : high * width],
                h_row[u, :, at : at + (high - low) * width],
                NT,
                preferred_element_type=jnp.float32,
            )
        small = acc[states:, size:] + (acc[states:, :size] + acc[:states, size:])
        value = acc[:states, :size] + small
        values.append(value if kind == "first" else 2.0 * value - before[q])
    if kind in ("other", "last"):
        flat = [jnp.concatenate(part, axis=1) for part in zip(*map(split, values))]
        flat = jnp.concatenate(flat)
        gram = lax.dot_general(flat, flat, NT, preferred_element_type=jnp.float32)
        gram = gram[:states] + gram[states:]
        gram = gram[:, :states] + gram[:, states:]
    if kind != "last":
        for q, value in enumerate(values):
            refs[0][q] = value
        if kind == "other":
            refs[1][:, 0:states] = gram
        return
    other_ref, other_gram_ref, flags_ref, kept_ref, sent_ref = refs
    odd, edge = flag(flags_ref, 0, (states, size)), flag(flags_ref, 1, (states, size))
    nodes = [[other_ref[q] for q in range(len(values))], values]
    gram = gram + other_gram_ref[:, 0:states]
    blocks = states // VEC
    for c in range(2):
        inner = jnp.where(odd, nodes[1 - c][0], nodes[c][0])
        border = jnp.where(odd, nodes[1 - c][1], nodes[c][1])
        kept, sent = jnp.where(edge, border, inner), jnp.where(edge, inner, border)
        for b in range(blocks):
            rows = slice(b * VEC, (b + 1) * VEC)
            kept_ref[-b % blocks, c * VEC : (c + 1) * VEC, :] = kept[rows]
            sent_ref[blocks - 1 - b, c * VEC : (c + 1) * VEC, :] = sent[rows]
    for b in range(blocks):
        rows = slice(b * VEC, (b + 1) * VEC)
        for ref, at in ((kept_ref, -b % blocks), (sent_ref, blocks - 1 - b)):
            ref[at, 2 * VEC :, :] = jnp.zeros((VEC, size), jnp.float32)
            ref[at, 2 * VEC :, 0:VEC] = gram[rows, rows]


def step(kind, u, name, h_ready, own, rim, *others):
    rows_in, states, size = rim.shape
    rows_out = sum(h.shape[0] for h in h_ready)
    shapes = [(rows_out, states, size)]
    if kind == "other":
        shapes.append((states, pl.cdiv(states, size) * size))
    elif kind == "last":
        blocks = states // VEC
        shapes = [(blocks, 3 * VEC, size)] * 2
    operands = [*h_ready, *own, rim, *others]
    cost = pl.CostEstimate(
        flops=8 * BLOCKS * rows_out * states * size * size,
        bytes_accessed=4 * BLOCKS * rows_out * size * size,
        transcendentals=0,
    )
    outs = pl.pallas_call(
        functools.partial(step_kernel, kind, u, len(h_ready)),
        in_specs=[VMEM] * len(operands),
        out_specs=[VMEM] * len(shapes),
        out_shape=[jax.ShapeDtypeStruct(shape, jnp.float32) for shape in shapes],
        scratch_shapes=[
            pltpu.VMEM((2 * states, rows_in * width * size), jnp.bfloat16) for width in (2, 1)
        ],
        compiler_params=pltpu.CompilerParams(vmem_limit_bytes=LIMIT),
        cost_estimate=cost,
        name=name,
    )(*operands)
    return outs[0] if len(outs) == 1 else outs


def finish_kernel(cols, node_count, flags_ref, parts_ref, rot_ref, out_ref):
    wide = parts_ref.shape[0]
    gram = parts_ref[0, cols * VEC : (cols + 1) * VEC, 0:VEC]
    for w in range(1, wide):
        gram = gram + parts_ref[w, cols * VEC : (cols + 1) * VEC, 0:VEC]
    gram = gram / node_count
    row = lax.broadcasted_iota(jnp.int32, (VEC, VEC), 0)
    col = lax.broadcasted_iota(jnp.int32, (VEC, VEC), 1)
    inverse = jnp.where(row == col, 1.0, 0.0).astype(jnp.float32)
    for k in range(VEC):
        scale = 1.0 / jnp.sqrt(gram[k : k + 1, k : k + 1])
        top = gram[k : k + 1, :] * scale
        top_inverse = inverse[k : k + 1, :] * scale
        factor = gram[:, k : k + 1] * scale
        gram = gram - factor * top
        inverse = jnp.where(row == k, top_inverse, jnp.where(row > k, inverse - factor * top_inverse, inverse))
    turn = rot_ref[...]
    mixer = turn[:, 0:1] * inverse[0:1, :]
    for k in range(1, VEC):
        mixer = mixer + turn[:, k : k + 1] * inverse[k : k + 1, :]
    columns = [mixer[:, d : d + 1] for d in range(VEC)]
    mixed = []
    for w in range(wide):
        for c in range(cols):
            block = parts_ref[w, c * VEC : (c + 1) * VEC, :]
            total = columns[0] * block[0:1, :]
            for d in range(1, VEC):
                total = total + columns[d] * block[d : d + 1, :]
            mixed.append(total)
    half = flag(flags_ref, 2, mixed[0].shape)
    for w in range(wide):
        for c in range(cols):
            first = mixed[-w % wide * cols + c]
            second = mixed[(wide // 2 - w) % wide * cols + c]
            out_ref[:, 0, w * cols + c, :] = jnp.where(half, second, first)


def finish(flags, cols, node_count, parts, turn):
    wide, _, size = parts.shape
    return pl.pallas_call(
        functools.partial(finish_kernel, cols, node_count),
        in_specs=[VMEM] * 3,
        out_specs=VMEM,
        out_shape=jax.ShapeDtypeStruct((VEC, 1, wide * cols, size), jnp.float32),
        compiler_params=pltpu.CompilerParams(vmem_limit_bytes=LIMIT),
        name="finish",
    )(flags, parts, turn)


def after(x, token):
    return lax.optimization_barrier((x, token))[0]


def body(slab, hblocks, blist, rotation):
    wide, grp = lax.axis_size("wide"), lax.axis_size("grp")
    _, _, cols, size = slab.shape
    slots = hblocks.shape[2]
    near = [(i, i ^ 1) for i in range(wide)]
    far = [(i, ((i + 1) ^ 1) - 1) for i in range(1, wide - 1)]
    mine, odd = lax.axis_index("grp"), lax.axis_index("wide") % 2
    x = mine // 2
    edge = half = x ^ (mine % 2)
    place = jnp.stack([odd, edge, half, x]).astype(jnp.int32)
    flags = jnp.broadcast_to(jnp.repeat(place, VEC)[:, None], (4 * VEC, size))

    def across(value):
        return lax.ppermute(value, "grp", [(i, i ^ 3) for i in range(grp)])

    def core(value):
        return lax.ppermute(value, "grp", [(i, i ^ 1) for i in range(grp)])

    def over_far(value):
        return lax.ppermute(value, "wide", far)

    def over_near(value):
        return lax.ppermute(value, "wide", near)

    own = arrange(flags, blist, slab)
    own_core = core(own[1])
    h_core = core(hblocks)
    border, inside = pick(flags, hblocks, h_core)
    own_across = across(after(jnp.stack([own[0], own_core]), border))
    rows = [own[0], own_core, own_across[0], own_across[1]]
    codes = jnp.stack([row[-VEC : cols - VEC, :slots] for row in rows]).astype(jnp.int32).reshape(-1)
    codes = jnp.concatenate([place, codes])
    states = (own.shape[1] - VEC) // cols
    zero = []
    for u in range(cols):
        parts = [row[u * states : (u + 1) * states] for row in rows]
        border_mine = jnp.stack([parts[m] for m in (1, 0, 2, 3)])
        border_core = jnp.stack([parts[m] for m in (0, 1, 3, 2)])
        zero.append(jnp.where(edge == 1, border_mine, border_core))

    zero[1] = after(zero[1], zero[0])
    far_rim, near_rim = over_far(zero[0]), over_near(zero[1])
    border = across(after(border, own_core))
    inside = across(after(inside, near_rim))
    h_two = [prepare("chip", codes, hblocks, h_core)]
    border_core = core(after(border, (far_rim, h_two)))
    h_three = h_two + [prepare("border", codes, border, border_core)]

    one = [step("first", 0, "one_0", h_three, zero, far_rim)]
    rim = after(near_rim, one[0])
    one.append(step("first", 1, "one_1", h_three, zero, rim))
    rims = over_far(one[0]), over_near(one[1])
    two, sent, before = [], (), []
    for u in range(cols):
        rim = after(rims[u], (sent, inside))
        two.append(step("next", u, f"two_{u}", h_two, one, rim, zero[u]))
        sent = jnp.concatenate([two[u], one[u][:1]])
        other = across(sent)
        two[u] = jnp.concatenate([two[u], other[1:2], other[0:1]])
        before.append(jnp.concatenate([one[u], other[2:]]))
    inside_core = core(after(inside, two[0]))
    h_four = h_three + [prepare("inner", codes, inside, inside_core)]
    rims = over_far(two[0]), over_near(two[1])
    three = [step("next", 0, "three_0", h_four, two, rims[0], before[0])]
    rim = after(rims[1], three[0])
    three.append(step("next", 1, "three_1", h_four, two, rim, before[1]))
    rims = over_far(three[0]), over_near(three[1])
    four = step("other", 0, "four_0", h_four, three, rims[0], two[0])
    kept, sent = step("last", 1, "four_1", h_four, three, rims[1], two[1], *four, flags)

    packed = jnp.concatenate([kept[:1], core(sent), kept[1:]])
    owners = wide // 2
    groups = [
        [((wide - i + owners * (g // 2 ^ g % 2)) % wide) * grp + g for i in range(wide)]
        for g in range(grp)
    ]
    packed = lax.all_to_all(
        packed,
        ("wide", "grp"),
        split_axis=0,
        concat_axis=0,
        tiled=True,
        axis_index_groups=groups,
    )
    turn = lax.dynamic_index_in_dim(rotation, lax.axis_index("wide"), 0, keepdims=False)
    node_count = grp * wide * cols * size
    return finish(flags, cols, node_count, packed, turn.T)


def solution(mesh):
    in_specs = (
        P(None, "grp", "wide", None),
        P("grp", "wide", None, None, None),
        P("grp", "wide", None),
        P(),
    )
    out_specs = P("wide", "grp", None, None)
    return jax.shard_map(body, mesh=mesh, in_specs=in_specs, out_specs=out_specs, check_vma=False)
```

```python
import functools

import jax
import jax.numpy as jnp
from jax import lax
from jax.experimental import pallas as pl
from jax.experimental.pallas import tpu as pltpu
from jax.sharding import PartitionSpec as P

VEC = 8
DEG = 4
LIMIT = 16 * 2**20
BLOCKS = 9
VMEM = pl.BlockSpec(memory_space=pltpu.VMEM)
SMEM = pl.BlockSpec(memory_space=pltpu.SMEM)
NT = (((1,), (1,)), ((), ()))


def split(x):
    high = x.astype(jnp.bfloat16)
    low = (x - high.astype(jnp.float32)).astype(jnp.bfloat16)
    return high, low


def flag(flags_ref, n, shape):
    return jnp.broadcast_to(flags_ref[n * VEC : n * VEC + 1, :], shape) == 1


def arrange_kernel(flags_ref, codes_ref, slab_ref, out_ref):
    all_states, _, cols, size = slab_ref.shape
    slots, states = codes_ref.shape[2], all_states // 2
    odd = flag(flags_ref, 0, (all_states, size))
    second = flag(flags_ref, 2, (states, size))
    both = [slab_ref[:, 0, c, :] for c in range(cols)]
    for u in range(cols):
        value = jnp.where(odd, both[cols - 1 - u], both[u])
        low, high = value[:states], value[states:]
        rows = slice(u * states, (u + 1) * states)
        out_ref[0, rows, :] = jnp.where(second, high, low)
        out_ref[1, rows, :] = jnp.where(second, low, high)
    codes = codes_ref[0].astype(jnp.float32)
    for h in range(2):
        out_ref[h, cols * states :, :] = jnp.zeros((VEC, size), jnp.float32)
        out_ref[h, cols * states : cols * states + cols, 0:slots] = codes


def arrange(flags, blist, slab):
    all_states, _, cols, size = slab.shape
    return pl.pallas_call(
        arrange_kernel,
        in_specs=[VMEM] * 3,
        out_specs=VMEM,
        out_shape=jax.ShapeDtypeStruct((2, cols * all_states // 2 + VEC, size), jnp.float32),
        compiler_params=pltpu.CompilerParams(vmem_limit_bytes=LIMIT),
        name="arrange",
    )(flags, blist, slab)


def pick_kernel(flags_ref, own_ref, core_ref, border_ref, inner_ref):
    shape = own_ref.shape[3:]
    edge, half = flag(flags_ref, 1, shape), flag(flags_ref, 2, shape)
    for k in range(own_ref.shape[2]):
        own = jnp.where(half, own_ref[0, 1, k], own_ref[0, 0, k])
        core = jnp.where(half, core_ref[0, 1, k], core_ref[0, 0, k])
        border_ref[0, 0, k] = jnp.where(edge, own, core)
        inner_ref[0, 0, k] = jnp.where(edge, core, own)


def pick(flags, own, core):
    rows, cols, *block = own.shape
    return pl.pallas_call(
        pick_kernel,
        in_specs=[VMEM] * 3,
        out_specs=[VMEM] * 2,
        out_shape=[jax.ShapeDtypeStruct((rows, 1, *block), own.dtype)] * 2,
        compiler_params=pltpu.CompilerParams(vmem_limit_bytes=LIMIT),
        name="pick",
    )(flags, own, core)


def prepare_kernel(mode, codes_ref, *refs):
    *h_refs, out_ref = refs
    _, cols, slots, size, _ = h_refs[0].shape
    odd, edge, half, x = (codes_ref[n] for n in range(4))
    out_ref[...] = jnp.zeros_like(out_ref)

    def convert(h_ref, h_col, c, q, row):
        u = jnp.bitwise_xor(c, odd)
        for k in range(slots):
            code = codes_ref[4 + (row * 2 + c) * slots + k]
            down = (code >= 3).astype(jnp.int32) + (code >= 6).astype(jnp.int32)
            along = code - 3 * down
            down = jnp.where(x == 1, 2 - down, down)
            along = u + jnp.where(odd == 1, 2 - along, along)
            rim = (along == 0) | (along == 3)
            block = jnp.where(rim, 6 + down, 2 * down + along - 1)
            lanes = pl.ds(pl.multiple_of(block * size, size), size)
            high, low = split(h_ref[0, h_col, k])
            out_ref[q, u, 0:size, lanes] = high
            out_ref[q, u, size : 2 * size, lanes] = low

    for h, h_ref in enumerate(h_refs):
        if mode == "chip":
            for c in range(cols):
                convert(h_ref, c, c, jnp.bitwise_xor(edge, h), h)
        else:
            row = 3 - edge if mode == "border" else 2 + edge
            convert(h_ref, 0, jnp.bitwise_xor(half, h), 0, row)


def prepare(mode, codes, *h_rows):
    _, _, slots, size, _ = h_rows[0].shape
    rows = 2 if mode == "chip" else 1
    return pl.pallas_call(
        functools.partial(prepare_kernel, mode),
        in_specs=[SMEM] + [VMEM] * len(h_rows),
        out_specs=VMEM,
        out_shape=jax.ShapeDtypeStruct((rows, 2, 2 * size, BLOCKS * size), jnp.bfloat16),
        compiler_params=pltpu.CompilerParams(vmem_limit_bytes=LIMIT),
        name="prepare_" + mode,
    )(codes, *h_rows)


def fill(x_ref, fields):
    rows, states, size = fields[0].shape
    for q in range(rows):
        for n, field in enumerate(fields):
            at = (q * len(fields) + n) * size
            high, low = split(field[q])
            x_ref[0:states, at : at + size] = high
            x_ref[states : 2 * states, at : at + size] = low


def step_kernel(kind, u, count, *refs):
    h_refs, (own_0, own_1, rim_ref, *refs) = refs[:count], refs[count:]
    *refs, own_x, rim_x = refs
    before, refs = (None, refs) if kind == "first" else (refs[0], refs[1:])
    rows_in, states, size = rim_ref.shape
    h_rows = [h_ref.at[q] for h_ref in h_refs for q in range(h_ref.shape[0])]
    fill(own_x, [own_0, own_1])
    fill(rim_x, [rim_ref])
    values = []
    for q, h_row in enumerate(h_rows):
        low, high = max(q - 1, 0), min(q + 2, rows_in)
        acc = 0.0
        for x_ref, width, first in ((own_x, 2 * size, 0), (rim_x, size, 6 * size)):
            at = first + (low - q + 1) * width
            acc = acc + lax.dot_general(
                x_ref[:, low * width : high * width],
                h_row[u, :, at : at + (high - low) * width],
                NT,
                preferred_element_type=jnp.float32,
            )
        small = acc[states:, size:] + (acc[states:, :size] + acc[:states, size:])
        value = acc[:states, :size] + small
        values.append(value if kind == "first" else 2.0 * value - before[q])
    if kind in ("other", "last"):
        flat = [jnp.concatenate(part, axis=1) for part in zip(*map(split, values))]
        flat = jnp.concatenate(flat)
        gram = lax.dot_general(flat, flat, NT, preferred_element_type=jnp.float32)
        gram = gram[:states] + gram[states:]
        gram = gram[:, :states] + gram[:, states:]
    if kind != "last":
        for q, value in enumerate(values):
            refs[0][q] = value
        if kind == "other":
            refs[1][:, 0:states] = gram
        return
    other_ref, other_gram_ref, flags_ref, kept_ref, sent_ref = refs
    odd, edge = flag(flags_ref, 0, (states, size)), flag(flags_ref, 1, (states, size))
    nodes = [[other_ref[q] for q in range(len(values))], values]
    gram = gram + other_gram_ref[:, 0:states]
    blocks = states // VEC
    for c in range(2):
        inner = jnp.where(odd, nodes[1 - c][0], nodes[c][0])
        border = jnp.where(odd, nodes[1 - c][1], nodes[c][1])
        kept, sent = jnp.where(edge, border, inner), jnp.where(edge, inner, border)
        for b in range(blocks):
            rows = slice(b * VEC, (b + 1) * VEC)
            kept_ref[blocks - 1 - b, c * VEC : (c + 1) * VEC, :] = kept[rows]
            sent_ref[blocks - 1 - b, c * VEC : (c + 1) * VEC, :] = sent[rows]
    for b in range(blocks):
        rows = slice(b * VEC, (b + 1) * VEC)
        for ref in (kept_ref, sent_ref):
            ref[blocks - 1 - b, 2 * VEC :, :] = jnp.zeros((VEC, size), jnp.float32)
            ref[blocks - 1 - b, 2 * VEC :, 0:VEC] = gram[rows, rows]


def step(kind, u, name, h_ready, own, rim, *others):
    rows_in, states, size = rim.shape
    rows_out = sum(h.shape[0] for h in h_ready)
    shapes = [(rows_out, states, size)]
    if kind == "other":
        shapes.append((states, pl.cdiv(states, size) * size))
    elif kind == "last":
        blocks = states // VEC
        shapes = [(blocks, 3 * VEC, size)] * 2
    operands = [*h_ready, *own, rim, *others]
    cost = pl.CostEstimate(
        flops=8 * BLOCKS * rows_out * states * size * size,
        bytes_accessed=4 * BLOCKS * rows_out * size * size,
        transcendentals=0,
    )
    outs = pl.pallas_call(
        functools.partial(step_kernel, kind, u, len(h_ready)),
        in_specs=[VMEM] * len(operands),
        out_specs=[VMEM] * len(shapes),
        out_shape=[jax.ShapeDtypeStruct(shape, jnp.float32) for shape in shapes],
        scratch_shapes=[
            pltpu.VMEM((2 * states, rows_in * width * size), jnp.bfloat16) for width in (2, 1)
        ],
        compiler_params=pltpu.CompilerParams(vmem_limit_bytes=LIMIT),
        cost_estimate=cost,
        name=name,
    )(*operands)
    return outs[0] if len(outs) == 1 else outs


def finish_kernel(cols, node_count, flags_ref, parts_ref, rot_ref, out_ref):
    wide = parts_ref.shape[0]
    gram = parts_ref[0, cols * VEC : (cols + 1) * VEC, 0:VEC]
    for w in range(1, wide):
        gram = gram + parts_ref[w, cols * VEC : (cols + 1) * VEC, 0:VEC]
    gram = gram / node_count
    row = lax.broadcasted_iota(jnp.int32, (VEC, VEC), 0)
    col = lax.broadcasted_iota(jnp.int32, (VEC, VEC), 1)
    inverse = jnp.where(row == col, 1.0, 0.0).astype(jnp.float32)
    for k in range(VEC):
        scale = 1.0 / jnp.sqrt(gram[k : k + 1, k : k + 1])
        top = gram[k : k + 1, :] * scale
        top_inverse = inverse[k : k + 1, :] * scale
        factor = gram[:, k : k + 1] * scale
        gram = gram - factor * top
        inverse = jnp.where(row == k, top_inverse, jnp.where(row > k, inverse - factor * top_inverse, inverse))
    number = jnp.broadcast_to(flags_ref[3 * VEC : 3 * VEC + 1, 0:VEC], (VEC, VEC))
    turn = rot_ref[0]
    for w in range(1, wide):
        turn = jnp.where(number == w, rot_ref[w], turn)
    turn = turn.T
    mixer = turn[:, 0:1] * inverse[0:1, :]
    for k in range(1, VEC):
        mixer = mixer + turn[:, k : k + 1] * inverse[k : k + 1, :]
    columns = [mixer[:, d : d + 1] for d in range(VEC)]
    mixed = []
    for w in range(wide):
        for c in range(cols):
            block = parts_ref[w, c * VEC : (c + 1) * VEC, :]
            total = columns[0] * block[0:1, :]
            for d in range(1, VEC):
                total = total + columns[d] * block[d : d + 1, :]
            mixed.append(total)
    half = flag(flags_ref, 2, mixed[0].shape)
    for w in range(wide):
        for c in range(cols):
            first = mixed[(wide - 1 - w) * cols + c]
            second = mixed[(wide - 1 - w + wide // 2) % wide * cols + c]
            out_ref[:, 0, w * cols + c, :] = jnp.where(half, second, first)


def finish(flags, cols, node_count, parts, rotation):
    wide, _, size = parts.shape
    return pl.pallas_call(
        functools.partial(finish_kernel, cols, node_count),
        in_specs=[VMEM] * 3,
        out_specs=VMEM,
        out_shape=jax.ShapeDtypeStruct((VEC, 1, wide * cols, size), jnp.float32),
        compiler_params=pltpu.CompilerParams(vmem_limit_bytes=LIMIT),
        name="finish",
    )(flags, parts, rotation)


def after(x, token):
    return lax.optimization_barrier((x, token))[0]


def body(slab, hblocks, blist, rotation):
    wide, grp = lax.axis_size("wide"), lax.axis_size("grp")
    _, _, cols, size = slab.shape
    slots = hblocks.shape[2]
    near = [(i, i ^ 1) for i in range(wide)]
    far = [(i, ((i + 1) ^ 1) - 1) for i in range(1, wide - 1)]
    mine, odd = lax.axis_index("grp"), lax.axis_index("wide") % 2
    x = mine // 2
    edge = half = x ^ (mine % 2)
    place = jnp.stack([odd, edge, half, x]).astype(jnp.int32)
    flags = jnp.stack([odd, edge, half, lax.axis_index("wide")]).astype(jnp.int32)
    flags = jnp.broadcast_to(jnp.repeat(flags, VEC)[:, None], (4 * VEC, size))

    def across(value):
        return lax.ppermute(value, "grp", [(i, i ^ 3) for i in range(grp)])

    def core(value):
        return lax.ppermute(value, "grp", [(i, i ^ 1) for i in range(grp)])

    def over_far(value):
        return lax.ppermute(value, "wide", far)

    def over_near(value):
        return lax.ppermute(value, "wide", near)

    own = arrange(flags, blist, slab)
    own_core = core(own[1])
    h_core = core(hblocks)
    border, inside = pick(flags, hblocks, h_core)
    own_across = across(after(jnp.stack([own[0], own_core]), border))
    rows = [own[0], own_core, own_across[0], own_across[1]]
    codes = jnp.stack([row[-VEC : cols - VEC, :slots] for row in rows]).astype(jnp.int32).reshape(-1)
    codes = jnp.concatenate([place, codes])
    states = (own.shape[1] - VEC) // cols
    zero = []
    for u in range(cols):
        parts = [row[u * states : (u + 1) * states] for row in rows]
        border_mine = jnp.stack([parts[m] for m in (1, 0, 2, 3)])
        border_core = jnp.stack([parts[m] for m in (0, 1, 3, 2)])
        zero.append(jnp.where(edge == 1, border_mine, border_core))

    zero[1] = after(zero[1], zero[0])
    far_rim, near_rim = over_far(zero[0]), over_near(zero[1])
    border = across(after(border, own_core))
    inside = across(after(inside, near_rim))
    h_two = [prepare("chip", codes, hblocks, h_core)]
    border_core = core(after(border, (far_rim, h_two)))
    h_three = h_two + [prepare("border", codes, border, border_core)]

    one = [step("first", 0, "one_0", h_three, zero, far_rim)]
    rim = after(near_rim, one[0])
    one.append(step("first", 1, "one_1", h_three, zero, rim))
    rims = over_far(one[0]), over_near(one[1])
    two, sent, before = [], (), []
    for u in range(cols):
        rim = after(rims[u], (sent, inside))
        two.append(step("next", u, f"two_{u}", h_two, one, rim, zero[u]))
        sent = jnp.concatenate([two[u], one[u][:1]])
        other = across(sent)
        two[u] = jnp.concatenate([two[u], other[1:2], other[0:1]])
        before.append(jnp.concatenate([one[u], other[2:]]))
    inside_core = core(after(inside, two[0]))
    h_four = h_three + [prepare("inner", codes, inside, inside_core)]
    rims = over_far(two[0]), over_near(two[1])
    three = [step("next", 0, "three_0", h_four, two, rims[0], before[0])]
    rim = after(rims[1], three[0])
    three.append(step("next", 1, "three_1", h_four, two, rim, before[1]))
    rims = over_far(three[0]), over_near(three[1])
    four = step("other", 0, "four_0", h_four, three, rims[0], two[0])
    kept, sent = step("last", 1, "four_1", h_four, three, rims[1], two[1], *four, flags)

    packed = jnp.concatenate([core(sent), kept])
    owners = wide // 2
    groups = [
        [((wide - 1 - i + owners * (g // 2 ^ g % 2)) % wide) * grp + g for i in range(wide)]
        for g in range(grp)
    ]
    packed = lax.all_to_all(
        packed,
        ("wide", "grp"),
        split_axis=0,
        concat_axis=0,
        tiled=True,
        axis_index_groups=groups,
    )
    node_count = grp * wide * cols * size
    return finish(flags, cols, node_count, packed, rotation)


def solution(mesh):
    in_specs = (
        P(None, "grp", "wide", None),
        P("grp", "wide", None, None, None),
        P("grp", "wide", None),
        P(),
    )
    out_specs = P("wide", "grp", None, None)
    return jax.shard_map(body, mesh=mesh, in_specs=in_specs, out_specs=out_specs, check_vma=False)
```

```python
import functools

import jax
import jax.numpy as jnp
from jax import lax
from jax.experimental import pallas as pl
from jax.experimental.pallas import tpu as pltpu
from jax.sharding import PartitionSpec as P

VEC = 8
DEG = 4
LIMIT = 16 * 2**20
BLOCKS = 9
VMEM = pl.BlockSpec(memory_space=pltpu.VMEM)
SMEM = pl.BlockSpec(memory_space=pltpu.SMEM)
NT = (((1,), (1,)), ((), ()))


def split(x):
    high = x.astype(jnp.bfloat16)
    low = (x - high.astype(jnp.float32)).astype(jnp.bfloat16)
    return high, low


def flag(flags_ref, n, shape):
    return jnp.broadcast_to(flags_ref[n * VEC : n * VEC + 1, :], shape) == 1


def arrange_kernel(flags_ref, codes_ref, slab_ref, out_ref):
    all_states, _, cols, size = slab_ref.shape
    slots, states = codes_ref.shape[2], all_states // 2
    odd = flag(flags_ref, 0, (all_states, size))
    second = flag(flags_ref, 2, (states, size))
    both = [slab_ref[:, 0, c, :] for c in range(cols)]
    for u in range(cols):
        value = jnp.where(odd, both[cols - 1 - u], both[u])
        low, high = value[:states], value[states:]
        rows = slice(u * states, (u + 1) * states)
        out_ref[0, rows, :] = jnp.where(second, high, low)
        out_ref[1, rows, :] = jnp.where(second, low, high)
    codes = codes_ref[0].astype(jnp.float32)
    for h in range(2):
        out_ref[h, cols * states :, :] = jnp.zeros((VEC, size), jnp.float32)
        out_ref[h, cols * states : cols * states + cols, 0:slots] = codes


def arrange(flags, blist, slab):
    all_states, _, cols, size = slab.shape
    return pl.pallas_call(
        arrange_kernel,
        in_specs=[VMEM] * 3,
        out_specs=VMEM,
        out_shape=jax.ShapeDtypeStruct((2, cols * all_states // 2 + VEC, size), jnp.float32),
        compiler_params=pltpu.CompilerParams(vmem_limit_bytes=LIMIT),
        name="arrange",
    )(flags, blist, slab)


def pick_kernel(flags_ref, own_ref, core_ref, border_ref, inner_ref):
    shape = own_ref.shape[3:]
    edge, half = flag(flags_ref, 1, shape), flag(flags_ref, 2, shape)
    for k in range(own_ref.shape[2]):
        own = jnp.where(half, own_ref[0, 1, k], own_ref[0, 0, k])
        core = jnp.where(half, core_ref[0, 1, k], core_ref[0, 0, k])
        border_ref[0, 0, k] = jnp.where(edge, own, core)
        inner_ref[0, 0, k] = jnp.where(edge, core, own)


def pick(flags, own, core):
    rows, cols, *block = own.shape
    return pl.pallas_call(
        pick_kernel,
        in_specs=[VMEM] * 3,
        out_specs=[VMEM] * 2,
        out_shape=[jax.ShapeDtypeStruct((rows, 1, *block), own.dtype)] * 2,
        compiler_params=pltpu.CompilerParams(vmem_limit_bytes=LIMIT),
        name="pick",
    )(flags, own, core)


def prepare_kernel(mode, codes_ref, *refs):
    *h_refs, out_ref = refs
    _, cols, slots, size, _ = h_refs[0].shape
    odd, edge, half, x = (codes_ref[n] for n in range(4))
    out_ref[...] = jnp.zeros_like(out_ref)

    def convert(h_ref, h_col, c, q, row):
        u = jnp.bitwise_xor(c, odd)
        for k in range(slots):
            code = codes_ref[4 + (row * 2 + c) * slots + k]
            down = (code >= 3).astype(jnp.int32) + (code >= 6).astype(jnp.int32)
            along = code - 3 * down
            down = jnp.where(x == 1, 2 - down, down)
            along = u + jnp.where(odd == 1, 2 - along, along)
            rim = (along == 0) | (along == 3)
            block = jnp.where(rim, 6 + down, 2 * down + along - 1)
            lanes = pl.ds(pl.multiple_of(block * size, size), size)
            high, low = split(h_ref[0, h_col, k])
            out_ref[q, u, 0:size, lanes] = high
            out_ref[q, u, size : 2 * size, lanes] = low

    for h, h_ref in enumerate(h_refs):
        if mode == "chip":
            for c in range(cols):
                convert(h_ref, c, c, jnp.bitwise_xor(edge, h), h)
        else:
            row = 3 - edge if mode == "border" else 2 + edge
            convert(h_ref, 0, jnp.bitwise_xor(half, h), 0, row)


def prepare(mode, codes, *h_rows):
    _, _, slots, size, _ = h_rows[0].shape
    rows = 2 if mode == "chip" else 1
    return pl.pallas_call(
        functools.partial(prepare_kernel, mode),
        in_specs=[SMEM] + [VMEM] * len(h_rows),
        out_specs=VMEM,
        out_shape=jax.ShapeDtypeStruct((rows, 2, 2 * size, BLOCKS * size), jnp.bfloat16),
        compiler_params=pltpu.CompilerParams(vmem_limit_bytes=LIMIT),
        name="prepare_" + mode,
    )(codes, *h_rows)


def fill(x_ref, fields):
    rows, states, size = fields[0].shape
    for q in range(rows):
        for n, field in enumerate(fields):
            at = (q * len(fields) + n) * size
            high, low = split(field[q])
            x_ref[0:states, at : at + size] = high
            x_ref[states : 2 * states, at : at + size] = low


def step_kernel(kind, u, count, *refs):
    h_refs, (own_0, own_1, rim_ref, *refs) = refs[:count], refs[count:]
    *refs, own_x, rim_x = refs
    before, refs = (None, refs) if kind == "first" else (refs[0], refs[1:])
    rows_in, states, size = rim_ref.shape
    h_rows = [h_ref.at[q] for h_ref in h_refs for q in range(h_ref.shape[0])]
    fill(own_x, [own_0, own_1])
    fill(rim_x, [rim_ref])
    values = []
    for q, h_row in enumerate(h_rows):
        low, high = max(q - 1, 0), min(q + 2, rows_in)
        acc = 0.0
        for x_ref, width, first in ((own_x, 2 * size, 0), (rim_x, size, 6 * size)):
            at = first + (low - q + 1) * width
            acc = acc + lax.dot_general(
                x_ref[:, low * width : high * width],
                h_row[u, :, at : at + (high - low) * width],
                NT,
                preferred_element_type=jnp.float32,
            )
        small = acc[states:, size:] + (acc[states:, :size] + acc[:states, size:])
        value = acc[:states, :size] + small
        values.append(value if kind == "first" else 2.0 * value - before[q])
    if kind in ("other", "last"):
        flat = [jnp.concatenate(part, axis=1) for part in zip(*map(split, values))]
        flat = jnp.concatenate(flat)
        gram = lax.dot_general(flat, flat, NT, preferred_element_type=jnp.float32)
        gram = gram[:states] + gram[states:]
        gram = gram[:, :states] + gram[:, states:]
    if kind != "last":
        for q, value in enumerate(values):
            refs[0][q] = value
        if kind == "other":
            refs[1][:, 0:states] = gram
        return
    other_ref, other_gram_ref, flags_ref, kept_ref, sent_ref = refs
    odd, edge = flag(flags_ref, 0, (states, size)), flag(flags_ref, 1, (states, size))
    nodes = [[other_ref[q] for q in range(len(values))], values]
    gram = gram + other_gram_ref[:, 0:states]
    blocks = states // VEC
    for c in range(2):
        inner = jnp.where(odd, nodes[1 - c][0], nodes[c][0])
        border = jnp.where(odd, nodes[1 - c][1], nodes[c][1])
        kept, sent = jnp.where(edge, border, inner), jnp.where(edge, inner, border)
        for b in range(blocks):
            rows = slice(b * VEC, (b + 1) * VEC)
            kept_ref[blocks - 1 - b, c * VEC : (c + 1) * VEC, :] = kept[rows]
            sent_ref[blocks - 1 - b, c * VEC : (c + 1) * VEC, :] = sent[rows]
    for b in range(blocks):
        rows = slice(b * VEC, (b + 1) * VEC)
        for ref in (kept_ref, sent_ref):
            ref[blocks - 1 - b, 2 * VEC :, :] = jnp.zeros((VEC, size), jnp.float32)
            ref[blocks - 1 - b, 2 * VEC :, 0:VEC] = gram[rows, rows]


def step(kind, u, name, h_ready, own, rim, *others):
    rows_in, states, size = rim.shape
    rows_out = sum(h.shape[0] for h in h_ready)
    shapes = [(rows_out, states, size)]
    if kind == "other":
        shapes.append((states, pl.cdiv(states, size) * size))
    elif kind == "last":
        blocks = states // VEC
        shapes = [(blocks, 3 * VEC, size)] * 2
    operands = [*h_ready, *own, rim, *others]
    cost = pl.CostEstimate(
        flops=8 * BLOCKS * rows_out * states * size * size,
        bytes_accessed=4 * BLOCKS * rows_out * size * size,
        transcendentals=0,
    )
    outs = pl.pallas_call(
        functools.partial(step_kernel, kind, u, len(h_ready)),
        in_specs=[VMEM] * len(operands),
        out_specs=[VMEM] * len(shapes),
        out_shape=[jax.ShapeDtypeStruct(shape, jnp.float32) for shape in shapes],
        scratch_shapes=[
            pltpu.VMEM((2 * states, rows_in * width * size), jnp.bfloat16) for width in (2, 1)
        ],
        compiler_params=pltpu.CompilerParams(vmem_limit_bytes=LIMIT),
        cost_estimate=cost,
        name=name,
    )(*operands)
    return outs[0] if len(outs) == 1 else outs


def finish_kernel(cols, node_count, flags_ref, parts_ref, rot_ref, out_ref):
    wide = parts_ref.shape[0]
    gram = parts_ref[0, cols * VEC : (cols + 1) * VEC, 0:VEC]
    for w in range(1, wide):
        gram = gram + parts_ref[w, cols * VEC : (cols + 1) * VEC, 0:VEC]
    gram = gram / node_count
    row = lax.broadcasted_iota(jnp.int32, (VEC, VEC), 0)
    col = lax.broadcasted_iota(jnp.int32, (VEC, VEC), 1)
    inverse = jnp.where(row == col, 1.0, 0.0).astype(jnp.float32)
    for k in range(VEC):
        scale = 1.0 / jnp.sqrt(gram[k : k + 1, k : k + 1])
        top = gram[k : k + 1, :] * scale
        top_inverse = inverse[k : k + 1, :] * scale
        factor = gram[:, k : k + 1] * scale
        gram = gram - factor * top
        inverse = jnp.where(row == k, top_inverse, jnp.where(row > k, inverse - factor * top_inverse, inverse))
    number = jnp.broadcast_to(flags_ref[3 * VEC : 3 * VEC + 1, 0:VEC], (VEC, VEC))
    turn = rot_ref[0]
    for w in range(1, wide):
        turn = jnp.where(number == w, rot_ref[w], turn)
    turn = turn.T
    mixer = turn[:, 0:1] * inverse[0:1, :]
    for k in range(1, VEC):
        mixer = mixer + turn[:, k : k + 1] * inverse[k : k + 1, :]
    columns = [mixer[:, d : d + 1] for d in range(VEC)]
    mixed = []
    for w in range(wide):
        for c in range(cols):
            block = parts_ref[w, c * VEC : (c + 1) * VEC, :]
            total = columns[0] * block[0:1, :]
            for d in range(1, VEC):
                total = total + columns[d] * block[d : d + 1, :]
            mixed.append(total)
    for w in range(wide):
        for c in range(cols):
            out_ref[:, 0, w * cols + c, :] = mixed[(wide - 1 - w) * cols + c]


def finish(flags, cols, node_count, parts, rotation):
    wide, _, size = parts.shape
    return pl.pallas_call(
        functools.partial(finish_kernel, cols, node_count),
        in_specs=[VMEM] * 3,
        out_specs=VMEM,
        out_shape=jax.ShapeDtypeStruct((VEC, 1, wide * cols, size), jnp.float32),
        compiler_params=pltpu.CompilerParams(vmem_limit_bytes=LIMIT),
        name="finish",
    )(flags, parts, rotation)


def after(x, token):
    return lax.optimization_barrier((x, token))[0]


def body(slab, hblocks, blist, rotation):
    wide, grp = lax.axis_size("wide"), lax.axis_size("grp")
    _, _, cols, size = slab.shape
    slots = hblocks.shape[2]
    near = [(i, i ^ 1) for i in range(wide)]
    far = [(i, ((i + 1) ^ 1) - 1) for i in range(1, wide - 1)]
    mine, odd = lax.axis_index("grp"), lax.axis_index("wide") % 2
    x = mine // 2
    edge = half = x ^ (mine % 2)
    place = jnp.stack([odd, edge, half, x]).astype(jnp.int32)
    flags = jnp.stack([odd, edge, half, lax.axis_index("wide")]).astype(jnp.int32)
    flags = jnp.broadcast_to(jnp.repeat(flags, VEC)[:, None], (4 * VEC, size))

    def across(value):
        return lax.ppermute(value, "grp", [(i, i ^ 3) for i in range(grp)])

    def core(value):
        return lax.ppermute(value, "grp", [(i, i ^ 1) for i in range(grp)])

    def over_far(value):
        return lax.ppermute(value, "wide", far)

    def over_near(value):
        return lax.ppermute(value, "wide", near)

    own = arrange(flags, blist, slab)
    own_core = core(own[1])
    h_core = core(hblocks)
    border, inside = pick(flags, hblocks, h_core)
    own_across = across(after(jnp.stack([own[0], own_core]), border))
    rows = [own[0], own_core, own_across[0], own_across[1]]
    codes = jnp.stack([row[-VEC : cols - VEC, :slots] for row in rows]).astype(jnp.int32).reshape(-1)
    codes = jnp.concatenate([place, codes])
    states = (own.shape[1] - VEC) // cols
    zero = []
    for u in range(cols):
        parts = [row[u * states : (u + 1) * states] for row in rows]
        border_mine = jnp.stack([parts[m] for m in (1, 0, 2, 3)])
        border_core = jnp.stack([parts[m] for m in (0, 1, 3, 2)])
        zero.append(jnp.where(edge == 1, border_mine, border_core))

    zero[1] = after(zero[1], zero[0])
    far_rim, near_rim = over_far(zero[0]), over_near(zero[1])
    border = across(after(border, own_core))
    inside = across(after(inside, near_rim))
    h_two = [prepare("chip", codes, hblocks, h_core)]
    border_core = core(after(border, (far_rim, h_two)))
    h_three = h_two + [prepare("border", codes, border, border_core)]

    one = [step("first", 0, "one_0", h_three, zero, far_rim)]
    rim = after(near_rim, one[0])
    one.append(step("first", 1, "one_1", h_three, zero, rim))
    rims = over_far(one[0]), over_near(one[1])
    two, sent, before = [], (), []
    for u in range(cols):
        rim = after(rims[u], (sent, inside))
        two.append(step("next", u, f"two_{u}", h_two, one, rim, zero[u]))
        sent = jnp.concatenate([two[u], one[u][:1]])
        other = across(sent)
        two[u] = jnp.concatenate([two[u], other[1:2], other[0:1]])
        before.append(jnp.concatenate([one[u], other[2:]]))
    inside_core = core(after(inside, two[0]))
    h_four = h_three + [prepare("inner", codes, inside, inside_core)]
    rims = over_far(two[0]), over_near(two[1])
    three = [step("next", 0, "three_0", h_four, two, rims[0], before[0])]
    rim = after(rims[1], three[0])
    three.append(step("next", 1, "three_1", h_four, two, rim, before[1]))
    rims = over_far(three[0]), over_near(three[1])
    four = step("other", 0, "four_0", h_four, three, rims[0], two[0])
    kept, sent = step("last", 1, "four_1", h_four, three, rims[1], two[1], *four, flags)

    sent = core(sent)
    packed = jnp.where(half == 1, jnp.concatenate([kept, sent]), jnp.concatenate([sent, kept]))
    groups = [[(wide - 1 - i) * grp + g for i in range(wide)] for g in range(grp)]
    packed = lax.all_to_all(
        packed,
        ("wide", "grp"),
        split_axis=0,
        concat_axis=0,
        tiled=True,
        axis_index_groups=groups,
    )
    node_count = grp * wide * cols * size
    return finish(flags, cols, node_count, packed, rotation)


def solution(mesh):
    in_specs = (
        P(None, "grp", "wide", None),
        P("grp", "wide", None, None, None),
        P("grp", "wide", None),
        P(),
    )
    out_specs = P("wide", "grp", None, None)
    return jax.shard_map(body, mesh=mesh, in_specs=in_specs, out_specs=out_specs, check_vma=False)
```

```python
import functools

import jax
import jax.numpy as jnp
from jax import lax
from jax.experimental import pallas as pl
from jax.experimental.pallas import tpu as pltpu
from jax.sharding import PartitionSpec as P

VEC = 8
DEG = 4
LIMIT = 16 * 2**20
BLOCKS = 9
VMEM = pl.BlockSpec(memory_space=pltpu.VMEM)
SMEM = pl.BlockSpec(memory_space=pltpu.SMEM)
NT = (((1,), (1,)), ((), ()))


def split(x):
    high = x.astype(jnp.bfloat16)
    low = (x - high.astype(jnp.float32)).astype(jnp.bfloat16)
    return high, low


def flag(flags_ref, n, shape):
    return jnp.broadcast_to(flags_ref[n * VEC : n * VEC + 1, :], shape) == 1


def arrange_kernel(flags_ref, codes_ref, slab_ref, out_ref):
    all_states, _, cols, size = slab_ref.shape
    slots, states = codes_ref.shape[2], all_states // 2
    odd = flag(flags_ref, 0, (all_states, size))
    second = flag(flags_ref, 2, (states, size))
    both = [slab_ref[:, 0, c, :] for c in range(cols)]
    for u in range(cols):
        value = jnp.where(odd, both[cols - 1 - u], both[u])
        low, high = value[:states], value[states:]
        rows = slice(u * states, (u + 1) * states)
        out_ref[0, rows, :] = jnp.where(second, high, low)
        out_ref[1, rows, :] = jnp.where(second, low, high)
    codes = codes_ref[0].astype(jnp.float32)
    for h in range(2):
        out_ref[h, cols * states :, :] = jnp.zeros((VEC, size), jnp.float32)
        out_ref[h, cols * states : cols * states + cols, 0:slots] = codes


def arrange(flags, blist, slab):
    all_states, _, cols, size = slab.shape
    return pl.pallas_call(
        arrange_kernel,
        in_specs=[VMEM] * 3,
        out_specs=VMEM,
        out_shape=jax.ShapeDtypeStruct((2, cols * all_states // 2 + VEC, size), jnp.float32),
        compiler_params=pltpu.CompilerParams(vmem_limit_bytes=LIMIT),
        name="arrange",
    )(flags, blist, slab)


def pick_kernel(flags_ref, own_ref, core_ref, border_ref, inner_ref):
    shape = own_ref.shape[3:]
    edge, half = flag(flags_ref, 1, shape), flag(flags_ref, 2, shape)
    for k in range(own_ref.shape[2]):
        own = jnp.where(half, own_ref[0, 1, k], own_ref[0, 0, k])
        core = jnp.where(half, core_ref[0, 1, k], core_ref[0, 0, k])
        border_ref[0, 0, k] = jnp.where(edge, own, core)
        inner_ref[0, 0, k] = jnp.where(edge, core, own)


def pick(flags, own, core):
    rows, cols, *block = own.shape
    return pl.pallas_call(
        pick_kernel,
        in_specs=[VMEM] * 3,
        out_specs=[VMEM] * 2,
        out_shape=[jax.ShapeDtypeStruct((rows, 1, *block), own.dtype)] * 2,
        compiler_params=pltpu.CompilerParams(vmem_limit_bytes=LIMIT),
        name="pick",
    )(flags, own, core)


def prepare_kernel(mode, codes_ref, *refs):
    *h_refs, out_ref = refs
    _, cols, slots, size, _ = h_refs[0].shape
    odd, edge, half, x = (codes_ref[n] for n in range(4))
    out_ref[...] = jnp.zeros_like(out_ref)

    def convert(h_ref, h_col, c, q, row):
        u = jnp.bitwise_xor(c, odd)
        for k in range(slots):
            code = codes_ref[4 + (row * 2 + c) * slots + k]
            down = (code >= 3).astype(jnp.int32) + (code >= 6).astype(jnp.int32)
            along = code - 3 * down
            down = jnp.where(x == 1, 2 - down, down)
            along = u + jnp.where(odd == 1, 2 - along, along)
            rim = (along == 0) | (along == 3)
            block = jnp.where(rim, 6 + down, 2 * down + along - 1)
            lanes = pl.ds(pl.multiple_of(block * size, size), size)
            high, low = split(h_ref[0, h_col, k])
            out_ref[q, u, 0:size, lanes] = high
            out_ref[q, u, size : 2 * size, lanes] = low

    for h, h_ref in enumerate(h_refs):
        if mode == "chip":
            for c in range(cols):
                convert(h_ref, c, c, jnp.bitwise_xor(edge, h), h)
        else:
            row = 3 - edge if mode == "border" else 2 + edge
            convert(h_ref, 0, jnp.bitwise_xor(half, h), 0, row)


def prepare(mode, codes, *h_rows):
    _, _, slots, size, _ = h_rows[0].shape
    rows = 2 if mode == "chip" else 1
    return pl.pallas_call(
        functools.partial(prepare_kernel, mode),
        in_specs=[SMEM] + [VMEM] * len(h_rows),
        out_specs=VMEM,
        out_shape=jax.ShapeDtypeStruct((rows, 2, 2 * size, BLOCKS * size), jnp.bfloat16),
        compiler_params=pltpu.CompilerParams(vmem_limit_bytes=LIMIT),
        name="prepare_" + mode,
    )(codes, *h_rows)


def fill(x_ref, fields):
    rows, states, size = fields[0].shape
    for q in range(rows):
        for n, field in enumerate(fields):
            at = (q * len(fields) + n) * size
            high, low = split(field[q])
            x_ref[0:states, at : at + size] = high
            x_ref[states : 2 * states, at : at + size] = low


def products(h_refs, u, x_ref, width, first, rows_in):
    states, size = x_ref.shape[0] // 2, h_refs[0].shape[2] // 2
    width, first = width * size, first * size
    h_rows = [h_ref.at[q] for h_ref in h_refs for q in range(h_ref.shape[0])]
    sums = []
    for q, h_row in enumerate(h_rows):
        low, high = max(q - 1, 0), min(q + 2, rows_in)
        at = first + (low - q + 1) * width
        acc = lax.dot_general(
            x_ref[:, low * width : high * width],
            h_row[u, :, at : at + (high - low) * width],
            NT,
            preferred_element_type=jnp.float32,
        )
        small = acc[states:, size:] + (acc[states:, :size] + acc[:states, size:])
        sums.append(acc[:states, :size] + small)
    return sums


def inner_kernel(u, count, *refs):
    h_refs, (own_0, own_1, before, out_ref, x_ref) = refs[:count], refs[count:]
    fill(x_ref, [own_0, own_1])
    for q, value in enumerate(products(h_refs, u, x_ref, 2, 0, own_0.shape[0])):
        out_ref[q] = 2.0 * value - before[q]


def inner(u, name, h_ready, own, before):
    rows_in, states, size = own[0].shape
    rows_out = sum(h.shape[0] for h in h_ready)
    operands = [*h_ready, *own, before]
    return pl.pallas_call(
        functools.partial(inner_kernel, u, len(h_ready)),
        in_specs=[VMEM] * len(operands),
        out_specs=VMEM,
        out_shape=jax.ShapeDtypeStruct((rows_out, states, size), jnp.float32),
        scratch_shapes=[pltpu.VMEM((2 * states, rows_in * 2 * size), jnp.bfloat16)],
        compiler_params=pltpu.CompilerParams(vmem_limit_bytes=LIMIT),
        cost_estimate=cost_of(rows_out, 6, states, size),
        name=name,
    )(*operands)


def cost_of(rows, blocks, states, size):
    return pl.CostEstimate(
        flops=8 * blocks * rows * states * size * size,
        bytes_accessed=4 * blocks * rows * size * size,
        transcendentals=0,
    )


def step_kernel(kind, u, count, *refs):
    h_refs, refs = refs[:count], refs[count:]
    if kind in ("first", "whole"):
        own_0, own_1, rim_ref, *refs, own_x, rim_x = refs
    else:
        rim_ref, acc_ref, *refs, rim_x = refs
    rows_in, states, size = rim_ref.shape
    fill(rim_x, [rim_ref])
    values = products(h_refs, u, rim_x, 1, 6, rows_in)
    if kind in ("first", "whole"):
        fill(own_x, [own_0, own_1])
        own = products(h_refs, u, own_x, 2, 0, rows_in)
        values = [value + own[q] for q, value in enumerate(values)]
        if kind == "whole":
            before, *refs = refs
            values = [2.0 * value - before[q] for q, value in enumerate(values)]
    else:
        values = [acc_ref[q] + 2.0 * value for q, value in enumerate(values)]
    if kind in ("other", "last"):
        flat = [jnp.concatenate(part, axis=1) for part in zip(*map(split, values))]
        flat = jnp.concatenate(flat)
        gram = lax.dot_general(flat, flat, NT, preferred_element_type=jnp.float32)
        gram = gram[:states] + gram[states:]
        gram = gram[:, :states] + gram[:, states:]
    if kind != "last":
        for q, value in enumerate(values):
            refs[0][q] = value
        if kind == "other":
            refs[1][:, 0:states] = gram
        return
    other_ref, other_gram_ref, flags_ref, kept_ref, sent_ref = refs
    odd, edge = flag(flags_ref, 0, (states, size)), flag(flags_ref, 1, (states, size))
    nodes = [[other_ref[q] for q in range(len(values))], values]
    gram = gram + other_gram_ref[:, 0:states]
    blocks = states // VEC
    for c in range(2):
        inner = jnp.where(odd, nodes[1 - c][0], nodes[c][0])
        border = jnp.where(odd, nodes[1 - c][1], nodes[c][1])
        kept, sent = jnp.where(edge, border, inner), jnp.where(edge, inner, border)
        for b in range(blocks):
            rows = slice(b * VEC, (b + 1) * VEC)
            kept_ref[blocks - 1 - b, c * VEC : (c + 1) * VEC, :] = kept[rows]
            sent_ref[blocks - 1 - b, c * VEC : (c + 1) * VEC, :] = sent[rows]
    for b in range(blocks):
        rows = slice(b * VEC, (b + 1) * VEC)
        for ref in (kept_ref, sent_ref):
            ref[blocks - 1 - b, 2 * VEC :, :] = jnp.zeros((VEC, size), jnp.float32)
            ref[blocks - 1 - b, 2 * VEC :, 0:VEC] = gram[rows, rows]


def step(kind, u, name, h_ready, *operands):
    merged = kind in ("first", "whole")
    rows_in, states, size = operands[0].shape
    rows_out = sum(h.shape[0] for h in h_ready)
    shapes = [(rows_out, states, size)]
    if kind == "other":
        shapes.append((states, pl.cdiv(states, size) * size))
    elif kind == "last":
        shapes = [(states // VEC, 3 * VEC, size)] * 2
    operands = [*h_ready, *operands]
    outs = pl.pallas_call(
        functools.partial(step_kernel, kind, u, len(h_ready)),
        in_specs=[VMEM] * len(operands),
        out_specs=[VMEM] * len(shapes),
        out_shape=[jax.ShapeDtypeStruct(shape, jnp.float32) for shape in shapes],
        scratch_shapes=[
            pltpu.VMEM((2 * states, rows_in * width * size), jnp.bfloat16)
            for width in ((2, 1) if merged else (1,))
        ],
        compiler_params=pltpu.CompilerParams(vmem_limit_bytes=LIMIT),
        cost_estimate=cost_of(rows_out, BLOCKS if merged else 3, states, size),
        name=name,
    )(*operands)
    return outs[0] if len(outs) == 1 else outs


def finish_kernel(cols, node_count, flags_ref, parts_ref, rot_ref, out_ref):
    wide = parts_ref.shape[0]
    gram = parts_ref[0, cols * VEC : (cols + 1) * VEC, 0:VEC]
    for w in range(1, wide):
        gram = gram + parts_ref[w, cols * VEC : (cols + 1) * VEC, 0:VEC]
    gram = gram / node_count
    row = lax.broadcasted_iota(jnp.int32, (VEC, VEC), 0)
    col = lax.broadcasted_iota(jnp.int32, (VEC, VEC), 1)
    inverse = jnp.where(row == col, 1.0, 0.0).astype(jnp.float32)
    for k in range(VEC):
        scale = 1.0 / jnp.sqrt(gram[k : k + 1, k : k + 1])
        top = gram[k : k + 1, :] * scale
        top_inverse = inverse[k : k + 1, :] * scale
        factor = gram[:, k : k + 1] * scale
        gram = gram - factor * top
        inverse = jnp.where(row == k, top_inverse, jnp.where(row > k, inverse - factor * top_inverse, inverse))
    number = jnp.broadcast_to(flags_ref[3 * VEC : 3 * VEC + 1, 0:VEC], (VEC, VEC))
    turn = rot_ref[0]
    for w in range(1, wide):
        turn = jnp.where(number == w, rot_ref[w], turn)
    turn = turn.T
    mixer = turn[:, 0:1] * inverse[0:1, :]
    for k in range(1, VEC):
        mixer = mixer + turn[:, k : k + 1] * inverse[k : k + 1, :]
    columns = [mixer[:, d : d + 1] for d in range(VEC)]
    mixed = []
    for w in range(wide):
        for c in range(cols):
            block = parts_ref[w, c * VEC : (c + 1) * VEC, :]
            total = columns[0] * block[0:1, :]
            for d in range(1, VEC):
                total = total + columns[d] * block[d : d + 1, :]
            mixed.append(total)
    for w in range(wide):
        for c in range(cols):
            out_ref[:, 0, w * cols + c, :] = mixed[(wide - 1 - w) * cols + c]


def finish(flags, cols, node_count, parts, rotation):
    wide, _, size = parts.shape
    return pl.pallas_call(
        functools.partial(finish_kernel, cols, node_count),
        in_specs=[VMEM] * 3,
        out_specs=VMEM,
        out_shape=jax.ShapeDtypeStruct((VEC, 1, wide * cols, size), jnp.float32),
        compiler_params=pltpu.CompilerParams(vmem_limit_bytes=LIMIT),
        name="finish",
    )(flags, parts, rotation)


def after(x, token):
    return lax.optimization_barrier((x, token))[0]


def body(slab, hblocks, blist, rotation):
    wide, grp = lax.axis_size("wide"), lax.axis_size("grp")
    _, _, cols, size = slab.shape
    slots = hblocks.shape[2]
    near = [(i, i ^ 1) for i in range(wide)]
    far = [(i, ((i + 1) ^ 1) - 1) for i in range(1, wide - 1)]
    mine, odd = lax.axis_index("grp"), lax.axis_index("wide") % 2
    x = mine // 2
    edge = half = x ^ (mine % 2)
    place = jnp.stack([odd, edge, half, x]).astype(jnp.int32)
    flags = jnp.stack([odd, edge, half, lax.axis_index("wide")]).astype(jnp.int32)
    flags = jnp.broadcast_to(jnp.repeat(flags, VEC)[:, None], (4 * VEC, size))

    def across(value):
        return lax.ppermute(value, "grp", [(i, i ^ 3) for i in range(grp)])

    def core(value):
        return lax.ppermute(value, "grp", [(i, i ^ 1) for i in range(grp)])

    def over_far(value):
        return lax.ppermute(value, "wide", far)

    def over_near(value):
        return lax.ppermute(value, "wide", near)

    own = arrange(flags, blist, slab)
    own_core = core(own[1])
    h_core = core(hblocks)
    border, inside = pick(flags, hblocks, h_core)
    own_across = across(after(jnp.stack([own[0], own_core]), border))
    rows = [own[0], own_core, own_across[0], own_across[1]]
    codes = jnp.stack([row[-VEC : cols - VEC, :slots] for row in rows]).astype(jnp.int32).reshape(-1)
    codes = jnp.concatenate([place, codes])
    states = (own.shape[1] - VEC) // cols
    zero = []
    for u in range(cols):
        parts = [row[u * states : (u + 1) * states] for row in rows]
        border_mine = jnp.stack([parts[m] for m in (1, 0, 2, 3)])
        border_core = jnp.stack([parts[m] for m in (0, 1, 3, 2)])
        zero.append(jnp.where(edge == 1, border_mine, border_core))

    zero[1] = after(zero[1], zero[0])
    far_rim, near_rim = over_far(zero[0]), over_near(zero[1])
    border = across(after(border, own_core))
    inside = across(after(inside, near_rim))
    h_two = [prepare("chip", codes, hblocks, h_core)]
    border_core = core(after(border, (far_rim, h_two)))
    h_three = h_two + [prepare("border", codes, border, border_core)]

    one = [step("first", 0, "one_0", h_three, *zero, far_rim)]
    rim = after(near_rim, one[0])
    one.append(step("first", 1, "one_1", h_three, *zero, rim))
    rims = over_far(one[0]), over_near(one[1])
    acc = [inner(u, f"two_inner_{u}", h_two, one, zero[u]) for u in range(cols)]
    two, sent, before = [], (), []
    for u in range(cols):
        rim = after(rims[u], (sent, inside))
        two.append(step("next", u, f"two_{u}", h_two, rim, acc[u]))
        sent = jnp.concatenate([two[u], one[u][:1]])
        other = across(sent)
        two[u] = jnp.concatenate([two[u], other[1:2], other[0:1]])
        before.append(jnp.concatenate([one[u], other[2:]]))
    inside_core = core(after(inside, two[0]))
    h_four = h_three + [prepare("inner", codes, inside, inside_core)]
    rims = over_far(two[0]), over_near(two[1])
    acc = inner(0, "three_inner_0", h_four, two, before[0])
    three = [step("next", 0, "three_0", h_four, rims[0], acc)]
    rim = after(rims[1], three[0])
    three.append(step("whole", 1, "three_1", h_four, *two, rim, before[1]))
    rims = over_far(three[0]), over_near(three[1])
    acc = [inner(u, f"four_inner_{u}", h_four, three, two[u]) for u in range(cols)]
    four = step("other", 0, "four_0", h_four, rims[0], acc[0])
    kept, sent = step("last", 1, "four_1", h_four, rims[1], acc[1], *four, flags)

    sent = core(sent)
    packed = jnp.where(half == 1, jnp.concatenate([kept, sent]), jnp.concatenate([sent, kept]))
    groups = [[(wide - 1 - i) * grp + g for i in range(wide)] for g in range(grp)]
    packed = lax.all_to_all(
        packed,
        ("wide", "grp"),
        split_axis=0,
        concat_axis=0,
        tiled=True,
        axis_index_groups=groups,
    )
    node_count = grp * wide * cols * size
    return finish(flags, cols, node_count, packed, rotation)


def solution(mesh):
    in_specs = (
        P(None, "grp", "wide", None),
        P("grp", "wide", None, None, None),
        P("grp", "wide", None),
        P(),
    )
    out_specs = P("wide", "grp", None, None)
    return jax.shard_map(body, mesh=mesh, in_specs=in_specs, out_specs=out_specs, check_vma=False)
```

```python
import functools

import jax
import jax.numpy as jnp
from jax import lax
from jax.experimental import pallas as pl
from jax.experimental.pallas import tpu as pltpu
from jax.sharding import PartitionSpec as P

VEC = 8
DEG = 4
LIMIT = 16 * 2**20
BLOCKS = 9
VMEM = pl.BlockSpec(memory_space=pltpu.VMEM)
SMEM = pl.BlockSpec(memory_space=pltpu.SMEM)
NT = (((1,), (1,)), ((), ()))


def split(x):
    high = x.astype(jnp.bfloat16)
    low = (x - high.astype(jnp.float32)).astype(jnp.bfloat16)
    return high, low


def flag(flags_ref, n, shape):
    return jnp.broadcast_to(flags_ref[n * VEC : n * VEC + 1, :], shape) == 1


def arrange_kernel(flags_ref, codes_ref, slab_ref, out_ref):
    all_states, _, cols, size = slab_ref.shape
    slots, states = codes_ref.shape[2], all_states // 2
    odd = flag(flags_ref, 0, (all_states, size))
    second = flag(flags_ref, 2, (states, size))
    both = [slab_ref[:, 0, c, :] for c in range(cols)]
    for u in range(cols):
        value = jnp.where(odd, both[cols - 1 - u], both[u])
        low, high = value[:states], value[states:]
        rows = slice(u * states, (u + 1) * states)
        out_ref[0, rows, :] = jnp.where(second, high, low)
        out_ref[1, rows, :] = jnp.where(second, low, high)
    codes = codes_ref[0].astype(jnp.float32)
    for h in range(2):
        out_ref[h, cols * states :, :] = jnp.zeros((VEC, size), jnp.float32)
        out_ref[h, cols * states : cols * states + cols, 0:slots] = codes


def arrange(flags, blist, slab):
    all_states, _, cols, size = slab.shape
    return pl.pallas_call(
        arrange_kernel,
        in_specs=[VMEM] * 3,
        out_specs=VMEM,
        out_shape=jax.ShapeDtypeStruct((2, cols * all_states // 2 + VEC, size), jnp.float32),
        compiler_params=pltpu.CompilerParams(vmem_limit_bytes=LIMIT),
        name="arrange",
    )(flags, blist, slab)


def pick_kernel(flags_ref, own_ref, core_ref, border_ref, inner_ref):
    shape = own_ref.shape[3:]
    edge, half = flag(flags_ref, 1, shape), flag(flags_ref, 2, shape)
    for k in range(own_ref.shape[2]):
        own = jnp.where(half, own_ref[0, 1, k], own_ref[0, 0, k])
        core = jnp.where(half, core_ref[0, 1, k], core_ref[0, 0, k])
        border_ref[0, 0, k] = jnp.where(edge, own, core)
        inner_ref[0, 0, k] = jnp.where(edge, core, own)


def pick(flags, own, core):
    rows, cols, *block = own.shape
    return pl.pallas_call(
        pick_kernel,
        in_specs=[VMEM] * 3,
        out_specs=[VMEM] * 2,
        out_shape=[jax.ShapeDtypeStruct((rows, 1, *block), own.dtype)] * 2,
        compiler_params=pltpu.CompilerParams(vmem_limit_bytes=LIMIT),
        name="pick",
    )(flags, own, core)


def prepare_kernel(mode, codes_ref, *refs):
    *h_refs, out_ref = refs
    _, cols, slots, size, _ = h_refs[0].shape
    odd, edge, half, x = (codes_ref[n] for n in range(4))
    out_ref[...] = jnp.zeros_like(out_ref)

    def convert(h_ref, h_col, c, q, row):
        u = jnp.bitwise_xor(c, odd)
        for k in range(slots):
            code = codes_ref[4 + (row * 2 + c) * slots + k]
            down = (code >= 3).astype(jnp.int32) + (code >= 6).astype(jnp.int32)
            along = code - 3 * down
            down = jnp.where(x == 1, 2 - down, down)
            along = u + jnp.where(odd == 1, 2 - along, along)
            rim = (along == 0) | (along == 3)
            block = jnp.where(rim, 6 + down, 2 * down + along - 1)
            lanes = pl.ds(pl.multiple_of(block * size, size), size)
            high, low = split(h_ref[0, h_col, k])
            out_ref[q, u, 0:size, lanes] = high
            out_ref[q, u, size : 2 * size, lanes] = low

    for h, h_ref in enumerate(h_refs):
        if mode == "chip":
            for c in range(cols):
                convert(h_ref, c, c, jnp.bitwise_xor(edge, h), h)
        else:
            row = 3 - edge if mode == "border" else 2 + edge
            convert(h_ref, 0, jnp.bitwise_xor(half, h), 0, row)


def prepare(mode, codes, *h_rows):
    _, _, slots, size, _ = h_rows[0].shape
    rows = 2 if mode == "chip" else 1
    return pl.pallas_call(
        functools.partial(prepare_kernel, mode),
        in_specs=[SMEM] + [VMEM] * len(h_rows),
        out_specs=VMEM,
        out_shape=jax.ShapeDtypeStruct((rows, 2, 2 * size, BLOCKS * size), jnp.bfloat16),
        compiler_params=pltpu.CompilerParams(vmem_limit_bytes=LIMIT),
        name="prepare_" + mode,
    )(codes, *h_rows)


def fill(x_ref, fields):
    rows, states, size = fields[0].shape
    for q in range(rows):
        for n, field in enumerate(fields):
            at = (q * len(fields) + n) * size
            high, low = split(field[q])
            x_ref[0:states, at : at + size] = high
            x_ref[states : 2 * states, at : at + size] = low


def products(h_refs, u, x_ref, width, first, rows_in):
    states, size = x_ref.shape[0] // 2, h_refs[0].shape[2] // 2
    width, first = width * size, first * size
    h_rows = [h_ref.at[q] for h_ref in h_refs for q in range(h_ref.shape[0])]
    sums = []
    for q, h_row in enumerate(h_rows):
        low, high = max(q - 1, 0), min(q + 2, rows_in)
        at = first + (low - q + 1) * width
        acc = lax.dot_general(
            x_ref[:, low * width : high * width],
            h_row[u, :, at : at + (high - low) * width],
            NT,
            preferred_element_type=jnp.float32,
        )
        small = acc[states:, size:] + (acc[states:, :size] + acc[:states, size:])
        sums.append(acc[:states, :size] + small)
    return sums


def inner_kernel(u, count, *refs):
    h_refs, (own_0, own_1, before, out_ref, x_ref) = refs[:count], refs[count:]
    fill(x_ref, [own_0, own_1])
    for q, value in enumerate(products(h_refs, u, x_ref, 2, 0, own_0.shape[0])):
        out_ref[q] = 2.0 * value - before[q]


def inner(u, name, h_ready, own, before):
    rows_in, states, size = own[0].shape
    rows_out = sum(h.shape[0] for h in h_ready)
    operands = [*h_ready, *own, before]
    return pl.pallas_call(
        functools.partial(inner_kernel, u, len(h_ready)),
        in_specs=[VMEM] * len(operands),
        out_specs=VMEM,
        out_shape=jax.ShapeDtypeStruct((rows_out, states, size), jnp.float32),
        scratch_shapes=[pltpu.VMEM((2 * states, rows_in * 2 * size), jnp.bfloat16)],
        compiler_params=pltpu.CompilerParams(vmem_limit_bytes=LIMIT),
        cost_estimate=cost_of(rows_out, 6, states, size),
        name=name,
    )(*operands)


def cost_of(rows, blocks, states, size):
    return pl.CostEstimate(
        flops=8 * blocks * rows * states * size * size,
        bytes_accessed=4 * blocks * rows * size * size,
        transcendentals=0,
    )


def step_kernel(kind, u, count, *refs):
    h_refs, refs = refs[:count], refs[count:]
    if kind == "first":
        own_0, own_1, rim_ref, *refs, own_x, rim_x = refs
    else:
        rim_ref, acc_ref, *refs, rim_x = refs
    rows_in, states, size = rim_ref.shape
    fill(rim_x, [rim_ref])
    values = products(h_refs, u, rim_x, 1, 6, rows_in)
    if kind == "first":
        fill(own_x, [own_0, own_1])
        own = products(h_refs, u, own_x, 2, 0, rows_in)
        values = [value + own[q] for q, value in enumerate(values)]
    else:
        values = [acc_ref[q] + 2.0 * value for q, value in enumerate(values)]
    if kind in ("other", "last"):
        flat = [jnp.concatenate(part, axis=1) for part in zip(*map(split, values))]
        flat = jnp.concatenate(flat)
        gram = lax.dot_general(flat, flat, NT, preferred_element_type=jnp.float32)
        gram = gram[:states] + gram[states:]
        gram = gram[:, :states] + gram[:, states:]
    if kind != "last":
        for q, value in enumerate(values):
            refs[0][q] = value
        if kind == "other":
            refs[1][:, 0:states] = gram
        return
    other_ref, other_gram_ref, flags_ref, kept_ref, sent_ref = refs
    odd, edge = flag(flags_ref, 0, (states, size)), flag(flags_ref, 1, (states, size))
    nodes = [[other_ref[q] for q in range(len(values))], values]
    gram = gram + other_gram_ref[:, 0:states]
    blocks = states // VEC
    for c in range(2):
        inner = jnp.where(odd, nodes[1 - c][0], nodes[c][0])
        border = jnp.where(odd, nodes[1 - c][1], nodes[c][1])
        kept, sent = jnp.where(edge, border, inner), jnp.where(edge, inner, border)
        for b in range(blocks):
            rows = slice(b * VEC, (b + 1) * VEC)
            kept_ref[blocks - 1 - b, c * VEC : (c + 1) * VEC, :] = kept[rows]
            sent_ref[blocks - 1 - b, c * VEC : (c + 1) * VEC, :] = sent[rows]
    for b in range(blocks):
        rows = slice(b * VEC, (b + 1) * VEC)
        for ref in (kept_ref, sent_ref):
            ref[blocks - 1 - b, 2 * VEC :, :] = jnp.zeros((VEC, size), jnp.float32)
            ref[blocks - 1 - b, 2 * VEC :, 0:VEC] = gram[rows, rows]


def step(kind, u, name, h_ready, *operands):
    merged = kind == "first"
    rows_in, states, size = operands[0].shape
    rows_out = sum(h.shape[0] for h in h_ready)
    shapes = [(rows_out, states, size)]
    if kind == "other":
        shapes.append((states, pl.cdiv(states, size) * size))
    elif kind == "last":
        shapes = [(states // VEC, 3 * VEC, size)] * 2
    operands = [*h_ready, *operands]
    outs = pl.pallas_call(
        functools.partial(step_kernel, kind, u, len(h_ready)),
        in_specs=[VMEM] * len(operands),
        out_specs=[VMEM] * len(shapes),
        out_shape=[jax.ShapeDtypeStruct(shape, jnp.float32) for shape in shapes],
        scratch_shapes=[
            pltpu.VMEM((2 * states, rows_in * width * size), jnp.bfloat16)
            for width in ((2, 1) if merged else (1,))
        ],
        compiler_params=pltpu.CompilerParams(vmem_limit_bytes=LIMIT),
        cost_estimate=cost_of(rows_out, BLOCKS if merged else 3, states, size),
        name=name,
    )(*operands)
    return outs[0] if len(outs) == 1 else outs


def finish_kernel(cols, node_count, flags_ref, parts_ref, rot_ref, out_ref):
    wide = parts_ref.shape[0]
    gram = parts_ref[0, cols * VEC : (cols + 1) * VEC, 0:VEC]
    for w in range(1, wide):
        gram = gram + parts_ref[w, cols * VEC : (cols + 1) * VEC, 0:VEC]
    gram = gram / node_count
    row = lax.broadcasted_iota(jnp.int32, (VEC, VEC), 0)
    col = lax.broadcasted_iota(jnp.int32, (VEC, VEC), 1)
    inverse = jnp.where(row == col, 1.0, 0.0).astype(jnp.float32)
    for k in range(VEC):
        scale = 1.0 / jnp.sqrt(gram[k : k + 1, k : k + 1])
        top = gram[k : k + 1, :] * scale
        top_inverse = inverse[k : k + 1, :] * scale
        factor = gram[:, k : k + 1] * scale
        gram = gram - factor * top
        inverse = jnp.where(row == k, top_inverse, jnp.where(row > k, inverse - factor * top_inverse, inverse))
    number = jnp.broadcast_to(flags_ref[3 * VEC : 3 * VEC + 1, 0:VEC], (VEC, VEC))
    turn = rot_ref[0]
    for w in range(1, wide):
        turn = jnp.where(number == w, rot_ref[w], turn)
    turn = turn.T
    mixer = turn[:, 0:1] * inverse[0:1, :]
    for k in range(1, VEC):
        mixer = mixer + turn[:, k : k + 1] * inverse[k : k + 1, :]
    columns = [mixer[:, d : d + 1] for d in range(VEC)]
    mixed = []
    for w in range(wide):
        for c in range(cols):
            block = parts_ref[w, c * VEC : (c + 1) * VEC, :]
            total = columns[0] * block[0:1, :]
            for d in range(1, VEC):
                total = total + columns[d] * block[d : d + 1, :]
            mixed.append(total)
    for w in range(wide):
        for c in range(cols):
            out_ref[:, 0, w * cols + c, :] = mixed[(wide - 1 - w) * cols + c]


def finish(flags, cols, node_count, parts, rotation):
    wide, _, size = parts.shape
    return pl.pallas_call(
        functools.partial(finish_kernel, cols, node_count),
        in_specs=[VMEM] * 3,
        out_specs=VMEM,
        out_shape=jax.ShapeDtypeStruct((VEC, 1, wide * cols, size), jnp.float32),
        compiler_params=pltpu.CompilerParams(vmem_limit_bytes=LIMIT),
        name="finish",
    )(flags, parts, rotation)


def after(x, token):
    return lax.optimization_barrier((x, token))[0]


def body(slab, hblocks, blist, rotation):
    wide, grp = lax.axis_size("wide"), lax.axis_size("grp")
    _, _, cols, size = slab.shape
    slots = hblocks.shape[2]
    near = [(i, i ^ 1) for i in range(wide)]
    far = [(i, ((i + 1) ^ 1) - 1) for i in range(1, wide - 1)]
    mine, odd = lax.axis_index("grp"), lax.axis_index("wide") % 2
    x = mine // 2
    edge = half = x ^ (mine % 2)
    place = jnp.stack([odd, edge, half, x]).astype(jnp.int32)
    flags = jnp.stack([odd, edge, half, lax.axis_index("wide")]).astype(jnp.int32)
    flags = jnp.broadcast_to(jnp.repeat(flags, VEC)[:, None], (4 * VEC, size))

    def across(value):
        return lax.ppermute(value, "grp", [(i, i ^ 3) for i in range(grp)])

    def core(value):
        return lax.ppermute(value, "grp", [(i, i ^ 1) for i in range(grp)])

    def over_far(value):
        return lax.ppermute(value, "wide", far)

    def over_near(value):
        return lax.ppermute(value, "wide", near)

    own = arrange(flags, blist, slab)
    own_core = core(own[1])
    h_core = core(hblocks)
    border, inside = pick(flags, hblocks, h_core)
    own_across = across(after(jnp.stack([own[0], own_core]), border))
    rows = [own[0], own_core, own_across[0], own_across[1]]
    codes = jnp.stack([row[-VEC : cols - VEC, :slots] for row in rows]).astype(jnp.int32).reshape(-1)
    codes = jnp.concatenate([place, codes])
    states = (own.shape[1] - VEC) // cols
    zero = []
    for u in range(cols):
        parts = [row[u * states : (u + 1) * states] for row in rows]
        border_mine = jnp.stack([parts[m] for m in (1, 0, 2, 3)])
        border_core = jnp.stack([parts[m] for m in (0, 1, 3, 2)])
        zero.append(jnp.where(edge == 1, border_mine, border_core))

    zero[1] = after(zero[1], zero[0])
    far_rim, near_rim = over_far(zero[0]), over_near(zero[1])
    border = across(after(border, own_core))
    inside = across(after(inside, near_rim))
    h_two = [prepare("chip", codes, hblocks, h_core)]
    border_core = core(after(border, (far_rim, h_two)))
    h_three = h_two + [prepare("border", codes, border, border_core)]

    one = [step("first", 0, "one_0", h_three, *zero, far_rim)]
    rim = after(near_rim, one[0])
    one.append(step("first", 1, "one_1", h_three, *zero, rim))
    rims = over_far(one[0]), over_near(one[1])
    acc = [inner(u, f"two_inner_{u}", h_two, one, zero[u]) for u in range(cols)]
    two, sent, before = [], (), []
    for u in range(cols):
        rim = after(rims[u], (sent, inside))
        two.append(step("next", u, f"two_{u}", h_two, rim, acc[u]))
        sent = jnp.concatenate([two[u], one[u][:1]])
        other = across(sent)
        two[u] = jnp.concatenate([two[u], other[1:2], other[0:1]])
        before.append(jnp.concatenate([one[u], other[2:]]))
    inside_core = core(after(inside, two[0]))
    h_four = h_three + [prepare("inner", codes, inside, inside_core)]
    rims = over_far(two[0]), over_near(two[1])
    acc = [inner(0, "three_inner_0", h_four, two, before[0])]
    acc.append(inner(1, "three_inner_1", h_four, two, after(before[1], acc[0])))
    three = [step("next", 0, "three_0", h_four, after(rims[0], acc[1]), acc[0])]
    rim = after(rims[1], three[0])
    three.append(step("next", 1, "three_1", h_four, rim, acc[1]))
    rims = over_far(three[0]), over_near(three[1])
    acc = [inner(u, f"four_inner_{u}", h_four, three, two[u]) for u in range(cols)]
    four = step("other", 0, "four_0", h_four, rims[0], acc[0])
    kept, sent = step("last", 1, "four_1", h_four, rims[1], acc[1], *four, flags)

    sent = core(sent)
    packed = jnp.where(half == 1, jnp.concatenate([kept, sent]), jnp.concatenate([sent, kept]))
    groups = [[(wide - 1 - i) * grp + g for i in range(wide)] for g in range(grp)]
    packed = lax.all_to_all(
        packed,
        ("wide", "grp"),
        split_axis=0,
        concat_axis=0,
        tiled=True,
        axis_index_groups=groups,
    )
    node_count = grp * wide * cols * size
    return finish(flags, cols, node_count, packed, rotation)


def solution(mesh):
    in_specs = (
        P(None, "grp", "wide", None),
        P("grp", "wide", None, None, None),
        P("grp", "wide", None),
        P(),
    )
    out_specs = P("wide", "grp", None, None)
    return jax.shard_map(body, mesh=mesh, in_specs=in_specs, out_specs=out_specs, check_vma=False)
```

```python
import functools

import jax
import jax.numpy as jnp
from jax import lax
from jax.experimental import pallas as pl
from jax.experimental.pallas import tpu as pltpu
from jax.sharding import PartitionSpec as P

VEC = 8
DEG = 4
LIMIT = 16 * 2**20
BLOCKS = 9
VMEM = pl.BlockSpec(memory_space=pltpu.VMEM)
SMEM = pl.BlockSpec(memory_space=pltpu.SMEM)
NT = (((1,), (1,)), ((), ()))


def split(x):
    high = x.astype(jnp.bfloat16)
    low = (x - high.astype(jnp.float32)).astype(jnp.bfloat16)
    return high, low


def flag(flags_ref, n, shape):
    return jnp.broadcast_to(flags_ref[n * VEC : n * VEC + 1, :], shape) == 1


def arrange_kernel(flags_ref, codes_ref, slab_ref, out_ref):
    all_states, _, cols, size = slab_ref.shape
    slots, states = codes_ref.shape[2], all_states // 2
    odd = flag(flags_ref, 0, (all_states, size))
    second = flag(flags_ref, 2, (states, size))
    both = [slab_ref[:, 0, c, :] for c in range(cols)]
    for u in range(cols):
        value = jnp.where(odd, both[cols - 1 - u], both[u])
        low, high = value[:states], value[states:]
        rows = slice(u * states, (u + 1) * states)
        out_ref[0, rows, :] = jnp.where(second, high, low)
        out_ref[1, rows, :] = jnp.where(second, low, high)
    codes = codes_ref[0].astype(jnp.float32)
    for h in range(2):
        out_ref[h, cols * states :, :] = jnp.zeros((VEC, size), jnp.float32)
        out_ref[h, cols * states : cols * states + cols, 0:slots] = codes


def arrange(flags, blist, slab):
    all_states, _, cols, size = slab.shape
    return pl.pallas_call(
        arrange_kernel,
        in_specs=[VMEM] * 3,
        out_specs=VMEM,
        out_shape=jax.ShapeDtypeStruct((2, cols * all_states // 2 + VEC, size), jnp.float32),
        compiler_params=pltpu.CompilerParams(vmem_limit_bytes=LIMIT),
        name="arrange",
    )(flags, blist, slab)


def pick_kernel(flags_ref, own_ref, core_ref, border_ref, inner_ref):
    shape = own_ref.shape[3:]
    edge, half = flag(flags_ref, 1, shape), flag(flags_ref, 2, shape)
    for k in range(own_ref.shape[2]):
        own = jnp.where(half, own_ref[0, 1, k], own_ref[0, 0, k])
        core = jnp.where(half, core_ref[0, 1, k], core_ref[0, 0, k])
        border_ref[0, 0, k] = jnp.where(edge, own, core)
        inner_ref[0, 0, k] = jnp.where(edge, core, own)


def pick(flags, own, core):
    rows, cols, *block = own.shape
    return pl.pallas_call(
        pick_kernel,
        in_specs=[VMEM] * 3,
        out_specs=[VMEM] * 2,
        out_shape=[jax.ShapeDtypeStruct((rows, 1, *block), own.dtype)] * 2,
        compiler_params=pltpu.CompilerParams(vmem_limit_bytes=LIMIT),
        name="pick",
    )(flags, own, core)


def prepare_kernel(mode, codes_ref, *refs):
    *h_refs, out_ref = refs
    _, cols, slots, size, _ = h_refs[0].shape
    odd, edge, half, x = (codes_ref[n] for n in range(4))
    out_ref[...] = jnp.zeros_like(out_ref)

    def convert(h_ref, h_col, c, q, row):
        u = jnp.bitwise_xor(c, odd)
        for k in range(slots):
            code = codes_ref[4 + (row * 2 + c) * slots + k]
            down = (code >= 3).astype(jnp.int32) + (code >= 6).astype(jnp.int32)
            along = code - 3 * down
            down = jnp.where(x == 1, 2 - down, down)
            along = u + jnp.where(odd == 1, 2 - along, along)
            rim = (along == 0) | (along == 3)
            block = jnp.where(rim, 6 + down, 2 * down + along - 1)
            lanes = pl.ds(pl.multiple_of(block * size, size), size)
            high, low = split(h_ref[0, h_col, k])
            out_ref[q, u, 0:size, lanes] = high
            out_ref[q, u, size : 2 * size, lanes] = low

    for h, h_ref in enumerate(h_refs):
        if mode == "chip":
            for c in range(cols):
                convert(h_ref, c, c, jnp.bitwise_xor(edge, h), h)
        else:
            row = 3 - edge if mode == "border" else 2 + edge
            convert(h_ref, 0, jnp.bitwise_xor(half, h), 0, row)


def prepare(mode, codes, *h_rows):
    _, _, slots, size, _ = h_rows[0].shape
    rows = 2 if mode == "chip" else 1
    return pl.pallas_call(
        functools.partial(prepare_kernel, mode),
        in_specs=[SMEM] + [VMEM] * len(h_rows),
        out_specs=VMEM,
        out_shape=jax.ShapeDtypeStruct((rows, 2, 2 * size, BLOCKS * size), jnp.bfloat16),
        compiler_params=pltpu.CompilerParams(vmem_limit_bytes=LIMIT),
        name="prepare_" + mode,
    )(codes, *h_rows)


def fill(x_ref, fields):
    rows, states, size = fields[0].shape
    for q in range(rows):
        for n, field in enumerate(fields):
            at = (q * len(fields) + n) * size
            high, low = split(field[q])
            x_ref[0:states, at : at + size] = high
            x_ref[states : 2 * states, at : at + size] = low


def products(h_refs, u, x_ref, width, first, rows_in):
    states, size = x_ref.shape[0] // 2, h_refs[0].shape[2] // 2
    width, first = width * size, first * size
    h_rows = [h_ref.at[q] for h_ref in h_refs for q in range(h_ref.shape[0])]
    sums = []
    for q, h_row in enumerate(h_rows):
        low, high = max(q - 1, 0), min(q + 2, rows_in)
        at = first + (low - q + 1) * width
        acc = lax.dot_general(
            x_ref[:, low * width : high * width],
            h_row[u, :, at : at + (high - low) * width],
            NT,
            preferred_element_type=jnp.float32,
        )
        small = acc[states:, size:] + (acc[states:, :size] + acc[:states, size:])
        sums.append(acc[:states, :size] + small)
    return sums


def inner_kernel(u, count, *refs):
    h_refs, (own_0, own_1, before, out_ref, x_ref) = refs[:count], refs[count:]
    fill(x_ref, [own_0, own_1])
    for q, value in enumerate(products(h_refs, u, x_ref, 2, 0, own_0.shape[0])):
        out_ref[q] = 2.0 * value - before[q]


def inner(u, name, h_ready, own, before):
    rows_in, states, size = own[0].shape
    rows_out = sum(h.shape[0] for h in h_ready)
    operands = [*h_ready, *own, before]
    return pl.pallas_call(
        functools.partial(inner_kernel, u, len(h_ready)),
        in_specs=[VMEM] * len(operands),
        out_specs=VMEM,
        out_shape=jax.ShapeDtypeStruct((rows_out, states, size), jnp.float32),
        scratch_shapes=[pltpu.VMEM((2 * states, rows_in * 2 * size), jnp.bfloat16)],
        compiler_params=pltpu.CompilerParams(vmem_limit_bytes=LIMIT),
        cost_estimate=cost_of(rows_out, 6, states, size),
        name=name,
    )(*operands)


def cost_of(rows, blocks, states, size):
    return pl.CostEstimate(
        flops=8 * blocks * rows * states * size * size,
        bytes_accessed=4 * blocks * rows * size * size,
        transcendentals=0,
    )


def step_kernel(kind, u, count, *refs):
    h_refs, refs = refs[:count], refs[count:]
    if kind in ("first", "whole"):
        own_0, own_1, rim_ref, *refs, own_x, rim_x = refs
    else:
        rim_ref, acc_ref, *refs, rim_x = refs
    rows_in, states, size = rim_ref.shape
    fill(rim_x, [rim_ref])
    values = products(h_refs, u, rim_x, 1, 6, rows_in)
    if kind in ("first", "whole"):
        fill(own_x, [own_0, own_1])
        own = products(h_refs, u, own_x, 2, 0, rows_in)
        values = [value + own[q] for q, value in enumerate(values)]
        if kind == "whole":
            before, *refs = refs
            values = [2.0 * value - before[q] for q, value in enumerate(values)]
    else:
        values = [acc_ref[q] + 2.0 * value for q, value in enumerate(values)]
    if kind in ("other", "last"):
        flat = [jnp.concatenate(part, axis=1) for part in zip(*map(split, values))]
        flat = jnp.concatenate(flat)
        gram = lax.dot_general(flat, flat, NT, preferred_element_type=jnp.float32)
        gram = gram[:states] + gram[states:]
        gram = gram[:, :states] + gram[:, states:]
    if kind != "last":
        for q, value in enumerate(values):
            refs[0][q] = value
        if kind == "other":
            refs[1][:, 0:states] = gram
        return
    other_ref, other_gram_ref, flags_ref, kept_ref, sent_ref = refs
    odd, edge = flag(flags_ref, 0, (states, size)), flag(flags_ref, 1, (states, size))
    nodes = [[other_ref[q] for q in range(len(values))], values]
    gram = gram + other_gram_ref[:, 0:states]
    blocks = states // VEC
    for c in range(2):
        inner = jnp.where(odd, nodes[1 - c][0], nodes[c][0])
        border = jnp.where(odd, nodes[1 - c][1], nodes[c][1])
        kept, sent = jnp.where(edge, border, inner), jnp.where(edge, inner, border)
        for b in range(blocks):
            rows = slice(b * VEC, (b + 1) * VEC)
            kept_ref[b, c * VEC : (c + 1) * VEC, :] = kept[rows]
            sent_ref[b, c * VEC : (c + 1) * VEC, :] = sent[rows]
    for b in range(blocks):
        rows = slice(b * VEC, (b + 1) * VEC)
        for ref in (kept_ref, sent_ref):
            ref[b, 2 * VEC :, :] = jnp.zeros((VEC, size), jnp.float32)
            ref[b, 2 * VEC :, 0:VEC] = gram[rows, rows]


def step(kind, u, name, h_ready, *operands):
    merged = kind in ("first", "whole")
    rows_in, states, size = operands[0].shape
    rows_out = sum(h.shape[0] for h in h_ready)
    shapes = [(rows_out, states, size)]
    if kind == "other":
        shapes.append((states, pl.cdiv(states, size) * size))
    elif kind == "last":
        shapes = [(states // VEC, 3 * VEC, size)] * 2
    operands = [*h_ready, *operands]
    outs = pl.pallas_call(
        functools.partial(step_kernel, kind, u, len(h_ready)),
        in_specs=[VMEM] * len(operands),
        out_specs=[VMEM] * len(shapes),
        out_shape=[jax.ShapeDtypeStruct(shape, jnp.float32) for shape in shapes],
        scratch_shapes=[
            pltpu.VMEM((2 * states, rows_in * width * size), jnp.bfloat16)
            for width in ((2, 1) if merged else (1,))
        ],
        compiler_params=pltpu.CompilerParams(vmem_limit_bytes=LIMIT),
        cost_estimate=cost_of(rows_out, BLOCKS if merged else 3, states, size),
        name=name,
    )(*operands)
    return outs[0] if len(outs) == 1 else outs


def finish_kernel(cols, node_count, flags_ref, parts_ref, rot_ref, out_ref):
    wide = parts_ref.shape[0]
    gram = parts_ref[0, cols * VEC : (cols + 1) * VEC, 0:VEC]
    for w in range(1, wide):
        gram = gram + parts_ref[w, cols * VEC : (cols + 1) * VEC, 0:VEC]
    gram = gram / node_count
    row = lax.broadcasted_iota(jnp.int32, (VEC, VEC), 0)
    col = lax.broadcasted_iota(jnp.int32, (VEC, VEC), 1)
    inverse = jnp.where(row == col, 1.0, 0.0).astype(jnp.float32)
    for k in range(VEC):
        scale = 1.0 / jnp.sqrt(gram[k : k + 1, k : k + 1])
        top = gram[k : k + 1, :] * scale
        top_inverse = inverse[k : k + 1, :] * scale
        factor = gram[:, k : k + 1] * scale
        gram = gram - factor * top
        inverse = jnp.where(row == k, top_inverse, jnp.where(row > k, inverse - factor * top_inverse, inverse))
    number = jnp.broadcast_to(flags_ref[3 * VEC : 3 * VEC + 1, 0:VEC], (VEC, VEC))
    turn = rot_ref[0]
    for w in range(1, wide):
        turn = jnp.where(number == w, rot_ref[w], turn)
    turn = turn.T
    mixer = turn[:, 0:1] * inverse[0:1, :]
    for k in range(1, VEC):
        mixer = mixer + turn[:, k : k + 1] * inverse[k : k + 1, :]
    columns = [mixer[:, d : d + 1] for d in range(VEC)]
    mixed = []
    for w in range(wide):
        for c in range(cols):
            block = parts_ref[w, c * VEC : (c + 1) * VEC, :]
            total = columns[0] * block[0:1, :]
            for d in range(1, VEC):
                total = total + columns[d] * block[d : d + 1, :]
            mixed.append(total)
    for w in range(wide):
        for c in range(cols):
            out_ref[:, 0, w * cols + c, :] = mixed[w * cols + c]


def finish(flags, cols, node_count, parts, rotation):
    wide, _, size = parts.shape
    return pl.pallas_call(
        functools.partial(finish_kernel, cols, node_count),
        in_specs=[VMEM] * 3,
        out_specs=VMEM,
        out_shape=jax.ShapeDtypeStruct((VEC, 1, wide * cols, size), jnp.float32),
        compiler_params=pltpu.CompilerParams(vmem_limit_bytes=LIMIT),
        name="finish",
    )(flags, parts, rotation)


def after(x, token):
    return lax.optimization_barrier((x, token))[0]


def body(slab, hblocks, blist, rotation):
    wide, grp = lax.axis_size("wide"), lax.axis_size("grp")
    _, _, cols, size = slab.shape
    slots = hblocks.shape[2]
    near = [(i, i ^ 1) for i in range(wide)]
    far = [(i, ((i + 1) ^ 1) - 1) for i in range(1, wide - 1)]
    mine, odd = lax.axis_index("grp"), lax.axis_index("wide") % 2
    x = mine // 2
    edge = half = x ^ (mine % 2)
    place = jnp.stack([odd, edge, half, x]).astype(jnp.int32)
    flags = jnp.stack([odd, edge, half, lax.axis_index("wide")]).astype(jnp.int32)
    flags = jnp.broadcast_to(jnp.repeat(flags, VEC)[:, None], (4 * VEC, size))

    def across(value):
        return lax.ppermute(value, "grp", [(i, i ^ 3) for i in range(grp)])

    def core(value):
        return lax.ppermute(value, "grp", [(i, i ^ 1) for i in range(grp)])

    def over_far(value):
        return lax.ppermute(value, "wide", far)

    def over_near(value):
        return lax.ppermute(value, "wide", near)

    own = arrange(flags, blist, slab)
    own_core = core(own[1])
    h_core = core(hblocks)
    border, inside = pick(flags, hblocks, h_core)
    own_across = across(after(jnp.stack([own[0], own_core]), border))
    rows = [own[0], own_core, own_across[0], own_across[1]]
    codes = jnp.stack([row[-VEC : cols - VEC, :slots] for row in rows]).astype(jnp.int32).reshape(-1)
    codes = jnp.concatenate([place, codes])
    states = (own.shape[1] - VEC) // cols
    zero = []
    for u in range(cols):
        parts = [row[u * states : (u + 1) * states] for row in rows]
        border_mine = jnp.stack([parts[m] for m in (1, 0, 2, 3)])
        border_core = jnp.stack([parts[m] for m in (0, 1, 3, 2)])
        zero.append(jnp.where(edge == 1, border_mine, border_core))

    zero[1] = after(zero[1], zero[0])
    far_rim, near_rim = over_far(zero[0]), over_near(zero[1])
    border = across(after(border, own_core))
    inside = across(after(inside, near_rim))
    h_two = [prepare("chip", codes, hblocks, h_core)]
    border_core = core(after(border, (far_rim, h_two)))
    h_three = h_two + [prepare("border", codes, border, border_core)]

    one = [step("first", 0, "one_0", h_three, *zero, far_rim)]
    rim = after(near_rim, one[0])
    one.append(step("first", 1, "one_1", h_three, *zero, rim))
    rims = over_far(one[0]), over_near(one[1])
    acc = [inner(u, f"two_inner_{u}", h_two, one, zero[u]) for u in range(cols)]
    two, sent, before = [], (), []
    for u in range(cols):
        rim = after(rims[u], (sent, inside))
        two.append(step("next", u, f"two_{u}", h_two, rim, acc[u]))
        sent = jnp.concatenate([two[u], one[u][:1]])
        other = across(sent)
        two[u] = jnp.concatenate([two[u], other[1:2], other[0:1]])
        before.append(jnp.concatenate([one[u], other[2:]]))
    inside_core = core(after(inside, two[0]))
    h_four = h_three + [prepare("inner", codes, inside, inside_core)]
    rims = over_far(two[0]), over_near(two[1])
    acc = inner(0, "three_inner_0", h_four, two, before[0])
    three = [step("next", 0, "three_0", h_four, rims[0], acc)]
    rim = after(rims[1], three[0])
    three.append(step("whole", 1, "three_1", h_four, *two, rim, before[1]))
    rims = over_far(three[0]), over_near(three[1])
    acc = [inner(u, f"four_inner_{u}", h_four, three, two[u]) for u in range(cols)]
    four = step("other", 0, "four_0", h_four, rims[0], acc[0])
    kept, sent = step("last", 1, "four_1", h_four, rims[1], acc[1], *four, flags)

    sent = core(sent)
    packed = jnp.where(half == 1, jnp.concatenate([sent, kept]), jnp.concatenate([kept, sent]))
    packed = lax.all_to_all(packed, "wide", split_axis=0, concat_axis=0, tiled=True)
    node_count = grp * wide * cols * size
    return finish(flags, cols, node_count, packed, rotation)


def solution(mesh):
    in_specs = (
        P(None, "grp", "wide", None),
        P("grp", "wide", None, None, None),
        P("grp", "wide", None),
        P(),
    )
    out_specs = P("wide", "grp", None, None)
    return jax.shard_map(body, mesh=mesh, in_specs=in_specs, out_specs=out_specs, check_vma=False)
```

```python
import functools

import jax
import jax.numpy as jnp
from jax import lax
from jax.experimental import pallas as pl
from jax.experimental.pallas import tpu as pltpu
from jax.sharding import PartitionSpec as P

VEC = 8
DEG = 4
LIMIT = 16 * 2**20
BLOCKS = 9
VMEM = pl.BlockSpec(memory_space=pltpu.VMEM)
SMEM = pl.BlockSpec(memory_space=pltpu.SMEM)
NT = (((1,), (1,)), ((), ()))


def split(x):
    high = x.astype(jnp.bfloat16)
    low = (x - high.astype(jnp.float32)).astype(jnp.bfloat16)
    return high, low


def flag(flags_ref, n, shape):
    return jnp.broadcast_to(flags_ref[n * VEC : n * VEC + 1, :], shape) == 1


def arrange_kernel(flags_ref, codes_ref, slab_ref, out_ref):
    all_states, _, cols, size = slab_ref.shape
    slots, states = codes_ref.shape[2], all_states // 2
    odd = flag(flags_ref, 0, (all_states, size))
    second = flag(flags_ref, 2, (states, size))
    both = [slab_ref[:, 0, c, :] for c in range(cols)]
    for u in range(cols):
        value = jnp.where(odd, both[cols - 1 - u], both[u])
        low, high = value[:states], value[states:]
        rows = slice(u * states, (u + 1) * states)
        out_ref[0, rows, :] = jnp.where(second, high, low)
        out_ref[1, rows, :] = jnp.where(second, low, high)
    codes = codes_ref[0].astype(jnp.float32)
    for h in range(2):
        out_ref[h, cols * states :, :] = jnp.zeros((VEC, size), jnp.float32)
        out_ref[h, cols * states : cols * states + cols, 0:slots] = codes


def arrange(flags, blist, slab):
    all_states, _, cols, size = slab.shape
    return pl.pallas_call(
        arrange_kernel,
        in_specs=[VMEM] * 3,
        out_specs=VMEM,
        out_shape=jax.ShapeDtypeStruct((2, cols * all_states // 2 + VEC, size), jnp.float32),
        compiler_params=pltpu.CompilerParams(vmem_limit_bytes=LIMIT),
        name="arrange",
    )(flags, blist, slab)


def pick_kernel(flags_ref, own_ref, core_ref, border_ref, inner_ref):
    shape = own_ref.shape[3:]
    edge, half = flag(flags_ref, 1, shape), flag(flags_ref, 2, shape)
    for k in range(own_ref.shape[2]):
        own = jnp.where(half, own_ref[0, 1, k], own_ref[0, 0, k])
        core = jnp.where(half, core_ref[0, 1, k], core_ref[0, 0, k])
        border_ref[0, 0, k] = jnp.where(edge, own, core)
        inner_ref[0, 0, k] = jnp.where(edge, core, own)


def pick(flags, own, core):
    rows, cols, *block = own.shape
    return pl.pallas_call(
        pick_kernel,
        in_specs=[VMEM] * 3,
        out_specs=[VMEM] * 2,
        out_shape=[jax.ShapeDtypeStruct((rows, 1, *block), own.dtype)] * 2,
        compiler_params=pltpu.CompilerParams(vmem_limit_bytes=LIMIT),
        name="pick",
    )(flags, own, core)


def prepare_kernel(mode, codes_ref, *refs):
    *h_refs, out_ref = refs
    _, cols, slots, size, _ = h_refs[0].shape
    odd, edge, half, x = (codes_ref[n] for n in range(4))
    out_ref[...] = jnp.zeros_like(out_ref)

    def convert(h_ref, h_col, c, q, row):
        u = jnp.bitwise_xor(c, odd)
        for k in range(slots):
            code = codes_ref[4 + (row * 2 + c) * slots + k]
            down = (code >= 3).astype(jnp.int32) + (code >= 6).astype(jnp.int32)
            along = code - 3 * down
            down = jnp.where(x == 1, 2 - down, down)
            along = u + jnp.where(odd == 1, 2 - along, along)
            rim = (along == 0) | (along == 3)
            block = jnp.where(rim, 6 + down, 2 * down + along - 1)
            lanes = pl.ds(pl.multiple_of(block * size, size), size)
            high, low = split(h_ref[0, h_col, k])
            out_ref[q, u, 0:size, lanes] = high
            out_ref[q, u, size : 2 * size, lanes] = low

    for h, h_ref in enumerate(h_refs):
        if mode == "chip":
            for c in range(cols):
                convert(h_ref, c, c, jnp.bitwise_xor(edge, h), h)
        else:
            row = 3 - edge if mode == "border" else 2 + edge
            convert(h_ref, 0, jnp.bitwise_xor(half, h), 0, row)


def prepare(mode, codes, *h_rows):
    _, _, slots, size, _ = h_rows[0].shape
    rows = 2 if mode == "chip" else 1
    return pl.pallas_call(
        functools.partial(prepare_kernel, mode),
        in_specs=[SMEM] + [VMEM] * len(h_rows),
        out_specs=VMEM,
        out_shape=jax.ShapeDtypeStruct((rows, 2, 2 * size, BLOCKS * size), jnp.bfloat16),
        compiler_params=pltpu.CompilerParams(vmem_limit_bytes=LIMIT),
        name="prepare_" + mode,
    )(codes, *h_rows)


def fill(x_ref, fields):
    rows, states, size = fields[0].shape
    for q in range(rows):
        for n, field in enumerate(fields):
            at = (q * len(fields) + n) * size
            high, low = split(field[q])
            x_ref[0:states, at : at + size] = high
            x_ref[states : 2 * states, at : at + size] = low


def products(h_refs, u, x_ref, width, first, rows_in):
    states, size = x_ref.shape[0] // 2, h_refs[0].shape[2] // 2
    width, first = width * size, first * size
    h_rows = [h_ref.at[q] for h_ref in h_refs for q in range(h_ref.shape[0])]
    sums = []
    for q, h_row in enumerate(h_rows):
        low, high = max(q - 1, 0), min(q + 2, rows_in)
        at = first + (low - q + 1) * width
        acc = lax.dot_general(
            x_ref[:, low * width : high * width],
            h_row[u, :, at : at + (high - low) * width],
            NT,
            preferred_element_type=jnp.float32,
        )
        small = acc[states:, size:] + (acc[states:, :size] + acc[:states, size:])
        sums.append(acc[:states, :size] + small)
    return sums


def inner_kernel(u, count, *refs):
    h_refs, (own_0, own_1, before, out_ref, x_ref) = refs[:count], refs[count:]
    fill(x_ref, [own_0, own_1])
    for q, value in enumerate(products(h_refs, u, x_ref, 2, 0, own_0.shape[0])):
        out_ref[q] = 2.0 * value - before[q]


def inner(u, name, h_ready, own, before):
    rows_in, states, size = own[0].shape
    rows_out = sum(h.shape[0] for h in h_ready)
    operands = [*h_ready, *own, before]
    return pl.pallas_call(
        functools.partial(inner_kernel, u, len(h_ready)),
        in_specs=[VMEM] * len(operands),
        out_specs=VMEM,
        out_shape=jax.ShapeDtypeStruct((rows_out, states, size), jnp.float32),
        scratch_shapes=[pltpu.VMEM((2 * states, rows_in * 2 * size), jnp.bfloat16)],
        compiler_params=pltpu.CompilerParams(vmem_limit_bytes=LIMIT),
        cost_estimate=cost_of(rows_out, 6, states, size),
        name=name,
    )(*operands)


def cost_of(rows, blocks, states, size):
    return pl.CostEstimate(
        flops=8 * blocks * rows * states * size * size,
        bytes_accessed=4 * blocks * rows * size * size,
        transcendentals=0,
    )


def step_kernel(kind, u, count, *refs):
    h_refs, refs = refs[:count], refs[count:]
    if kind in ("first", "whole"):
        own_0, own_1, rim_ref, *refs, own_x, rim_x = refs
    else:
        rim_ref, acc_ref, *refs, rim_x = refs
    rows_in, states, size = rim_ref.shape
    fill(rim_x, [rim_ref])
    values = products(h_refs, u, rim_x, 1, 6, rows_in)
    if kind in ("first", "whole"):
        fill(own_x, [own_0, own_1])
        own = products(h_refs, u, own_x, 2, 0, rows_in)
        values = [value + own[q] for q, value in enumerate(values)]
        if kind == "whole":
            before, *refs = refs
            values = [2.0 * value - before[q] for q, value in enumerate(values)]
    else:
        values = [acc_ref[q] + 2.0 * value for q, value in enumerate(values)]
    if kind in ("other", "last"):
        flat = [jnp.concatenate(part, axis=1) for part in zip(*map(split, values))]
        flat = jnp.concatenate(flat)
        gram = lax.dot_general(flat, flat, NT, preferred_element_type=jnp.float32)
        gram = gram[:states] + gram[states:]
        gram = gram[:, :states] + gram[:, states:]
    if kind != "last":
        for q, value in enumerate(values):
            refs[0][q] = value
        if kind == "other":
            refs[1][:, 0:states] = gram
        return
    other_ref, other_gram_ref, flags_ref, kept_ref, sent_ref = refs
    odd, edge = flag(flags_ref, 0, (states, size)), flag(flags_ref, 1, (states, size))
    nodes = [[other_ref[q] for q in range(len(values))], values]
    gram = gram + other_gram_ref[:, 0:states]
    blocks = states // VEC
    for c in range(2):
        inner = jnp.where(odd, nodes[1 - c][0], nodes[c][0])
        border = jnp.where(odd, nodes[1 - c][1], nodes[c][1])
        kept, sent = jnp.where(edge, border, inner), jnp.where(edge, inner, border)
        for b in range(blocks):
            rows = slice(b * VEC, (b + 1) * VEC)
            kept_ref[blocks - 1 - b, c * VEC : (c + 1) * VEC, :] = kept[rows]
            sent_ref[blocks - 1 - b, c * VEC : (c + 1) * VEC, :] = sent[rows]
    for b in range(blocks):
        rows = slice(b * VEC, (b + 1) * VEC)
        for ref in (kept_ref, sent_ref):
            ref[blocks - 1 - b, 2 * VEC :, :] = jnp.zeros((VEC, size), jnp.float32)
            ref[blocks - 1 - b, 2 * VEC :, 0:VEC] = gram[rows, rows]


def step(kind, u, name, h_ready, *operands):
    merged = kind in ("first", "whole")
    rows_in, states, size = operands[0].shape
    rows_out = sum(h.shape[0] for h in h_ready)
    shapes = [(rows_out, states, size)]
    if kind == "other":
        shapes.append((states, pl.cdiv(states, size) * size))
    elif kind == "last":
        shapes = [(states // VEC, 3 * VEC, size)] * 2
    operands = [*h_ready, *operands]
    outs = pl.pallas_call(
        functools.partial(step_kernel, kind, u, len(h_ready)),
        in_specs=[VMEM] * len(operands),
        out_specs=[VMEM] * len(shapes),
        out_shape=[jax.ShapeDtypeStruct(shape, jnp.float32) for shape in shapes],
        scratch_shapes=[
            pltpu.VMEM((2 * states, rows_in * width * size), jnp.bfloat16)
            for width in ((2, 1) if merged else (1,))
        ],
        compiler_params=pltpu.CompilerParams(vmem_limit_bytes=LIMIT),
        cost_estimate=cost_of(rows_out, BLOCKS if merged else 3, states, size),
        name=name,
    )(*operands)
    return outs[0] if len(outs) == 1 else outs


def finish_kernel(cols, node_count, flags_ref, parts_ref, rot_ref, out_ref):
    wide = parts_ref.shape[0]
    gram = parts_ref[0, cols * VEC : (cols + 1) * VEC, 0:VEC]
    for w in range(1, wide):
        gram = gram + parts_ref[w, cols * VEC : (cols + 1) * VEC, 0:VEC]
    gram = gram / node_count
    row = lax.broadcasted_iota(jnp.int32, (VEC, VEC), 0)
    col = lax.broadcasted_iota(jnp.int32, (VEC, VEC), 1)
    inverse = jnp.where(row == col, 1.0, 0.0).astype(jnp.float32)
    for k in range(VEC):
        scale = 1.0 / jnp.sqrt(gram[k : k + 1, k : k + 1])
        top = gram[k : k + 1, :] * scale
        top_inverse = inverse[k : k + 1, :] * scale
        factor = gram[:, k : k + 1] * scale
        gram = gram - factor * top
        inverse = jnp.where(row == k, top_inverse, jnp.where(row > k, inverse - factor * top_inverse, inverse))
    number = jnp.broadcast_to(flags_ref[3 * VEC : 3 * VEC + 1, 0:VEC], (VEC, VEC))
    turn = rot_ref[0]
    for w in range(1, wide):
        turn = jnp.where(number == w, rot_ref[w], turn)
    turn = turn.T
    mixer = turn[:, 0:1] * inverse[0:1, :]
    for k in range(1, VEC):
        mixer = mixer + turn[:, k : k + 1] * inverse[k : k + 1, :]
    columns = [mixer[:, d : d + 1] for d in range(VEC)]
    mixed = []
    for w in range(wide):
        for c in range(cols):
            block = parts_ref[w, c * VEC : (c + 1) * VEC, :]
            total = columns[0] * block[0:1, :]
            for d in range(1, VEC):
                total = total + columns[d] * block[d : d + 1, :]
            mixed.append(total)
    for w in range(wide):
        for c in range(cols):
            out_ref[:, 0, w * cols + c, :] = mixed[(wide - 1 - w) * cols + c]


def finish(flags, cols, node_count, parts, rotation):
    wide, _, size = parts.shape
    return pl.pallas_call(
        functools.partial(finish_kernel, cols, node_count),
        in_specs=[VMEM] * 3,
        out_specs=VMEM,
        out_shape=jax.ShapeDtypeStruct((VEC, 1, wide * cols, size), jnp.float32),
        compiler_params=pltpu.CompilerParams(vmem_limit_bytes=LIMIT),
        name="finish",
    )(flags, parts, rotation)


def after(x, token):
    return lax.optimization_barrier((x, token))[0]


def body(slab, hblocks, blist, rotation):
    wide, grp = lax.axis_size("wide"), lax.axis_size("grp")
    _, _, cols, size = slab.shape
    slots = hblocks.shape[2]
    near = [(i, i ^ 1) for i in range(wide)]
    far = [(i, ((i + 1) ^ 1) - 1) for i in range(1, wide - 1)]
    mine, odd = lax.axis_index("grp"), lax.axis_index("wide") % 2
    x = mine // 2
    edge = half = x ^ (mine % 2)
    place = jnp.stack([odd, edge, half, x]).astype(jnp.int32)
    flags = jnp.stack([odd, edge, half, lax.axis_index("wide")]).astype(jnp.int32)
    flags = jnp.broadcast_to(jnp.repeat(flags, VEC)[:, None], (4 * VEC, size))

    def across(value):
        return lax.ppermute(value, "grp", [(i, i ^ 3) for i in range(grp)])

    def core(value):
        return lax.ppermute(value, "grp", [(i, i ^ 1) for i in range(grp)])

    def over_far(value):
        return lax.ppermute(value, "wide", far)

    def over_near(value):
        return lax.ppermute(value, "wide", near)

    own = arrange(flags, blist, slab)
    own_core = core(own[1])
    h_core = core(hblocks)
    border, inside = pick(flags, hblocks, h_core)
    own_across = across(after(jnp.stack([own[0], own_core]), border))
    rows = [own[0], own_core, own_across[0], own_across[1]]
    codes = jnp.stack([row[-VEC : cols - VEC, :slots] for row in rows]).astype(jnp.int32).reshape(-1)
    codes = jnp.concatenate([place, codes])
    states = (own.shape[1] - VEC) // cols
    zero = []
    for u in range(cols):
        parts = [row[u * states : (u + 1) * states] for row in rows]
        border_mine = jnp.stack([parts[m] for m in (1, 0, 2, 3)])
        border_core = jnp.stack([parts[m] for m in (0, 1, 3, 2)])
        zero.append(jnp.where(edge == 1, border_mine, border_core))

    zero[1] = after(zero[1], zero[0])
    far_rim, near_rim = over_far(zero[0]), over_near(zero[1])
    border = across(after(border, own_core))
    inside = across(after(inside, near_rim))
    h_two = [prepare("chip", codes, hblocks, h_core)]
    border_core = core(after(border, (far_rim, h_two)))
    h_three = h_two + [prepare("border", codes, border, border_core)]

    one = [step("first", 0, "one_0", h_three, *zero, far_rim)]
    rim = after(near_rim, one[0])
    one.append(step("first", 1, "one_1", h_three, *zero, rim))
    rims = over_far(one[0]), over_near(one[1])
    acc = [inner(u, f"two_inner_{u}", h_two, one, zero[u]) for u in range(cols)]
    two = [step("next", 0, "two_0", h_two, rims[0], after(acc[0], inside))]
    rim = after(rims[1], (two[0], inside))
    two.append(step("next", 1, "two_1", h_two, rim, acc[1]))
    other = across(two[0]), across(jnp.concatenate([two[1], one[0][:1], one[1][:1]]))
    two = [jnp.concatenate([two[u], other[u][1:2], other[u][0:1]]) for u in range(cols)]
    before = [jnp.concatenate([one[u], other[1][2 + u : 3 + u]]) for u in range(cols)]
    inside_core = core(after(inside, two[0]))
    h_four = h_three + [prepare("inner", codes, inside, inside_core)]
    rims = over_far(two[0]), over_near(two[1])
    acc = inner(0, "three_inner_0", h_four, two, before[0])
    three = [step("next", 0, "three_0", h_four, rims[0], acc)]
    rim = after(rims[1], three[0])
    three.append(step("whole", 1, "three_1", h_four, *two, rim, before[1]))
    rims = over_far(three[0]), over_near(three[1])
    acc = [inner(u, f"four_inner_{u}", h_four, three, two[u]) for u in range(cols)]
    four = step("other", 0, "four_0", h_four, rims[0], acc[0])
    kept, sent = step("last", 1, "four_1", h_four, rims[1], acc[1], *four, flags)

    sent = core(sent)
    packed = jnp.where(half == 1, jnp.concatenate([kept, sent]), jnp.concatenate([sent, kept]))
    groups = [[(wide - 1 - i) * grp + g for i in range(wide)] for g in range(grp)]
    packed = lax.all_to_all(
        packed,
        ("wide", "grp"),
        split_axis=0,
        concat_axis=0,
        tiled=True,
        axis_index_groups=groups,
    )
    node_count = grp * wide * cols * size
    return finish(flags, cols, node_count, packed, rotation)


def solution(mesh):
    in_specs = (
        P(None, "grp", "wide", None),
        P("grp", "wide", None, None, None),
        P("grp", "wide", None),
        P(),
    )
    out_specs = P("wide", "grp", None, None)
    return jax.shard_map(body, mesh=mesh, in_specs=in_specs, out_specs=out_specs, check_vma=False)
```

```python
import functools

import jax
import jax.numpy as jnp
from jax import lax
from jax.experimental import pallas as pl
from jax.experimental.pallas import tpu as pltpu
from jax.sharding import PartitionSpec as P

VEC = 8
DEG = 4
LIMIT = 16 * 2**20
BLOCKS = 9
VMEM = pl.BlockSpec(memory_space=pltpu.VMEM)
SMEM = pl.BlockSpec(memory_space=pltpu.SMEM)
NT = (((1,), (1,)), ((), ()))


def split(x):
    high = x.astype(jnp.bfloat16)
    low = (x - high.astype(jnp.float32)).astype(jnp.bfloat16)
    return high, low


def flag(flags_ref, n, shape):
    return jnp.broadcast_to(flags_ref[n * VEC : n * VEC + 1, :], shape) == 1


def arrange_kernel(flags_ref, codes_ref, slab_ref, out_ref):
    all_states, _, cols, size = slab_ref.shape
    slots, states = codes_ref.shape[2], all_states // 2
    odd = flag(flags_ref, 0, (all_states, size))
    second = flag(flags_ref, 2, (states, size))
    both = [slab_ref[:, 0, c, :] for c in range(cols)]
    for u in range(cols):
        value = jnp.where(odd, both[cols - 1 - u], both[u])
        low, high = value[:states], value[states:]
        rows = slice(u * states, (u + 1) * states)
        out_ref[0, rows, :] = jnp.where(second, high, low)
        out_ref[1, rows, :] = jnp.where(second, low, high)
    codes = codes_ref[0].astype(jnp.float32)
    for h in range(2):
        out_ref[h, cols * states :, :] = jnp.zeros((VEC, size), jnp.float32)
        out_ref[h, cols * states : cols * states + cols, 0:slots] = codes


def arrange(flags, blist, slab):
    all_states, _, cols, size = slab.shape
    return pl.pallas_call(
        arrange_kernel,
        in_specs=[VMEM] * 3,
        out_specs=VMEM,
        out_shape=jax.ShapeDtypeStruct((2, cols * all_states // 2 + VEC, size), jnp.float32),
        compiler_params=pltpu.CompilerParams(vmem_limit_bytes=LIMIT),
        name="arrange",
    )(flags, blist, slab)


def pick_kernel(flags_ref, own_ref, core_ref, border_ref, inner_ref):
    shape = own_ref.shape[3:]
    edge, half = flag(flags_ref, 1, shape), flag(flags_ref, 2, shape)
    for k in range(own_ref.shape[2]):
        own = jnp.where(half, own_ref[0, 1, k], own_ref[0, 0, k])
        core = jnp.where(half, core_ref[0, 1, k], core_ref[0, 0, k])
        border_ref[0, 0, k] = jnp.where(edge, own, core)
        inner_ref[0, 0, k] = jnp.where(edge, core, own)


def pick(flags, own, core):
    rows, cols, *block = own.shape
    return pl.pallas_call(
        pick_kernel,
        in_specs=[VMEM] * 3,
        out_specs=[VMEM] * 2,
        out_shape=[jax.ShapeDtypeStruct((rows, 1, *block), own.dtype)] * 2,
        compiler_params=pltpu.CompilerParams(vmem_limit_bytes=LIMIT),
        name="pick",
    )(flags, own, core)


def prepare_kernel(mode, codes_ref, *refs):
    *h_refs, out_ref = refs
    _, cols, slots, size, _ = h_refs[0].shape
    odd, edge, half, x = (codes_ref[n] for n in range(4))
    out_ref[...] = jnp.zeros_like(out_ref)

    def convert(h_ref, h_col, c, q, row):
        u = jnp.bitwise_xor(c, odd)
        for k in range(slots):
            code = codes_ref[4 + (row * 2 + c) * slots + k]
            down = (code >= 3).astype(jnp.int32) + (code >= 6).astype(jnp.int32)
            along = code - 3 * down
            down = jnp.where(x == 1, 2 - down, down)
            along = u + jnp.where(odd == 1, 2 - along, along)
            rim = (along == 0) | (along == 3)
            block = jnp.where(rim, 6 + down, 2 * down + along - 1)
            lanes = pl.ds(pl.multiple_of(block * size, size), size)
            high, low = split(h_ref[0, h_col, k])
            out_ref[q, u, 0:size, lanes] = high
            out_ref[q, u, size : 2 * size, lanes] = low

    for h, h_ref in enumerate(h_refs):
        if mode == "chip":
            for c in range(cols):
                convert(h_ref, c, c, jnp.bitwise_xor(edge, h), h)
        else:
            row = 3 - edge if mode == "border" else 2 + edge
            convert(h_ref, 0, jnp.bitwise_xor(half, h), 0, row)


def prepare(mode, codes, *h_rows):
    _, _, slots, size, _ = h_rows[0].shape
    rows = 2 if mode == "chip" else 1
    return pl.pallas_call(
        functools.partial(prepare_kernel, mode),
        in_specs=[SMEM] + [VMEM] * len(h_rows),
        out_specs=VMEM,
        out_shape=jax.ShapeDtypeStruct((rows, 2, 2 * size, BLOCKS * size), jnp.bfloat16),
        compiler_params=pltpu.CompilerParams(vmem_limit_bytes=LIMIT),
        name="prepare_" + mode,
    )(codes, *h_rows)


def fill(x_ref, fields):
    rows, states, size = fields[0].shape
    for q in range(rows):
        for n, field in enumerate(fields):
            at = (q * len(fields) + n) * size
            high, low = split(field[q])
            x_ref[0:states, at : at + size] = high
            x_ref[states : 2 * states, at : at + size] = low


def products(h_refs, u, x_ref, width, first, rows_in):
    states, size = x_ref.shape[0] // 2, h_refs[0].shape[2] // 2
    width, first = width * size, first * size
    h_rows = [h_ref.at[q] for h_ref in h_refs for q in range(h_ref.shape[0])]
    sums = []
    for q, h_row in enumerate(h_rows):
        low, high = max(q - 1, 0), min(q + 2, rows_in)
        at = first + (low - q + 1) * width
        acc = lax.dot_general(
            x_ref[:, low * width : high * width],
            h_row[u, :, at : at + (high - low) * width],
            NT,
            preferred_element_type=jnp.float32,
        )
        small = acc[states:, size:] + (acc[states:, :size] + acc[:states, size:])
        sums.append(acc[:states, :size] + small)
    return sums


def inner_kernel(u, count, *refs):
    h_refs, (own_0, own_1, before, out_ref, x_ref) = refs[:count], refs[count:]
    fill(x_ref, [own_0, own_1])
    for q, value in enumerate(products(h_refs, u, x_ref, 2, 0, own_0.shape[0])):
        out_ref[q] = 2.0 * value - before[q]


def inner(u, name, h_ready, own, before):
    rows_in, states, size = own[0].shape
    rows_out = sum(h.shape[0] for h in h_ready)
    operands = [*h_ready, *own, before]
    return pl.pallas_call(
        functools.partial(inner_kernel, u, len(h_ready)),
        in_specs=[VMEM] * len(operands),
        out_specs=VMEM,
        out_shape=jax.ShapeDtypeStruct((rows_out, states, size), jnp.float32),
        scratch_shapes=[pltpu.VMEM((2 * states, rows_in * 2 * size), jnp.bfloat16)],
        compiler_params=pltpu.CompilerParams(vmem_limit_bytes=LIMIT),
        cost_estimate=cost_of(rows_out, 6, states, size),
        name=name,
    )(*operands)


def cost_of(rows, blocks, states, size):
    return pl.CostEstimate(
        flops=8 * blocks * rows * states * size * size,
        bytes_accessed=4 * blocks * rows * size * size,
        transcendentals=0,
    )


def step_kernel(kind, u, count, *refs):
    h_refs, refs = refs[:count], refs[count:]
    if kind in ("first", "whole"):
        own_0, own_1, rim_ref, *refs, own_x, rim_x = refs
    else:
        rim_ref, acc_ref, *refs, rim_x = refs
    rows_in, states, size = rim_ref.shape
    fill(rim_x, [rim_ref])
    values = products(h_refs, u, rim_x, 1, 6, rows_in)
    if kind in ("first", "whole"):
        fill(own_x, [own_0, own_1])
        own = products(h_refs, u, own_x, 2, 0, rows_in)
        values = [value + own[q] for q, value in enumerate(values)]
        if kind == "whole":
            before, *refs = refs
            values = [2.0 * value - before[q] for q, value in enumerate(values)]
    else:
        values = [acc_ref[q] + 2.0 * value for q, value in enumerate(values)]
    if kind in ("other", "last"):
        flat = [jnp.concatenate(part, axis=1) for part in zip(*map(split, values))]
        flat = jnp.concatenate(flat)
        gram = lax.dot_general(flat, flat, NT, preferred_element_type=jnp.float32)
        gram = gram[:states] + gram[states:]
        gram = gram[:, :states] + gram[:, states:]
    if kind != "last":
        for q, value in enumerate(values):
            refs[0][q] = value
        if kind == "other":
            refs[1][:, 0:states] = gram
        return
    other_ref, other_gram_ref, flags_ref, kept_ref, sent_ref = refs
    odd, edge = flag(flags_ref, 0, (states, size)), flag(flags_ref, 1, (states, size))
    nodes = [[other_ref[q] for q in range(len(values))], values]
    gram = gram + other_gram_ref[:, 0:states]
    blocks = states // VEC
    for c in range(2):
        inner = jnp.where(odd, nodes[1 - c][0], nodes[c][0])
        border = jnp.where(odd, nodes[1 - c][1], nodes[c][1])
        kept, sent = jnp.where(edge, border, inner), jnp.where(edge, inner, border)
        for b in range(blocks):
            rows = slice(b * VEC, (b + 1) * VEC)
            kept_ref[blocks - 1 - b, c * VEC : (c + 1) * VEC, :] = kept[rows]
            sent_ref[blocks - 1 - b, c * VEC : (c + 1) * VEC, :] = sent[rows]
    for b in range(blocks):
        rows = slice(b * VEC, (b + 1) * VEC)
        for ref in (kept_ref, sent_ref):
            ref[blocks - 1 - b, 2 * VEC :, :] = jnp.zeros((VEC, size), jnp.float32)
            ref[blocks - 1 - b, 2 * VEC :, 0:VEC] = gram[rows, rows]


def step(kind, u, name, h_ready, *operands):
    merged = kind in ("first", "whole")
    rows_in, states, size = operands[0].shape
    rows_out = sum(h.shape[0] for h in h_ready)
    shapes = [(rows_out, states, size)]
    if kind == "other":
        shapes.append((states, pl.cdiv(states, size) * size))
    elif kind == "last":
        shapes = [(states // VEC, 3 * VEC, size)] * 2
    operands = [*h_ready, *operands]
    outs = pl.pallas_call(
        functools.partial(step_kernel, kind, u, len(h_ready)),
        in_specs=[VMEM] * len(operands),
        out_specs=[VMEM] * len(shapes),
        out_shape=[jax.ShapeDtypeStruct(shape, jnp.float32) for shape in shapes],
        scratch_shapes=[
            pltpu.VMEM((2 * states, rows_in * width * size), jnp.bfloat16)
            for width in ((2, 1) if merged else (1,))
        ],
        compiler_params=pltpu.CompilerParams(vmem_limit_bytes=LIMIT),
        cost_estimate=cost_of(rows_out, BLOCKS if merged else 3, states, size),
        name=name,
    )(*operands)
    return outs[0] if len(outs) == 1 else outs


def finish_kernel(cols, node_count, flags_ref, parts_ref, rot_ref, out_ref):
    wide = parts_ref.shape[0]
    gram = parts_ref[0, cols * VEC : (cols + 1) * VEC, 0:VEC]
    for w in range(1, wide):
        gram = gram + parts_ref[w, cols * VEC : (cols + 1) * VEC, 0:VEC]
    gram = gram / node_count
    row = lax.broadcasted_iota(jnp.int32, (VEC, VEC), 0)
    col = lax.broadcasted_iota(jnp.int32, (VEC, VEC), 1)
    inverse = jnp.where(row == col, 1.0, 0.0).astype(jnp.float32)
    for k in range(VEC):
        scale = 1.0 / jnp.sqrt(gram[k : k + 1, k : k + 1])
        top = gram[k : k + 1, :] * scale
        top_inverse = inverse[k : k + 1, :] * scale
        factor = gram[:, k : k + 1] * scale
        gram = gram - factor * top
        inverse = jnp.where(row == k, top_inverse, jnp.where(row > k, inverse - factor * top_inverse, inverse))
    number = jnp.broadcast_to(flags_ref[3 * VEC : 3 * VEC + 1, 0:VEC], (VEC, VEC))
    turn = rot_ref[0]
    for w in range(1, wide):
        turn = jnp.where(number == w, rot_ref[w], turn)
    turn = turn.T
    mixer = turn[:, 0:1] * inverse[0:1, :]
    for k in range(1, VEC):
        mixer = mixer + turn[:, k : k + 1] * inverse[k : k + 1, :]
    columns = [mixer[:, d : d + 1] for d in range(VEC)]
    mixed = []
    for w in range(wide):
        for c in range(cols):
            terms = [columns[d] * parts_ref[w, pl.ds(c * VEC + d, 1), :] for d in range(VEC)]
            while len(terms) > 1:
                terms = [low + high for low, high in zip(terms[::2], terms[1::2])]
            mixed += terms
    for w in range(wide):
        for c in range(cols):
            out_ref[:, 0, w * cols + c, :] = mixed[(wide - 1 - w) * cols + c]


def finish(flags, cols, node_count, parts, rotation):
    wide, _, size = parts.shape
    return pl.pallas_call(
        functools.partial(finish_kernel, cols, node_count),
        in_specs=[VMEM] * 3,
        out_specs=VMEM,
        out_shape=jax.ShapeDtypeStruct((VEC, 1, wide * cols, size), jnp.float32),
        compiler_params=pltpu.CompilerParams(vmem_limit_bytes=LIMIT),
        name="finish",
    )(flags, parts, rotation)


def after(x, token):
    return lax.optimization_barrier((x, token))[0]


def body(slab, hblocks, blist, rotation):
    wide, grp = lax.axis_size("wide"), lax.axis_size("grp")
    _, _, cols, size = slab.shape
    slots = hblocks.shape[2]
    near = [(i, i ^ 1) for i in range(wide)]
    far = [(i, ((i + 1) ^ 1) - 1) for i in range(1, wide - 1)]
    mine, odd = lax.axis_index("grp"), lax.axis_index("wide") % 2
    x = mine // 2
    edge = half = x ^ (mine % 2)
    place = jnp.stack([odd, edge, half, x]).astype(jnp.int32)
    flags = jnp.stack([odd, edge, half, lax.axis_index("wide")]).astype(jnp.int32)
    flags = jnp.broadcast_to(jnp.repeat(flags, VEC)[:, None], (4 * VEC, size))

    def across(value):
        return lax.ppermute(value, "grp", [(i, i ^ 3) for i in range(grp)])

    def core(value):
        return lax.ppermute(value, "grp", [(i, i ^ 1) for i in range(grp)])

    def over_far(value):
        return lax.ppermute(value, "wide", far)

    def over_near(value):
        return lax.ppermute(value, "wide", near)

    own = arrange(flags, blist, slab)
    own_core = core(own[1])
    h_core = core(hblocks)
    border, inside = pick(flags, hblocks, h_core)
    own_across = across(after(jnp.stack([own[0], own_core]), border))
    rows = [own[0], own_core, own_across[0], own_across[1]]
    codes = jnp.stack([row[-VEC : cols - VEC, :slots] for row in rows]).astype(jnp.int32).reshape(-1)
    codes = jnp.concatenate([place, codes])
    states = (own.shape[1] - VEC) // cols
    zero = []
    for u in range(cols):
        parts = [row[u * states : (u + 1) * states] for row in rows]
        border_mine = jnp.stack([parts[m] for m in (1, 0, 2, 3)])
        border_core = jnp.stack([parts[m] for m in (0, 1, 3, 2)])
        zero.append(jnp.where(edge == 1, border_mine, border_core))

    zero[1] = after(zero[1], zero[0])
    far_rim, near_rim = over_far(zero[0]), over_near(zero[1])
    border = across(after(border, own_core))
    inside = across(after(inside, near_rim))
    h_two = [prepare("chip", codes, hblocks, h_core)]
    border_core = core(after(border, (far_rim, h_two)))
    h_three = h_two + [prepare("border", codes, border, border_core)]

    one = [step("first", 0, "one_0", h_three, *zero, far_rim)]
    rim = after(near_rim, one[0])
    one.append(step("first", 1, "one_1", h_three, *zero, rim))
    rims = over_far(one[0]), over_near(one[1])
    acc = [inner(u, f"two_inner_{u}", h_two, one, zero[u]) for u in range(cols)]
    two, sent, before = [], (), []
    for u in range(cols):
        rim = after(rims[u], (sent, inside))
        two.append(step("next", u, f"two_{u}", h_two, rim, acc[u]))
        sent = jnp.concatenate([two[u], one[u][:1]])
        other = across(sent)
        two[u] = jnp.concatenate([two[u], other[1:2], other[0:1]])
        before.append(jnp.concatenate([one[u], other[2:]]))
    inside_core = core(after(inside, two[0]))
    h_four = h_three + [prepare("inner", codes, inside, inside_core)]
    rims = over_far(two[0]), over_near(two[1])
    acc = inner(0, "three_inner_0", h_four, two, before[0])
    three = [step("next", 0, "three_0", h_four, rims[0], acc)]
    rim = after(rims[1], three[0])
    three.append(step("whole", 1, "three_1", h_four, *two, rim, before[1]))
    rims = over_far(three[0]), over_near(three[1])
    acc = [inner(u, f"four_inner_{u}", h_four, three, two[u]) for u in range(cols)]
    four = step("other", 0, "four_0", h_four, rims[0], acc[0])
    kept, sent = step("last", 1, "four_1", h_four, rims[1], acc[1], *four, flags)

    sent = core(sent)
    packed = jnp.where(half == 1, jnp.concatenate([kept, sent]), jnp.concatenate([sent, kept]))
    groups = [[(wide - 1 - i) * grp + g for i in range(wide)] for g in range(grp)]
    packed = lax.all_to_all(
        packed,
        ("wide", "grp"),
        split_axis=0,
        concat_axis=0,
        tiled=True,
        axis_index_groups=groups,
    )
    node_count = grp * wide * cols * size
    return finish(flags, cols, node_count, packed, rotation)


def solution(mesh):
    in_specs = (
        P(None, "grp", "wide", None),
        P("grp", "wide", None, None, None),
        P("grp", "wide", None),
        P(),
    )
    out_specs = P("wide", "grp", None, None)
    return jax.shard_map(body, mesh=mesh, in_specs=in_specs, out_specs=out_specs, check_vma=False)
```

```python
import functools

import jax
import jax.numpy as jnp
from jax import lax
from jax.experimental import pallas as pl
from jax.experimental.pallas import tpu as pltpu
from jax.sharding import PartitionSpec as P

VEC = 8
DEG = 4
LIMIT = 16 * 2**20
BLOCKS = 9
VMEM = pl.BlockSpec(memory_space=pltpu.VMEM)
SMEM = pl.BlockSpec(memory_space=pltpu.SMEM)
NT = (((1,), (1,)), ((), ()))


def split(x):
    high = x.astype(jnp.bfloat16)
    low = (x - high.astype(jnp.float32)).astype(jnp.bfloat16)
    return high, low


def flag(flags_ref, n, shape):
    return jnp.broadcast_to(flags_ref[n * VEC : n * VEC + 1, :], shape) == 1


def arrange_kernel(flags_ref, codes_ref, slab_ref, out_ref):
    all_states, _, cols, size = slab_ref.shape
    slots, states = codes_ref.shape[2], all_states // 2
    odd = flag(flags_ref, 0, (all_states, size))
    second = flag(flags_ref, 2, (states, size))
    both = [slab_ref[:, 0, c, :] for c in range(cols)]
    for u in range(cols):
        value = jnp.where(odd, both[cols - 1 - u], both[u])
        low, high = value[:states], value[states:]
        rows = slice(u * states, (u + 1) * states)
        out_ref[0, rows, :] = jnp.where(second, high, low)
        out_ref[1, rows, :] = jnp.where(second, low, high)
    codes = codes_ref[0].astype(jnp.float32)
    for h in range(2):
        out_ref[h, cols * states :, :] = jnp.zeros((VEC, size), jnp.float32)
        out_ref[h, cols * states : cols * states + cols, 0:slots] = codes


def arrange(flags, blist, slab):
    all_states, _, cols, size = slab.shape
    return pl.pallas_call(
        arrange_kernel,
        in_specs=[VMEM] * 3,
        out_specs=VMEM,
        out_shape=jax.ShapeDtypeStruct((2, cols * all_states // 2 + VEC, size), jnp.float32),
        compiler_params=pltpu.CompilerParams(vmem_limit_bytes=LIMIT),
        name="arrange",
    )(flags, blist, slab)


def pick_kernel(flags_ref, own_ref, core_ref, border_ref, inner_ref):
    shape = own_ref.shape[3:]
    edge, half = flag(flags_ref, 1, shape), flag(flags_ref, 2, shape)
    for k in range(own_ref.shape[2]):
        own = jnp.where(half, own_ref[0, 1, k], own_ref[0, 0, k])
        core = jnp.where(half, core_ref[0, 1, k], core_ref[0, 0, k])
        border_ref[0, 0, k] = jnp.where(edge, own, core)
        inner_ref[0, 0, k] = jnp.where(edge, core, own)


def pick(flags, own, core):
    rows, cols, *block = own.shape
    return pl.pallas_call(
        pick_kernel,
        in_specs=[VMEM] * 3,
        out_specs=[VMEM] * 2,
        out_shape=[jax.ShapeDtypeStruct((rows, 1, *block), own.dtype)] * 2,
        compiler_params=pltpu.CompilerParams(vmem_limit_bytes=LIMIT),
        name="pick",
    )(flags, own, core)


def prepare_kernel(mode, codes_ref, *refs):
    *h_refs, out_ref = refs
    _, cols, slots, size, _ = h_refs[0].shape
    odd, edge, half, x = (codes_ref[n] for n in range(4))
    out_ref[...] = jnp.zeros_like(out_ref)

    def convert(h_ref, h_col, c, q, row):
        u = jnp.bitwise_xor(c, odd)
        for k in range(slots):
            code = codes_ref[4 + (row * 2 + c) * slots + k]
            down = (code >= 3).astype(jnp.int32) + (code >= 6).astype(jnp.int32)
            along = code - 3 * down
            down = jnp.where(x == 1, 2 - down, down)
            along = u + jnp.where(odd == 1, 2 - along, along)
            rim = (along == 0) | (along == 3)
            block = jnp.where(rim, 6 + down, 2 * down + along - 1)
            lanes = pl.ds(pl.multiple_of(block * size, size), size)
            high, low = split(h_ref[0, h_col, k])
            out_ref[q, u, 0:size, lanes] = high
            out_ref[q, u, size : 2 * size, lanes] = low

    for h, h_ref in enumerate(h_refs):
        if mode == "chip":
            for c in range(cols):
                convert(h_ref, c, c, jnp.bitwise_xor(edge, h), h)
        else:
            row = 3 - edge if mode == "border" else 2 + edge
            convert(h_ref, 0, jnp.bitwise_xor(half, h), 0, row)


def prepare(mode, codes, *h_rows):
    _, _, slots, size, _ = h_rows[0].shape
    rows = 2 if mode == "chip" else 1
    return pl.pallas_call(
        functools.partial(prepare_kernel, mode),
        in_specs=[SMEM] + [VMEM] * len(h_rows),
        out_specs=VMEM,
        out_shape=jax.ShapeDtypeStruct((rows, 2, 2 * size, BLOCKS * size), jnp.bfloat16),
        compiler_params=pltpu.CompilerParams(vmem_limit_bytes=LIMIT),
        name="prepare_" + mode,
    )(codes, *h_rows)


def fill(x_ref, fields):
    rows, states, size = fields[0].shape
    for q in range(rows):
        for n, field in enumerate(fields):
            at = (q * len(fields) + n) * size
            high, low = split(field[q])
            x_ref[0:states, at : at + size] = high
            x_ref[states : 2 * states, at : at + size] = low


def products(h_refs, u, x_ref, width, first, rows_in):
    states, size = x_ref.shape[0] // 2, h_refs[0].shape[2] // 2
    width, first = width * size, first * size
    h_rows = [h_ref.at[q] for h_ref in h_refs for q in range(h_ref.shape[0])]
    sums = []
    for q, h_row in enumerate(h_rows):
        low, high = max(q - 1, 0), min(q + 2, rows_in)
        at = first + (low - q + 1) * width
        acc = lax.dot_general(
            x_ref[:, low * width : high * width],
            h_row[u, :, at : at + (high - low) * width],
            NT,
            preferred_element_type=jnp.float32,
        )
        small = acc[states:, size:] + (acc[states:, :size] + acc[:states, size:])
        sums.append(acc[:states, :size] + small)
    return sums


def inner_kernel(u, count, *refs):
    h_refs, (own_0, own_1, before, out_ref, x_ref) = refs[:count], refs[count:]
    fill(x_ref, [own_0, own_1])
    for q, value in enumerate(products(h_refs, u, x_ref, 2, 0, own_0.shape[0])):
        out_ref[q] = 2.0 * value - before[q]


def inner(u, name, h_ready, own, before):
    rows_in, states, size = own[0].shape
    rows_out = sum(h.shape[0] for h in h_ready)
    operands = [*h_ready, *own, before]
    return pl.pallas_call(
        functools.partial(inner_kernel, u, len(h_ready)),
        in_specs=[VMEM] * len(operands),
        out_specs=VMEM,
        out_shape=jax.ShapeDtypeStruct((rows_out, states, size), jnp.float32),
        scratch_shapes=[pltpu.VMEM((2 * states, rows_in * 2 * size), jnp.bfloat16)],
        compiler_params=pltpu.CompilerParams(vmem_limit_bytes=LIMIT),
        cost_estimate=cost_of(rows_out, 6, states, size),
        name=name,
    )(*operands)


def cost_of(rows, blocks, states, size):
    return pl.CostEstimate(
        flops=8 * blocks * rows * states * size * size,
        bytes_accessed=4 * blocks * rows * size * size,
        transcendentals=0,
    )


def step_kernel(kind, u, count, *refs):
    h_refs, refs = refs[:count], refs[count:]
    if kind in ("first", "whole"):
        own_0, own_1, rim_ref, *refs, own_x, rim_x = refs
    else:
        rim_ref, acc_ref, *refs, rim_x = refs
    rows_in, states, size = rim_ref.shape
    fill(rim_x, [rim_ref])
    values = products(h_refs, u, rim_x, 1, 6, rows_in)
    if kind in ("first", "whole"):
        fill(own_x, [own_0, own_1])
        own = products(h_refs, u, own_x, 2, 0, rows_in)
        values = [value + own[q] for q, value in enumerate(values)]
        if kind == "whole":
            before, *refs = refs
            values = [2.0 * value - before[q] for q, value in enumerate(values)]
    else:
        values = [acc_ref[q] + 2.0 * value for q, value in enumerate(values)]
    if kind in ("other", "last"):
        flat = [jnp.concatenate(part, axis=1) for part in zip(*map(split, values))]
        flat = jnp.concatenate(flat)
        gram = lax.dot_general(flat, flat, NT, preferred_element_type=jnp.float32)
        gram = gram[:states] + gram[states:]
        gram = gram[:, :states] + gram[:, states:]
    if kind != "last":
        for q, value in enumerate(values):
            refs[0][q] = value
        if kind == "other":
            refs[1][:, 0:states] = gram
        return
    other_ref, other_gram_ref, flags_ref, kept_ref, sent_ref = refs
    odd, edge = flag(flags_ref, 0, (states, size)), flag(flags_ref, 1, (states, size))
    nodes = [[other_ref[q] for q in range(len(values))], values]
    gram = gram + other_gram_ref[:, 0:states]
    blocks = states // VEC
    for c in range(2):
        inner = jnp.where(odd, nodes[1 - c][0], nodes[c][0])
        border = jnp.where(odd, nodes[1 - c][1], nodes[c][1])
        kept, sent = jnp.where(edge, border, inner), jnp.where(edge, inner, border)
        for b in range(blocks):
            rows = slice(b * VEC, (b + 1) * VEC)
            kept_ref[blocks - 1 - b, c * VEC : (c + 1) * VEC, :] = kept[rows]
            sent_ref[blocks - 1 - b, c * VEC : (c + 1) * VEC, :] = sent[rows]
    for b in range(blocks):
        rows = slice(b * VEC, (b + 1) * VEC)
        for ref in (kept_ref, sent_ref):
            ref[blocks - 1 - b, 2 * VEC :, :] = jnp.zeros((VEC, size), jnp.float32)
            ref[blocks - 1 - b, 2 * VEC :, 0:VEC] = gram[rows, rows]


def step(kind, u, name, h_ready, *operands):
    merged = kind in ("first", "whole")
    rows_in, states, size = operands[0].shape
    rows_out = sum(h.shape[0] for h in h_ready)
    shapes = [(rows_out, states, size)]
    if kind == "other":
        shapes.append((states, pl.cdiv(states, size) * size))
    elif kind == "last":
        shapes = [(states // VEC, 3 * VEC, size)] * 2
    operands = [*h_ready, *operands]
    outs = pl.pallas_call(
        functools.partial(step_kernel, kind, u, len(h_ready)),
        in_specs=[VMEM] * len(operands),
        out_specs=[VMEM] * len(shapes),
        out_shape=[jax.ShapeDtypeStruct(shape, jnp.float32) for shape in shapes],
        scratch_shapes=[
            pltpu.VMEM((2 * states, rows_in * width * size), jnp.bfloat16)
            for width in ((2, 1) if merged else (1,))
        ],
        compiler_params=pltpu.CompilerParams(vmem_limit_bytes=LIMIT),
        cost_estimate=cost_of(rows_out, BLOCKS if merged else 3, states, size),
        name=name,
    )(*operands)
    return outs[0] if len(outs) == 1 else outs


def finish_kernel(cols, node_count, flags_ref, parts_ref, rot_ref, out_ref):
    wide = parts_ref.shape[0]
    gram = parts_ref[0, cols * VEC : (cols + 1) * VEC, 0:VEC]
    for w in range(1, wide):
        gram = gram + parts_ref[w, cols * VEC : (cols + 1) * VEC, 0:VEC]
    gram = gram / node_count
    row = lax.broadcasted_iota(jnp.int32, (VEC, VEC), 0)
    col = lax.broadcasted_iota(jnp.int32, (VEC, VEC), 1)
    inverse = jnp.where(row == col, 1.0, 0.0).astype(jnp.float32)
    for k in range(VEC):
        scale = 1.0 / jnp.sqrt(gram[k : k + 1, k : k + 1])
        top = gram[k : k + 1, :] * scale
        top_inverse = inverse[k : k + 1, :] * scale
        factor = gram[:, k : k + 1] * scale
        gram = gram - factor * top
        inverse = jnp.where(row == k, top_inverse, jnp.where(row > k, inverse - factor * top_inverse, inverse))
    number = jnp.broadcast_to(flags_ref[3 * VEC : 3 * VEC + 1, 0:VEC], (VEC, VEC))
    turn = rot_ref[0]
    for w in range(1, wide):
        turn = jnp.where(number == w, rot_ref[w], turn)
    turn = turn.T
    mixer = turn[:, 0:1] * inverse[0:1, :]
    for k in range(1, VEC):
        mixer = mixer + turn[:, k : k + 1] * inverse[k : k + 1, :]
    columns = [mixer[:, d : d + 1] for d in range(VEC)]
    mixed = []
    for w in range(wide):
        for c in range(cols):
            terms = [columns[d] * parts_ref[w, pl.ds(c * VEC + d, 1), :] for d in range(VEC)]
            while len(terms) > 1:
                terms = [low + high for low, high in zip(terms[::2], terms[1::2])]
            mixed += terms
    for w in range(wide):
        for c in range(cols):
            out_ref[:, 0, w * cols + c, :] = mixed[(wide - 1 - w) * cols + c]


def finish(flags, cols, node_count, parts, rotation):
    wide, _, size = parts.shape
    return pl.pallas_call(
        functools.partial(finish_kernel, cols, node_count),
        in_specs=[VMEM] * 3,
        out_specs=VMEM,
        out_shape=jax.ShapeDtypeStruct((VEC, 1, wide * cols, size), jnp.float32),
        compiler_params=pltpu.CompilerParams(vmem_limit_bytes=LIMIT),
        name="finish",
    )(flags, parts, rotation)


def after(x, token):
    return lax.optimization_barrier((x, token))[0]


def body(slab, hblocks, blist, rotation):
    wide, grp = lax.axis_size("wide"), lax.axis_size("grp")
    _, _, cols, size = slab.shape
    slots = hblocks.shape[2]
    near = [(i, i ^ 1) for i in range(wide)]
    far = [(i, ((i + 1) ^ 1) - 1) for i in range(1, wide - 1)]
    mine, odd = lax.axis_index("grp"), lax.axis_index("wide") % 2
    x = mine // 2
    edge = half = x ^ (mine % 2)
    place = jnp.stack([odd, edge, half, x]).astype(jnp.int32)
    flags = jnp.stack([odd, edge, half, lax.axis_index("wide")]).astype(jnp.int32)
    flags = jnp.broadcast_to(jnp.repeat(flags, VEC)[:, None], (4 * VEC, size))

    def across(value):
        return lax.ppermute(value, "grp", [(i, i ^ 3) for i in range(grp)])

    def core(value):
        return lax.ppermute(value, "grp", [(i, i ^ 1) for i in range(grp)])

    def over_far(value):
        return lax.ppermute(value, "wide", far)

    def over_near(value):
        return lax.ppermute(value, "wide", near)

    own = arrange(flags, blist, slab)
    own_core = core(own[1])
    h_core = core(hblocks)
    border, inside = pick(flags, hblocks, h_core)
    own_across = across(after(jnp.stack([own[0], own_core]), border))
    rows = [own[0], own_core, own_across[0], own_across[1]]
    codes = jnp.stack([row[-VEC : cols - VEC, :slots] for row in rows]).astype(jnp.int32).reshape(-1)
    codes = jnp.concatenate([place, codes])
    states = (own.shape[1] - VEC) // cols
    zero = []
    for u in range(cols):
        parts = [row[u * states : (u + 1) * states] for row in rows]
        border_mine = jnp.stack([parts[m] for m in (1, 0, 2, 3)])
        border_core = jnp.stack([parts[m] for m in (0, 1, 3, 2)])
        zero.append(jnp.where(edge == 1, border_mine, border_core))

    zero[1] = after(zero[1], zero[0])
    far_rim, near_rim = over_far(zero[0]), over_near(zero[1])
    border = across(after(border, own_core))
    inside = across(after(inside, near_rim))
    h_two = [prepare("chip", codes, hblocks, h_core)]
    border_core = core(after(border, (far_rim, h_two)))
    h_three = h_two + [prepare("border", codes, border, border_core)]

    one = [step("first", 0, "one_0", h_three, *zero, far_rim)]
    rim = after(near_rim, one[0])
    one.append(step("first", 1, "one_1", h_three, *zero, rim))
    rims = over_far(one[0]), over_near(one[1])
    acc = [inner(u, f"two_inner_{u}", h_two, one, zero[u]) for u in range(cols)]
    two = [step("next", 0, "two_0", h_two, rims[0], after(acc[0], inside))]
    rim = after(rims[1], (two[0], inside))
    two.append(step("next", 1, "two_1", h_two, rim, acc[1]))
    other = across(two[0]), across(jnp.concatenate([two[1], one[0][:1], one[1][:1]]))
    two = [jnp.concatenate([two[u], other[u][1:2], other[u][0:1]]) for u in range(cols)]
    before = [jnp.concatenate([one[u], other[1][2 + u : 3 + u]]) for u in range(cols)]
    inside_core = core(after(inside, two[0]))
    h_four = h_three + [prepare("inner", codes, inside, inside_core)]
    rims = over_far(two[0]), over_near(two[1])
    acc = inner(0, "three_inner_0", h_four, two, before[0])
    three = [step("next", 0, "three_0", h_four, rims[0], acc)]
    rim = after(rims[1], three[0])
    three.append(step("whole", 1, "three_1", h_four, *two, rim, before[1]))
    rims = over_far(three[0]), over_near(three[1])
    acc = [inner(u, f"four_inner_{u}", h_four, three, two[u]) for u in range(cols)]
    four = step("other", 0, "four_0", h_four, rims[0], acc[0])
    kept, sent = step("last", 1, "four_1", h_four, rims[1], acc[1], *four, flags)

    sent = core(sent)
    packed = jnp.where(half == 1, jnp.concatenate([kept, sent]), jnp.concatenate([sent, kept]))
    groups = [[(wide - 1 - i) * grp + g for i in range(wide)] for g in range(grp)]
    packed = lax.all_to_all(
        packed,
        ("wide", "grp"),
        split_axis=0,
        concat_axis=0,
        tiled=True,
        axis_index_groups=groups,
    )
    node_count = grp * wide * cols * size
    return finish(flags, cols, node_count, packed, rotation)


def solution(mesh):
    in_specs = (
        P(None, "grp", "wide", None),
        P("grp", "wide", None, None, None),
        P("grp", "wide", None),
        P(),
    )
    out_specs = P("wide", "grp", None, None)
    return jax.shard_map(body, mesh=mesh, in_specs=in_specs, out_specs=out_specs, check_vma=False)
```
